32 devices in a mesh: dp: 16 (over z, x, core), fsdp: 2 (over y).
Axes of the slice: x: 2, y: 2, z: 4, core: 2. Of those that a mesh axis runs over, the one named last changes fastest.
Arguments:
- tokens: bfloat16 [4, 16384, 768], P(None, ('dp', 'fsdp')), may hold values from -6 to 6
- lengths: int32 [4, 32, 8], P(None, ('dp', 'fsdp')), may hold values from 0 to 512, as said below
- cotangent: bfloat16 [4, 16384, 768], P(None, ('dp', 'fsdp')), may hold values from -6 to 6
- attn_norm_gain: bfloat16 [768], P(('dp', 'fsdp')), may hold values from 0.5 to 1.5
- attn_norm_bias: bfloat16 [768], P(('dp', 'fsdp')), may hold values from -1 to 1
- qkv_weight: bfloat16 [768, 2304], P(('dp', 'fsdp')), may hold values from -0.21875 to 0.21875
- qkv_bias: bfloat16 [2304], P(('dp', 'fsdp')), may hold values from -1 to 1
- out_weight: bfloat16 [768, 768], P(('dp', 'fsdp')), may hold values from -0.625 to 0.625
- out_bias: bfloat16 [768], P(('dp', 'fsdp')), may hold values from -1 to 1
- mlp_norm_gain: bfloat16 [768], P(('dp', 'fsdp')), may hold values from 0.5 to 1.5
- mlp_norm_bias: bfloat16 [768], P(('dp', 'fsdp')), may hold values from -1 to 1
- up_weight: bfloat16 [768, 3072], P(('dp', 'fsdp')), may hold values from -0.21875 to 0.21875
- up_bias: bfloat16 [3072], P(('dp', 'fsdp')), may hold values from -1 to 1
- down_weight: bfloat16 [3072, 768], P(('dp', 'fsdp')), may hold values from -0.109375 to 0.109375
- down_bias: bfloat16 [768], P(('dp', 'fsdp')), may hold values from -1 to 1
Outputs:
- block_out: bfloat16 [4, 16384, 768], P(None, ('dp', 'fsdp'))
- grad_tokens: bfloat16 [4, 16384, 768], P(None, ('dp', 'fsdp'))
- grad_attn_norm_gain: float32 [768], P(('dp', 'fsdp'))
- grad_attn_norm_bias: float32 [768], P(('dp', 'fsdp'))
- grad_qkv_weight: float32 [768, 2304], P(('dp', 'fsdp'))
- grad_qkv_bias: float32 [2304], P(('dp', 'fsdp'))
- grad_out_weight: float32 [768, 768], P(('dp', 'fsdp'))
- grad_out_bias: float32 [768], P(('dp', 'fsdp'))
- grad_mlp_norm_gain: float32 [768], P(('dp', 'fsdp'))
- grad_mlp_norm_bias: float32 [768], P(('dp', 'fsdp'))
- grad_up_weight: float32 [768, 3072], P(('dp', 'fsdp'))
- grad_up_bias: float32 [3072], P(('dp', 'fsdp'))
- grad_down_weight: float32 [3072, 768], P(('dp', 'fsdp'))
- grad_down_bias: float32 [768], P(('dp', 'fsdp'))
The draws below stay inside these ranges and needn't reach their ends.
Inputs may be any that keep to these rules, and one draw needn't show every extreme that they name: Each row lists the lengths of the sequences packed into one row of 512 positions, in order: a slot holds 0 (unused, only after all used ones) or 64 to 512; a row's lengths sum to at most 512; in every draw some row holds one sequence of 512.
All inputs are finite; a program needn't handle non-finite values.
Results may differ from the reference program's by a relative error of at most 0.01.
Values may be sent and summed in bfloat16 or wider, within the bound.
No kernel may reach another device: no remote copies, remote signals or barrier semaphores. Data moves between devices by JAX's collectives and lax.ppermute only.
A program may use at most 320 MiB of HBM per device.

```python
import jax
import jax.numpy as jnp
from jax import lax

D = 768
HEADS = 12
HEAD = 64
FF = 3072
ROW = 512
MICRO = 4
MINLEN = 64
SEQS = 8
SHARDS = 32
ROWS = 16384


def draw_lengths(key, part):
    key = jax.random.fold_in(key, 11)
    key_base, key_tier, key_pick = jax.random.split(key, 3)
    shape_all = (MICRO, SHARDS, SEQS)
    base_len = jax.random.randint(key_base, shape_all, MINLEN, 2 * MINLEN)
    tier_draw = jax.random.randint(key_tier, shape_all, 0, 8)
    factor = jnp.where(tier_draw < 4, 1, jnp.where(tier_draw < 6, 2, jnp.where(tier_draw < 7, 4, 8)))
    raw_len = jnp.minimum(base_len * factor, ROW)
    seq_ends = jnp.cumsum(raw_len, axis=-1, dtype=jnp.int32)
    packed = jnp.where(seq_ends <= ROW, raw_len, 0)
    chosen = jax.random.randint(key_pick, (), 0, MICRO * SHARDS)
    row_ids = jnp.arange(MICRO * SHARDS, dtype=jnp.int32).reshape(MICRO, SHARDS, 1)
    slot_ids = jnp.arange(SEQS, dtype=jnp.int32)
    single = jnp.where(slot_ids == 0, ROW, 0)
    return jnp.where(row_ids == chosen, single[None, None, :], packed).astype(jnp.int32)


def spiked(values, rng, source, target, parts, factor):
    owner, partner = [(jnp.arange(values.shape[position]) // (values.shape[position] // parts)).reshape([-1 if axis == position else 1 for axis in range(values.ndim)]) for position in (source, target)]
    chosen = jax.random.permutation(rng, parts)[partner]
    strong = (owner == chosen) | (owner == (partner + parts // 2) % parts)
    return jnp.where(strong, factor * values, values)


def levels(own_key, extent, cuts, smallest, top_value):
    level, own = 1.0, jax.random.fold_in(own_key, 6)
    for dim, blocks in cuts:
        heights = jnp.exp(jax.random.uniform(jax.random.fold_in(own, dim), (blocks,), jnp.float32, smallest / len(cuts), top_value / len(cuts)))
        level = level * jnp.repeat(heights, extent[dim] // blocks).reshape([-1 if axis == dim else 1 for axis in range(len(extent))])
    return level


def gaussian(rng, shape, scale, reach, pieces=(), kind=jnp.bfloat16):
    level = levels(rng, shape, pieces, -0.22, 0.18) if pieces else 1.0
    entries = jax.random.normal(rng, shape, jnp.float32) * scale * level
    return jnp.minimum(jnp.maximum(entries, -reach), reach).astype(kind)


def gaussian_with(rng, dims, width, most, shards, heavy, kind=jnp.bfloat16):
    values = width * jax.random.normal(rng, dims, jnp.float32)
    if shards:
        values = values * levels(rng, dims, shards, -0.22, 0.18)
    return jnp.clip(spiked(values, jax.random.fold_in(rng, 3), *heavy), -most, most).astype(kind)


def setup_inputs(seed: int = 0) -> dict:
    splits = jax.random.split(jax.random.key(seed), 16)
    return {
        "tokens": gaussian(splits[0], (MICRO, ROWS, D), 1.0, 6.0, ((1, 32),)),
        "lengths": draw_lengths(jax.random.fold_in(splits[15], 71), 0),
        "cotangent": gaussian_with(splits[2], (MICRO, ROWS, D), 1.0, 6.0, ((1, 32),), (1, 2, 32, 2.75)),
        "attn_norm_gain": jnp.clip(1.0 + 0.1 * jax.random.normal(splits[3], (D,), jnp.float32), 0.5, 1.5).astype(jnp.bfloat16),
        "attn_norm_bias": gaussian(splits[4], (D,), 0.2, 1.0, ((0, 32),)),
        "qkv_weight": gaussian(splits[5], (D, 3 * D), D ** -0.5, 0.21875, ((0, 32),)),
        "qkv_bias": gaussian(splits[6], (3 * D,), 0.2, 1.0, ((0, 32),)),
        "out_weight": gaussian(splits[7], (D, D), (D // 8) ** -0.5, 0.625, ((0, 32),)),
        "out_bias": gaussian(splits[8], (D,), 0.2, 1.0, ((0, 32),)),
        "mlp_norm_gain": jnp.clip(1.0 + 0.1 * jax.random.normal(splits[9], (D,), jnp.float32), 0.5, 1.5).astype(jnp.bfloat16),
        "mlp_norm_bias": gaussian(splits[10], (D,), 0.2, 1.0, ((0, 32),)),
        "up_weight": gaussian(splits[11], (D, FF), D ** -0.5, 0.21875, ((0, 32),)),
        "up_bias": gaussian(splits[12], (FF,), 0.2, 1.0, ((0, 32),)),
        "down_weight": gaussian(splits[13], (FF, D), FF ** -0.5, 0.109375, ((0, 32),)),
        "down_bias": gaussian(splits[14], (D,), 0.2, 1.0, ((0, 32),)),
    }


@jax.custom_vjp
def low(v):
    return lax.optimization_barrier(v.astype(jnp.bfloat16)).astype(jnp.float32)

@jax.custom_vjp
def low_back(v):
    return v

def low_keep(v):
    return (low(v), None)

def low_pass(kept, grad):
    return (grad,)

def back_keep(v):
    return (v, None)

def back_low(kept, grad):
    return (low(grad),)
low.defvjp(low_keep, low_pass)
low_back.defvjp(back_keep, back_low)

def matmul(left, right):
    return jnp.dot(left, right, precision=lax.Precision.HIGHEST, preferred_element_type=jnp.float32)

def layer_norm(inputs, gain, shift):
    centred = inputs - lax.optimization_barrier(jnp.mean(inputs, axis=-1, keepdims=True))
    spread = lax.optimization_barrier(jnp.mean(centred * centred, axis=-1, keepdims=True))
    return centred * lax.rsqrt(spread + 1e-05) * gain + shift

def seq_masks(seq_lens, row_count):
    seq_ends = jnp.cumsum(seq_lens, dtype=jnp.int32)
    places = jnp.arange(row_count, dtype=jnp.int32)
    segment = lax.optimization_barrier(jnp.sum((seq_ends[None, :] <= places[:, None]).astype(jnp.int32), axis=1))
    allowed = (segment[:, None] == segment[None, :]) & (places[None, :] <= places[:, None])
    return allowed

def row_forward(params, inputs, seq_lens):
    gain_one, bias_one, weight_qkv, bias_qkv, weight_out, bias_out, gain_two, bias_two, weight_up, bias_up, weight_down, bias_down = params
    row_count = inputs.shape[0]
    allowed = seq_masks(seq_lens, row_count)
    normed_one = low(layer_norm(inputs, gain_one, bias_one))
    merged = low_back(low(matmul(normed_one, weight_qkv) + bias_qkv))
    queries = merged[:, :D].reshape(row_count, HEADS, HEAD)
    keys_all = merged[:, D:2 * D].reshape(row_count, HEADS, HEAD)
    values_all = merged[:, 2 * D:].reshape(row_count, HEADS, HEAD)
    scores = low_back(jnp.einsum('qhd,khd->hqk', queries, keys_all, precision=lax.Precision.HIGHEST) * HEAD ** (-0.5))
    magnitude = jnp.sqrt(scores * scores + 1.0)
    masked = jnp.where(allowed[None], magnitude, -jnp.inf)
    log_total = jax.nn.logsumexp(masked, axis=-1, keepdims=True)
    signed = jnp.tanh(scores) * jnp.exp(masked - log_total)
    mixed = jnp.einsum('hqk,khd->qhd', low(signed), values_all, precision=lax.Precision.HIGHEST)
    mixed = low_back(low(mixed.reshape(row_count, D)))
    hidden = inputs + low_back(matmul(mixed, weight_out) + bias_out)
    normed_two = low(layer_norm(hidden, gain_two, bias_two))
    pre_act = low_back(matmul(normed_two, weight_up) + bias_up)
    activated = low(jax.nn.gelu(pre_act))
    return hidden + low_back(matmul(activated, weight_down) + bias_down)

def reference(tokens, lengths, cotangent, attn_norm_gain, attn_norm_bias, qkv_weight, qkv_bias, out_weight, out_bias, mlp_norm_gain, mlp_norm_bias, up_weight, up_bias, down_weight, down_bias):
    params = tuple((item.astype(jnp.float32) for item in (attn_norm_gain, attn_norm_bias, qkv_weight, qkv_bias, out_weight, out_bias, mlp_norm_gain, mlp_norm_bias, up_weight, up_bias, down_weight, down_bias)))
    inputs = tokens.astype(jnp.float32).reshape(-1, ROW, tokens.shape[2])
    seq_table = lengths.reshape(-1, lengths.shape[2])
    seq_ends = jnp.cumsum(seq_table, axis=1, dtype=jnp.int32)
    valid = (jnp.arange(ROW, dtype=jnp.int32)[None, :] < seq_ends[:, -1:]).astype(jnp.float32)

    def whole(param_set, all_inputs):
        step_fn = jax.checkpoint(lambda row_pair: row_forward(param_set, row_pair[0], row_pair[1]))
        return lax.map(step_fn, (all_inputs, seq_table))
    result, pullback = jax.vjp(whole, params, inputs)
    seed_grad = cotangent.astype(jnp.float32).reshape(inputs.shape) * valid[:, :, None]
    param_grads, input_grad = pullback(seed_grad)
    grad_gain_one, grad_bias_one, grad_qkv, grad_bias_qkv, grad_out, grad_bias_out, grad_gain_two, grad_bias_two, grad_up, grad_bias_up, grad_down, grad_bias_down = param_grads
    return (result.reshape(tokens.shape).astype(jnp.bfloat16), input_grad.reshape(tokens.shape).astype(jnp.bfloat16), grad_gain_one, grad_bias_one, grad_qkv, grad_bias_qkv, grad_out, grad_bias_out, grad_gain_two, grad_bias_two, grad_up, grad_bias_up, grad_down, grad_bias_down)
```

```python
import jax
import jax.numpy as jnp
from jax import lax
from jax.experimental import pallas as pl
from jax.experimental.pallas import tpu as pltpu
from jax.sharding import PartitionSpec as P

HEAD = 64
PAIR = 2 * HEAD
SCALE = HEAD ** (-0.5)
AXES = ("dp", "fsdp")
F32 = jnp.float32
BF16 = jnp.bfloat16
HIDE = -1e30
GELU = 0.7978845608028654


def contract(left, right, left_dim, right_dim):
    return lax.dot_general(
        left, right, (((left_dim,), (right_dim,)), ((), ())), preferred_element_type=F32
    )


def mult(left, right):
    return contract(left, right, 1, 0)


def cross_rows(left, right):
    return contract(left, right, 0, 0)


def back_mult(grad_rows, weight):
    return contract(grad_rows, weight, 1, 1)


def normalize(inputs):
    centred = inputs - jnp.mean(inputs, axis=-1, keepdims=True)
    root = lax.rsqrt(jnp.mean(centred * centred, axis=-1, keepdims=True) + 1e-05)
    return centred * root, root


def norm_back(normed, root, grad, gain):
    scaled = grad * gain
    return root * (
        scaled
        - jnp.mean(scaled, axis=-1, keepdims=True)
        - normed * jnp.mean(scaled * normed, axis=-1, keepdims=True)
    )


def gelu_parts(u):
    smooth = jnp.tanh(GELU * (u + 0.044715 * (u * u * u)))
    slope = 0.5 * (1.0 + smooth) + 0.5 * u * (1.0 - smooth * smooth) * GELU * (
        1.0 + 3 * 0.044715 * u * u
    )
    return 0.5 * u * (1.0 + smooth), slope


def allowed_bias(key_seg, query_seg, row):
    keys = lax.broadcasted_iota(jnp.int32, (row, row), 0)
    queries = lax.broadcasted_iota(jnp.int32, (row, row), 1)
    return jnp.where((key_seg == query_seg) & (keys <= queries), 0.0, HIDE)


def forward_kernel(q_ref, k_ref, v_ref, key_seg, query_seg, mixed_ref, total_ref, bias):
    row = q_ref.shape[0]
    half = row // 2

    @pl.when(pl.program_id(1) == 0)
    def _():
        bias[...] = allowed_bias(key_seg[0], query_seg[0], row)

    lane = lax.broadcasted_iota(jnp.int32, (1, PAIR), 1)
    keys = k_ref[...]
    values = v_ref[...].T
    for part in range(2):
        here = slice(part * half, (part + 1) * half)
        seen = (part + 1) * half
        queries = q_ref[here, :] * jnp.asarray(SCALE, BF16)
        both = []
        for head in range(2):
            own = (lane < HEAD) == (head == 0)
            scores = back_mult(keys[:seen], jnp.where(own, queries, jnp.zeros((), BF16)))
            square = scores * scores + 1.0
            shown = square * lax.rsqrt(square) + bias[:seen, here]
            top = jnp.max(shown, axis=0, keepdims=True)
            weight = jnp.exp(shown - top)
            total = jnp.sum(weight, axis=0, keepdims=True)
            signed = (jnp.tanh(scores) * weight).astype(BF16)
            mixed = mult(values[head * HEAD : (head + 1) * HEAD, :seen], signed)
            both.append(mixed * (1.0 / total))
            total_ref[0, 0, head : head + 1, here] = top + jnp.log(total)
        mixed_ref[here, :] = jnp.concatenate(both, axis=0).T.astype(BF16)


def attention_forward(merged, key_seg, query_seg, row):
    count, width = merged.shape
    model = width // 3
    pairs = model // PAIR
    rows = count // row
    area = rows * pairs * 2 * row * row
    return pl.pallas_call(
        forward_kernel,
        grid=(rows, pairs),
        in_specs=[
            pl.BlockSpec((row, PAIR), lambda r, h: (r, h)),
            pl.BlockSpec((row, PAIR), lambda r, h: (r, h + pairs)),
            pl.BlockSpec((row, PAIR), lambda r, h: (r, h + 2 * pairs)),
            pl.BlockSpec((1, row, 1), lambda r, h: (r, 0, 0)),
            pl.BlockSpec((1, 1, row), lambda r, h: (r, 0, 0)),
        ],
        out_specs=[
            pl.BlockSpec((row, PAIR), lambda r, h: (r, h)),
            pl.BlockSpec((1, 1, 2, row), lambda r, h: (r, h, 0, 0)),
        ],
        out_shape=[
            jax.ShapeDtypeStruct((count, model), BF16),
            jax.ShapeDtypeStruct((rows, pairs, 2, row), F32),
        ],
        scratch_shapes=[pltpu.VMEM((row, row), F32)],
        compiler_params=pltpu.CompilerParams(vmem_limit_bytes=40 * 2**20),
        cost_estimate=pl.CostEstimate(
            flops=area * 4 * HEAD * 6, bytes_accessed=count * width * 3, transcendentals=area * 3
        ),
        name="attention_forward",
    )(merged, merged, merged, key_seg, query_seg)


def backward_kernel(
    q_ref, k_ref, v_ref, mixed_ref, grad_ref, total_ref, key_seg, query_seg, dq_ref, dk_ref, dv_ref, bias
):
    row = q_ref.shape[0]
    half = row // 2

    @pl.when(pl.program_id(1) == 0)
    def _():
        bias[...] = allowed_bias(key_seg[0], query_seg[0], row)

    lane = lax.broadcasted_iota(jnp.int32, (1, PAIR), 1)
    keys = k_ref[...]
    values = v_ref[...]
    turned = keys.T
    key_grads = [jnp.zeros((half, PAIR), F32) for _ in range(2)]
    value_grads = [jnp.zeros((half, PAIR), F32) for _ in range(2)]
    for part in range(2):
        here = slice(part * half, (part + 1) * half)
        seen = (part + 1) * half
        queries = q_ref[here, :] * jnp.asarray(SCALE, BF16)
        grads = grad_ref[here, :]
        centres = (grads.astype(F32) * mixed_ref[here, :].astype(F32)).T
        both = []
        for head in range(2):
            span = slice(head * HEAD, (head + 1) * HEAD)
            own = (lane < HEAD) == (head == 0)
            head_queries = jnp.where(own, queries, jnp.zeros((), BF16))
            head_grads = jnp.where(own, grads, jnp.zeros((), BF16))
            centre = jnp.sum(centres[span], axis=0, keepdims=True)
            scores = back_mult(keys[:seen], head_queries)
            weight_grad = back_mult(values[:seen], head_grads)
            square = scores * scores + 1.0
            root = lax.rsqrt(square)
            weight = jnp.exp(
                square * root + (bias[:seen, here] - total_ref[0, 0, head : head + 1, here])
            )
            smooth = jnp.tanh(scores)
            signed = (smooth * weight).astype(BF16)
            bent = weight_grad * smooth
            score_grad = weight * (
                (weight_grad - bent * smooth) + (scores * root) * (bent - centre)
            )
            score_grad = score_grad.astype(BF16)
            value_part = mult(signed, head_grads)
            key_part = mult(score_grad, head_queries)
            for block in range(part + 1):
                rows = slice(block * half, (block + 1) * half)
                value_grads[block] = value_grads[block] + value_part[rows]
                key_grads[block] = key_grads[block] + key_part[rows]
            both.append(mult(turned[span, :seen], score_grad))
        dq_ref[here, :] = (jnp.concatenate(both, axis=0).T * SCALE).astype(BF16)
    for block in range(2):
        rows = slice(block * half, (block + 1) * half)
        dk_ref[rows, :] = key_grads[block].astype(BF16)
        dv_ref[rows, :] = value_grads[block].astype(BF16)


def attention_backward(merged, mixed, mixed_grad, total, key_seg, query_seg, row):
    count, width = merged.shape
    model = width // 3
    pairs = model // PAIR
    rows = count // row
    area = rows * pairs * 2 * row * row
    block = pl.BlockSpec((row, PAIR), lambda r, h: (r, h))
    return pl.pallas_call(
        backward_kernel,
        grid=(rows, pairs),
        in_specs=[
            block,
            pl.BlockSpec((row, PAIR), lambda r, h: (r, h + pairs)),
            pl.BlockSpec((row, PAIR), lambda r, h: (r, h + 2 * pairs)),
            block,
            block,
            pl.BlockSpec((1, 1, 2, row), lambda r, h: (r, h, 0, 0)),
            pl.BlockSpec((1, row, 1), lambda r, h: (r, 0, 0)),
            pl.BlockSpec((1, 1, row), lambda r, h: (r, 0, 0)),
        ],
        out_specs=[block, block, block],
        out_shape=[jax.ShapeDtypeStruct((count, model), BF16)] * 3,
        scratch_shapes=[pltpu.VMEM((row, row), F32)],
        compiler_params=pltpu.CompilerParams(vmem_limit_bytes=40 * 2**20),
        cost_estimate=pl.CostEstimate(
            flops=area * 10 * HEAD * 4, bytes_accessed=count * width * 5, transcendentals=area * 3
        ),
        name="attention_backward",
    )(merged, merged, merged, mixed, mixed_grad, total, key_seg, query_seg)


class Links:
    def __init__(self, mesh):
        self.outer = mesh.shape["dp"]
        self.inner = mesh.shape["fsdp"]
        self.count = self.outer * self.inner
        self.far = [(k << 2) * self.inner for k in range(self.outer // 4)]
        self.near = [(b << 1) * self.inner + f for b in range(2) for f in range(self.inner)]
        self.core = self.inner

    def place(self):
        return lax.axis_index("dp") * self.inner + lax.axis_index("fsdp")

    def swap(self, piece, mask):
        return lax.ppermute(piece, AXES, [(i, i ^ mask) for i in range(self.count)])

    def spread(self, shard):
        column = jnp.stack([shard] + [self.swap(shard, mask) for mask in self.far[1:]])
        plane = [column] + [self.swap(column, mask) for mask in self.near[1:]]
        return plane + [self.swap(piece, self.core) for piece in plane]

    def arrange(self, pieces, columns):
        masks = self.near + [mask ^ self.core for mask in self.near]
        far = self.far
        held = len(pieces)
        rows = pieces[0].shape[1]

        def kernel(me_ref, *refs):
            targets, sem = refs[held:-1], refs[-1]
            me = me_ref[0]
            copies = []
            for piece, mask in zip(refs[:held], masks):
                for k, step in enumerate(far):
                    owner = jnp.bitwise_xor(me, mask ^ step)
                    for target, (start, width, parts) in zip(targets, columns):
                        for part in range(parts):
                            copies.append(
                                pltpu.make_async_copy(
                                    piece.at[k, :, pl.ds(start + part * width, width)],
                                    target.at[owner * parts + part],
                                    sem,
                                )
                            )
            for copy in copies:
                copy.start()
            for copy in copies:
                copy.wait()

        return pl.pallas_call(
            kernel,
            in_specs=[pl.BlockSpec(memory_space=pltpu.SMEM)]
            + [pl.BlockSpec(memory_space=pl.ANY)] * held,
            out_specs=[pl.BlockSpec(memory_space=pltpu.VMEM)] * len(columns),
            out_shape=[
                jax.ShapeDtypeStruct((self.count * parts, rows, width), BF16)
                for _, width, parts in columns
            ],
            scratch_shapes=[pltpu.SemaphoreType.DMA],
            compiler_params=pltpu.CompilerParams(vmem_limit_bytes=40 * 2**20),
            name="arrange",
        )(jnp.full((1,), self.place(), jnp.int32), *pieces)

    def reduce(self, grads, join):
        dp = lax.axis_index("dp")
        core, side, column, inner = dp & 1, (dp >> 1) & 1, dp >> 2, lax.axis_index("fsdp")

        def pick(array, index, axis):
            return lax.dynamic_index_in_dim(array, index, axis, keepdims=False)

        views = [
            grad.reshape((self.outer // 4, 2, 2, self.inner) + grad.shape[1:]) for grad in grads
        ]
        got = [self.swap(pick(view, 1 - core, 2), self.core) for view in views]
        mine = [pick(view, core, 2) for view in views]
        sums = []
        for b in range(2):
            for f in range(self.inner):

                def cut(array):
                    return pick(pick(array, side ^ b, 1), inner ^ f, 1).astype(F32)

                sums.append(join([(cut(a) + cut(b)).astype(BF16) for a, b in zip(mine, got)]))
        sums = sums[:1] + [self.swap(part, mask) for part, mask in zip(sums[1:], self.near[1:])]
        result = None
        for k, mask in enumerate(self.far):
            part = sum(pick(array, column ^ k, 0).astype(F32) for array in sums)
            if k == 0:
                result = part
            else:
                result = result + self.swap(part.astype(BF16), mask).astype(F32)
        return result


def run(
    links,
    tokens,
    lengths,
    cotangent,
    attn_norm_gain,
    attn_norm_bias,
    qkv_weight,
    qkv_bias,
    out_weight,
    out_bias,
    mlp_norm_gain,
    mlp_norm_bias,
    up_weight,
    up_bias,
    down_weight,
    down_bias,
):
    micro, row, model = tokens.shape
    count = micro * row
    shard = qkv_weight.shape[0]
    wide = up_weight.shape[1]
    wide_parts = wide // model
    devices = links.count

    vectors = (
        attn_norm_gain,
        attn_norm_bias,
        qkv_bias,
        out_bias,
        mlp_norm_gain,
        mlp_norm_bias,
        up_bias,
        down_bias,
    )
    extra = jnp.concatenate([vector.reshape(shard, -1) for vector in vectors], axis=1)
    extra = jnp.pad(extra, ((0, 0), (0, PAIR - extra.shape[1])))
    first_pieces = links.spread(jnp.concatenate([qkv_weight, extra], axis=1))
    rest = jnp.concatenate(
        [out_weight, up_weight]
        + [down_weight[part * shard : (part + 1) * shard] for part in range(wide_parts)],
        axis=1,
    )
    rest_pieces = links.spread(rest)
    full_qkv, full_extra = links.arrange(first_pieces, [(0, 3 * model, 1), (3 * model, PAIR, 1)])
    full_qkv = full_qkv.reshape(model, 3 * model)
    full_extra = full_extra.reshape(model, PAIR).T.astype(F32)
    full_vectors = []
    at = 0
    for vector in vectors:
        parts = vector.shape[0] // shard
        full_vectors.append(full_extra[at : at + parts].T.reshape(1, -1))
        at += parts
    gain_one, bias_one, bias_qkv, bias_out, gain_two, bias_two, bias_up, bias_down = full_vectors

    ends = jnp.cumsum(lengths.reshape(micro, -1), axis=1, dtype=jnp.int32)
    places = jnp.arange(row, dtype=jnp.int32)
    segment = jnp.sum((ends[:, None, :] <= places[None, :, None]).astype(jnp.int32), axis=2)
    valid = (places[None, :] < ends[:, -1:]).reshape(count, 1)
    key_seg, query_seg = segment[:, :, None], segment[:, None, :]

    residual = tokens.reshape(count, model).astype(F32)
    unit_one, root_one = normalize(residual)
    normed_one = (unit_one * gain_one + bias_one).astype(BF16)
    merged = (mult(normed_one, full_qkv) + bias_qkv).astype(BF16)
    mixed, log_total = attention_forward(merged, key_seg, query_seg, row)

    full_out, full_up, full_down = links.arrange(
        rest_pieces, [(0, model, 1), (model, wide, 1), (model + wide, model, wide_parts)]
    )
    full_out = full_out.reshape(model, model)
    full_up = full_up.reshape(model, wide)
    full_down = full_down.reshape(wide, model)

    hidden = residual + mult(mixed, full_out) + bias_out
    unit_two, root_two = normalize(hidden)
    normed_two = (unit_two * gain_two + bias_two).astype(BF16)
    pre_act = mult(normed_two, full_up) + bias_up
    activated, slope = gelu_parts(pre_act)
    activated = activated.astype(BF16)
    block_out = (hidden + mult(activated, full_down) + bias_down).astype(BF16)

    down_grad = jnp.where(valid, cotangent.reshape(count, model), jnp.zeros((), BF16))
    out_grad = down_grad.astype(F32)
    grad_down = cross_rows(activated, down_grad)
    grad_bias_down = jnp.sum(out_grad, axis=0)
    up_grad = (slope * back_mult(down_grad, full_down)).astype(BF16)
    grad_up = cross_rows(normed_two, up_grad)
    grad_bias_up = jnp.sum(up_grad.astype(F32), axis=0)
    normed_grad = back_mult(up_grad, full_up)
    grad_gain_two = jnp.sum(normed_grad * unit_two, axis=0)
    grad_bias_two = jnp.sum(normed_grad, axis=0)
    hidden_grad = out_grad + norm_back(unit_two, root_two, normed_grad, gain_two)
    proj_grad = hidden_grad.astype(BF16)
    grad_out = cross_rows(mixed, proj_grad)
    grad_bias_out = jnp.sum(proj_grad.astype(F32), axis=0)

    late = links.reduce(
        [
            grad_out.astype(BF16).reshape(devices, shard, model),
            grad_up.astype(BF16).reshape(devices, shard, wide),
            grad_down.astype(BF16).reshape(devices, wide_parts * shard, model),
        ],
        lambda cuts: jnp.concatenate(
            [cuts[0], cuts[2]]
            + [cuts[1][:, :, part * model : (part + 1) * model] for part in range(wide_parts)],
            axis=1,
        ),
    )
    out_shard = late[:shard]
    down_shard = late[shard : shard * (1 + wide_parts)]
    up_shard = late[shard * (1 + wide_parts) :].reshape(wide_parts, shard, model)
    up_shard = jnp.concatenate([up_shard[part] for part in range(wide_parts)], axis=1)

    mixed_grad = back_mult(proj_grad, full_out).astype(BF16)
    merged_grad = jnp.concatenate(
        attention_backward(merged, mixed, mixed_grad, log_total, key_seg, query_seg, row), axis=1
    )
    grad_qkv = cross_rows(normed_one, merged_grad)
    grad_bias_qkv = jnp.sum(merged_grad.astype(F32), axis=0)
    first_grad = back_mult(merged_grad, full_qkv)
    grad_gain_one = jnp.sum(first_grad * unit_one, axis=0)
    grad_bias_one = jnp.sum(first_grad, axis=0)
    token_grad = (hidden_grad + norm_back(unit_one, root_one, first_grad, gain_one)).astype(BF16)

    sums = (
        grad_gain_one,
        grad_bias_one,
        grad_bias_qkv,
        grad_bias_out,
        grad_gain_two,
        grad_bias_two,
        grad_bias_up,
        grad_bias_down,
    )
    tail = jnp.concatenate([total.reshape(model, -1) for total in sums], axis=1)
    tail = jnp.pad(tail, ((0, 0), (0, PAIR - tail.shape[1])))
    last = links.reduce(
        [
            grad_qkv.astype(BF16).reshape(devices, shard, 3 * model),
            tail.astype(BF16).reshape(devices, shard, PAIR),
        ],
        lambda cuts: jnp.concatenate(cuts, axis=2),
    )
    parts = []
    at = 3 * model
    for vector in vectors:
        width = vector.shape[0] // shard
        parts.append(last[:, at : at + width].reshape(-1))
        at += width
    (
        gain_one_shard,
        bias_one_shard,
        bias_qkv_shard,
        bias_out_shard,
        gain_two_shard,
        bias_two_shard,
        bias_up_shard,
        bias_down_shard,
    ) = parts
    return (
        block_out.reshape(tokens.shape),
        token_grad.reshape(tokens.shape),
        gain_one_shard,
        bias_one_shard,
        last[:, : 3 * model],
        bias_qkv_shard,
        out_shard,
        bias_out_shard,
        gain_two_shard,
        bias_two_shard,
        up_shard,
        bias_up_shard,
        down_shard,
        bias_down_shard,
    )


def solution(mesh):
    links = Links(mesh)
    rows = P(None, AXES, None)
    vector = P(AXES)
    matrix = P(AXES, None)
    params = (
        vector,
        vector,
        matrix,
        vector,
        matrix,
        vector,
        vector,
        vector,
        matrix,
        vector,
        matrix,
        vector,
    )
    return jax.shard_map(
        lambda *args: run(links, *args),
        mesh=mesh,
        in_specs=(rows, rows, rows) + params,
        out_specs=(rows, rows) + params,
        check_vma=False,
    )
```

```python
import functools

import jax
import jax.numpy as jnp
from jax import lax
from jax.experimental import pallas as pl
from jax.experimental.pallas import tpu as pltpu
from jax.sharding import PartitionSpec as P

HEAD = 64
PAIR = 2 * HEAD
LANES = 128
SCALE = HEAD ** (-0.5)
AXES = ("dp", "fsdp")
F32 = jnp.float32
BF16 = jnp.bfloat16
HIDE = -1e30
LOG2E = 1.4426950408889634
GELU = 0.7978845608028654
ONCE = pl.Buffered(1)


def contract(left, right, left_dim, right_dim):
    return lax.dot_general(
        left, right, (((left_dim,), (right_dim,)), ((), ())), preferred_element_type=F32
    )


def mult(left, right):
    return contract(left, right, 1, 0)


def cross_rows(left, right):
    return contract(left, right, 0, 0)


def back_mult(grad_rows, weight):
    return contract(grad_rows, weight, 1, 1)


def normalize(inputs):
    centred = inputs - jnp.mean(inputs, axis=-1, keepdims=True)
    root = lax.rsqrt(jnp.mean(centred * centred, axis=-1, keepdims=True) + 1e-05)
    return centred * root, root


def norm_back(normed, root, grad, gain):
    scaled = grad * gain
    return root * (
        scaled
        - jnp.mean(scaled, axis=-1, keepdims=True)
        - normed * jnp.mean(scaled * normed, axis=-1, keepdims=True)
    )


def column_sum(values):
    return jnp.sum(values, axis=0, keepdims=True)


def gate(values, *others):
    return lax.optimization_barrier((values, others))[0]


def whole(array):
    return pl.BlockSpec(array.shape, lambda i: (0,) * array.ndim, pipeline_mode=ONCE)


def token_rows(tile, width):
    return pl.BlockSpec((tile, width), lambda i: (i, 0))


def vector_out(width):
    return pl.BlockSpec((1, width), lambda i: (0, 0))


def shape(*dims, kind=BF16):
    return jax.ShapeDtypeStruct(dims, kind)


def kernel_limits(mib=60):
    return pltpu.CompilerParams(vmem_limit_bytes=mib * 2**20)


def cost(flops, size, transcendentals=0):
    return pl.CostEstimate(
        flops=flops // 4, bytes_accessed=size // 4, transcendentals=transcendentals // 4
    )


def first_step(*refs):
    @pl.when(pl.program_id(0) == 0)
    def _():
        for ref in refs:
            ref[...] = jnp.zeros_like(ref)


def qkv_forward_kernel(x_ref, vectors, weight, normed_ref, merged_ref, *, sub):
    count, model = x_ref.shape

    def norm(start):
        unit, _ = normalize(x_ref[start : start + sub, :].astype(F32))
        normed = (unit * vectors[0:1, :model] + vectors[1:2, :model]).astype(BF16)
        normed_ref[start : start + sub, :] = normed
        return normed

    normed = norm(0)
    for start in range(0, count, sub):
        later = norm(start + sub) if start + sub < count else None
        merged = mult(normed, weight[...]) + vectors[2:3, : 3 * model]
        merged_ref[start : start + sub, :] = merged.astype(BF16)
        normed = later


def qkv_forward(inputs, vectors, weight, tile=512, sub=128):
    count, model = inputs.shape
    width = weight.shape[1]
    return pl.pallas_call(
        functools.partial(qkv_forward_kernel, sub=sub),
        grid=(count // tile,),
        in_specs=[token_rows(tile, model), whole(vectors), whole(weight)],
        out_specs=[token_rows(tile, model), token_rows(tile, width)],
        out_shape=[shape(count, model), shape(count, width)],
        compiler_params=kernel_limits(),
        cost_estimate=cost(
            2 * count * model * width, 2 * (2 * count * model + (count + model) * width)
        ),
        name="qkv_forward",
    )(inputs, vectors, weight)


def mlp_kernel(
    ends, mixed_ref, x_ref, cot_ref, vectors, w_out, w_up, w_down,
    hidden_ref, normed_ref, act_ref, up_grad_ref, down_grad_ref, proj_grad_ref, hidden_grad_ref,
    mixed_grad_ref, sum_gain, sum_shift, sum_up, sum_out, sum_down, *, row, sub, chunk
):
    first_step(sum_gain, sum_shift, sum_up, sum_out, sum_down)
    tile, model = x_ref.shape
    wide = w_up.shape[1]
    b_out, gain, shift = (vectors[k : k + 1, :model] for k in (3, 4, 5))
    step = pl.program_id(0)
    steps = row // tile
    last_end = ends[step // steps, ends.shape[1] - 1]
    units = [(start, at) for start in range(0, tile, sub) for at in range(0, wide, chunk)]
    normed, units_two, roots, totals = {}, {}, {}, {}

    def begin(start):
        rows = slice(start, start + sub)
        hidden = x_ref[rows, :].astype(F32) + mult(mixed_ref[rows, :], w_out[...]) + b_out
        hidden_ref[rows, :] = hidden
        units_two[start], roots[start] = normalize(hidden)
        normed[start] = (units_two[start] * gain + shift).astype(BF16)
        normed_ref[rows, :] = normed[start]
        place = lax.broadcasted_iota(jnp.int32, (sub, 1), 0) + (step % steps * tile + start)
        down_grad = jnp.where(place < last_end, cot_ref[rows, :], jnp.zeros((), BF16))
        down_grad_ref[rows, :] = down_grad
        sum_down[...] += column_sum(down_grad.astype(F32))

    def products(start, at):
        if start not in normed:
            begin(start)
        cols = slice(at, at + chunk)
        return (
            mult(normed[start], w_up[:, cols]) + vectors[6:7, cols],
            back_mult(down_grad_ref[start : start + sub, :], w_down[cols, :]),
        )

    def finish(start):
        rows = slice(start, start + sub)
        normed_grad = totals[start]
        sum_gain[...] += column_sum(normed_grad * units_two[start])
        sum_shift[...] += column_sum(normed_grad)
        hidden_grad = norm_back(units_two[start], roots[start], normed_grad, gain)
        hidden_grad = down_grad_ref[rows, :].astype(F32) + hidden_grad
        hidden_grad_ref[rows, :] = hidden_grad
        proj_grad = hidden_grad.astype(BF16)
        proj_grad_ref[rows, :] = proj_grad
        sum_out[...] += column_sum(proj_grad.astype(F32))
        mixed_grad_ref[rows, :] = back_mult(proj_grad, w_out[...]).astype(BF16)

    ready = products(*units[0])
    waiting = None
    for index, (start, at) in enumerate(units):
        u, act_grad = ready
        if index + 1 < len(units):
            ready = products(*units[index + 1])
        rows, cols = slice(start, start + sub), slice(at, at + chunk)
        square = u * u
        smooth = jnp.tanh(u * (GELU + (GELU * 0.044715) * square))
        part = 0.5 * smooth
        share = 0.5 + part
        act_ref[rows, cols] = (u * share).astype(BF16)
        slope = share + (u * (0.5 - part * smooth)) * (GELU + (3 * GELU * 0.044715) * square)
        up_grad = (slope * act_grad).astype(BF16)
        up_grad_ref[rows, cols] = up_grad
        sum_up[:, cols] += column_sum(up_grad.astype(F32))
        grad = back_mult(up_grad, w_up[:, cols])
        totals[start] = grad if start not in totals else totals[start] + grad
        if waiting is not None:
            finish(waiting)
            waiting = None
        if at + chunk == wide:
            waiting = start
    finish(waiting)


def mlp(ends, mixed, x, cot, vectors, w_out, w_up, w_down, row, tile=512, sub=512, chunk=768):
    count, model = x.shape
    wide = w_up.shape[1]
    consts = (vectors, w_out, w_up, w_down)
    widths = [(model, F32), (model, BF16), (wide, BF16), (wide, BF16), (model, BF16)]
    widths += [(model, BF16), (model, F32), (model, BF16)]
    sums = [model, model, wide, model, model]
    return pl.pallas_call(
        functools.partial(mlp_kernel, row=row, sub=sub, chunk=chunk),
        grid=(count // tile,),
        in_specs=[pl.BlockSpec(memory_space=pltpu.SMEM)]
        + [token_rows(tile, model)] * 3
        + [whole(item) for item in consts],
        out_specs=[token_rows(tile, width) for width, _ in widths]
        + [vector_out(width) for width in sums],
        out_shape=[shape(count, width, kind=kind) for width, kind in widths]
        + [shape(1, width, kind=F32) for width in sums],
        compiler_params=kernel_limits(),
        cost_estimate=cost(
            2 * count * model * (3 * wide + 2 * model), count * (26 * model + 4 * wide), count * wide
        ),
        name="mlp",
    )(ends, mixed, x, cot, *consts)


def mlp_out_kernel(hidden_ref, act_ref, vectors, w_down, out_ref):
    model = hidden_ref.shape[1]
    out = hidden_ref[...] + mult(act_ref[...], w_down[...]) + vectors[7:8, :model]
    out_ref[...] = out.astype(BF16)


def mlp_out(hidden, act, vectors, w_down, tile=256):
    count, model = hidden.shape
    wide = act.shape[1]
    return pl.pallas_call(
        mlp_out_kernel,
        grid=(count // tile,),
        in_specs=[token_rows(tile, model), token_rows(tile, wide), whole(vectors), whole(w_down)],
        out_specs=token_rows(tile, model),
        out_shape=shape(count, model),
        compiler_params=kernel_limits(),
        cost_estimate=cost(2 * count * model * wide, count * (6 * model + 2 * wide)),
        name="mlp_out",
    )(hidden, act, vectors, w_down)


def whole_grad_kernel(left_ref, right_ref, out_ref):
    out_ref[...] = cross_rows(left_ref[...], right_ref[...]).astype(out_ref.dtype)


def whole_grad(left, right, kind, name, tile=768):
    count, high = left.shape
    wide = right.shape[1]
    tile = min(tile, high)
    return pl.pallas_call(
        whole_grad_kernel,
        grid=(high // tile,),
        in_specs=[
            pl.BlockSpec((count, tile), lambda i: (0, i)),
            pl.BlockSpec((count, wide), lambda i: (0, 0), pipeline_mode=ONCE),
        ],
        out_specs=pl.BlockSpec((tile, wide), lambda i: (i, 0)),
        out_shape=shape(high, wide, kind=kind),
        compiler_params=kernel_limits(),
        cost_estimate=cost(
            2 * count * high * wide, 2 * (count * high + count * wide + 2 * high * wide)
        ),
        name=name,
    )(left, right)


def weight_grad_kernel(core_ref, left_ref, right_ref, keep, send, *, group):
    grad = cross_rows(left_ref[...], right_ref[...]).astype(BF16)
    halves = [
        jnp.concatenate(
            [grad[k : k + group] for k in range(which * group, grad.shape[0], 2 * group)], axis=0
        )
        for which in range(2)
    ]
    for core in range(2):

        @pl.when(core_ref[0] == core)
        def _():
            keep[...] = halves[core]
            send[...] = halves[1 - core]


def weight_grad(core, group, left, right, name, tile=768):
    count, high = left.shape
    wide = right.shape[1]
    tile = min(tile, wide)
    return pl.pallas_call(
        functools.partial(weight_grad_kernel, group=group),
        grid=(wide // tile,),
        in_specs=[
            pl.BlockSpec(memory_space=pltpu.SMEM),
            pl.BlockSpec((count, high), lambda i: (0, 0), pipeline_mode=ONCE),
            pl.BlockSpec((count, tile), lambda i: (0, i)),
        ],
        out_specs=[pl.BlockSpec((high // 2, tile), lambda i: (0, i))] * 2,
        out_shape=[shape(high // 2, wide)] * 2,
        compiler_params=kernel_limits(),
        cost_estimate=cost(
            2 * count * high * wide, 2 * (count * high + count * wide + high * wide)
        ),
        name=name,
    )(core, left, right)


def qkv_backward_kernel(
    grad_ref, x_ref, hidden_grad_ref, vectors, weight, out_ref, sum_gain, sum_shift, *, sub
):
    first_step(sum_gain, sum_shift)
    count, model = x_ref.shape
    gain = vectors[0:1, :model]

    def lower(start):
        return back_mult(grad_ref[start : start + sub, :], weight[...])

    ready = lower(0)
    for start in range(0, count, sub):
        normed_grad = ready
        if start + sub < count:
            ready = lower(start + sub)
        rows = slice(start, start + sub)
        unit, root = normalize(x_ref[rows, :].astype(F32))
        sum_gain[...] += column_sum(normed_grad * unit)
        sum_shift[...] += column_sum(normed_grad)
        inner = norm_back(unit, root, normed_grad, gain)
        out_ref[rows, :] = (hidden_grad_ref[rows, :] + inner).astype(BF16)


def qkv_backward(grad, x, hidden_grad, vectors, weight, tile=512, sub=256):
    count, model = x.shape
    width = weight.shape[1]
    return pl.pallas_call(
        functools.partial(qkv_backward_kernel, sub=sub),
        grid=(count // tile,),
        in_specs=[token_rows(tile, width)]
        + [token_rows(tile, model)] * 2
        + [whole(vectors), whole(weight)],
        out_specs=[token_rows(tile, model), vector_out(model), vector_out(model)],
        out_shape=[
            shape(count, model),
            shape(1, model, kind=F32),
            shape(1, model, kind=F32),
        ],
        compiler_params=kernel_limits(),
        cost_estimate=cost(
            2 * count * model * width, 2 * (4 * count * model + (count + model) * width)
        ),
        name="qkv_backward",
    )(grad, x, hidden_grad, vectors, weight)


def segments(ends, index, shape, axis):
    place = lax.broadcasted_iota(jnp.int32, shape, axis)
    found = jnp.zeros(shape, jnp.int32)
    for slot in range(ends.shape[1]):
        found = found + (ends[index, slot] <= place).astype(jnp.int32)
    return found


def allowed_bias(ends, row):
    index = pl.program_id(0)
    keys = lax.broadcasted_iota(jnp.int32, (row, row), 0)
    queries = lax.broadcasted_iota(jnp.int32, (row, row), 1)
    same = segments(ends, index, (row, 1), 0) == segments(ends, index, (1, row), 1)
    return jnp.where(same & (keys <= queries), 0.0, HIDE)


def pair_lanes(pair):
    return slice(pair * PAIR, (pair + 1) * PAIR)


def head_rows(head):
    return slice(head * HEAD, (head + 1) * HEAD)


def own_lanes(values, head):
    lane = lax.broadcasted_iota(jnp.int32, (1, PAIR), 1)
    return jnp.where((lane < HEAD) == (head == 0), values, jnp.zeros((), BF16))


def key_blocks(half, part, step):
    for start in range(0, (part + 1) * half, step):
        low = max(0, (start - part * half) // LANES * LANES) if start >= part * half else 0
        yield start, low


def widen(values, low, fill):
    if low == 0:
        return values
    pad = jnp.full((values.shape[0], low), fill, values.dtype)
    return jnp.concatenate([pad, values], axis=1)


def folded(values, combine):
    return combine(values.reshape(values.shape[0] // 8, 8, values.shape[1]), axis=0)


def unit_list(pairs):
    return [(pair, part, head) for pair in range(pairs) for part in range(2) for head in range(2)]


def forward_kernel(
    ends, q_ref, k_ref, v_ref, mixed_ref, total_ref, bias, *, pairs, step, lead
):
    row = q_ref.shape[0]
    half = row // 2
    bias[...] = allowed_bias(ends, row)

    def scores_of(pair, part, head):
        seen = (part + 1) * half
        queries = q_ref[part * half : seen, pair_lanes(pair)] * jnp.asarray(SCALE, BF16)
        return back_mult(k_ref[:seen, pair_lanes(pair)], own_lanes(queries, head))

    def weigh(part, scores):
        base = part * half
        top = jnp.full((8, half), HIDE, F32)
        shown = []
        for start, low in key_blocks(half, part, step):
            block = scores[start : start + step, low:]
            square = block * block + 1.0
            mag = square * (lax.rsqrt(square) * LOG2E)
            mag = mag + bias[start : start + step, base + low : base + half]
            shown.append(mag)
            top = jnp.maximum(top, widen(folded(mag, jnp.max), low, HIDE))
        top = jnp.max(top, axis=0, keepdims=True)
        total = jnp.zeros((8, half), F32)
        signed = []
        for (start, low), mag in zip(key_blocks(half, part, step), shown):
            weight = jnp.exp2(mag - top[:, low:])
            total = total + widen(folded(weight, jnp.sum), low, 0.0)
            block = jnp.tanh(scores[start : start + step, low:]) * weight
            signed.append(widen(block.astype(BF16), low, 0.0))
        return jnp.concatenate(signed, axis=0), top, jnp.sum(total, axis=0, keepdims=True)

    units = unit_list(pairs)
    scores = [scores_of(*unit) for unit in units[:lead]]
    turned, parts = {}, {}

    def finish(unit, signed, top, total):
        pair, part, head = unit
        here = slice(part * half, (part + 1) * half)
        total_ref[0, pair, head : head + 1, here] = top * (1.0 / LOG2E) + jnp.log(total)
        values = turned[pair][head_rows(head), : (part + 1) * half]
        parts[unit] = mult(values, signed) * (1.0 / total)
        if head == 1:
            both = jnp.concatenate([parts[pair, part, 0], parts[unit]], axis=0)
            mixed_ref[here, pair_lanes(pair)] = both.T.astype(BF16)

    waiting = None
    for index, unit in enumerate(units):
        if index + lead < len(units):
            scores.append(scores_of(*units[index + lead]))
        if unit[0] not in turned:
            turned[unit[0]] = v_ref[:, pair_lanes(unit[0])].T
        weighed = weigh(unit[1], scores[index])
        if waiting is not None:
            finish(*waiting)
        waiting = (unit,) + weighed
    finish(*waiting)


def attention_forward(ends, merged, row):
    count, width = merged.shape
    model = width // 3
    pairs = model // PAIR
    micro = count // row
    area = micro * pairs * 2 * row * row

    def third(index):
        return pl.BlockSpec((row, model), lambda r: (r, index))

    return pl.pallas_call(
        functools.partial(forward_kernel, pairs=pairs, step=32, lead=2),
        grid=(micro,),
        in_specs=[
            pl.BlockSpec(memory_space=pltpu.SMEM),
            third(0),
            third(1),
            third(2),
        ],
        out_specs=[
            pl.BlockSpec((row, model), lambda r: (r, 0)),
            pl.BlockSpec((1, pairs, 2, row), lambda r: (r, 0, 0, 0)),
        ],
        out_shape=[shape(count, model), shape(micro, pairs, 2, row, kind=F32)],
        scratch_shapes=[pltpu.VMEM((row, row), F32)],
        compiler_params=kernel_limits(),
        cost_estimate=cost(area * 4 * HEAD * 5, count * width * 3, area * 3),
        name="attention_forward",
    )(ends, merged, merged, merged)


def backward_kernel(
    ends, q_ref, k_ref, v_ref, mixed_ref, grad_ref, total_ref,
    out_ref, sum_ref, bias, *, pairs, step, lead, lag
):
    row = q_ref.shape[0]
    half = row // 2
    model = pairs * PAIR
    first_step(sum_ref)
    bias[...] = allowed_bias(ends, row)

    def put(section, pair, rows, values):
        cols = slice(section * model + pair * PAIR, section * model + (pair + 1) * PAIR)
        values = values.astype(BF16)
        out_ref[rows, cols] = values
        sum_ref[:, cols] += column_sum(values.astype(F32))

    def queries_and_grads(pair, part, head):
        here = slice(part * half, (part + 1) * half)
        queries = q_ref[here, pair_lanes(pair)] * jnp.asarray(SCALE, BF16)
        return own_lanes(queries, head), own_lanes(grad_ref[here, pair_lanes(pair)], head)

    def products(pair, part, head):
        seen = (part + 1) * half
        queries, grads = queries_and_grads(pair, part, head)
        return (
            back_mult(k_ref[:seen, pair_lanes(pair)], queries),
            back_mult(v_ref[:seen, pair_lanes(pair)], grads),
        )

    centres, turned, sums, query_parts = {}, {}, {}, {}

    def weigh(pair, part, head, scores, weight_grads):
        base = part * half
        here = slice(base, base + half)
        if (pair, part) not in centres:
            grads = grad_ref[here, pair_lanes(pair)].astype(F32)
            centres[pair, part] = (grads * mixed_ref[here, pair_lanes(pair)].astype(F32)).T
        centre = column_sum(centres[pair, part][head_rows(head)])
        total = total_ref[0, pair, head : head + 1, here] * LOG2E
        signed, score_grads = [], []
        for start, low in key_blocks(half, part, step):
            block = scores[start : start + step, low:]
            weight_grad = weight_grads[start : start + step, low:]
            square = block * block + 1.0
            root = lax.rsqrt(square)
            shift = bias[start : start + step, base + low : base + half] - total[:, low:]
            weight = jnp.exp2(square * (root * LOG2E) + shift)
            smooth = jnp.tanh(block)
            bent = weight_grad * smooth
            score_grad = weight * (
                (weight_grad - bent * smooth) + (block * root) * (bent - centre[:, low:])
            )
            signed.append(widen((smooth * weight).astype(BF16), low, 0.0))
            score_grads.append(widen(score_grad.astype(BF16), low, 0.0))
        return jnp.concatenate(signed, axis=0), jnp.concatenate(score_grads, axis=0)

    def finish(unit, signed, score_grads):
        pair, part, head = unit
        queries, grads = queries_and_grads(*unit)
        for section, grad in ((2, mult(signed, grads)), (1, mult(score_grads, queries))):
            for block in range(part + 1):
                add = grad[block * half : (block + 1) * half]
                key = (pair, section, block)
                sums[key] = add if key not in sums else sums[key] + add
        if pair not in turned:
            turned[pair] = k_ref[:, pair_lanes(pair)].T
        keys = turned[pair][head_rows(head), : (part + 1) * half]
        query_parts[unit] = mult(keys, score_grads)
        if head == 1:
            both = jnp.concatenate([query_parts[pair, part, 0], query_parts[unit]], axis=0)
            put(0, pair, slice(part * half, (part + 1) * half), both.T * SCALE)
        if head == 1 and part == 1:
            for section in (1, 2):
                for block in range(2):
                    rows = slice(block * half, (block + 1) * half)
                    put(section, pair, rows, sums[pair, section, block])

    units = unit_list(pairs)
    ready = [products(*unit) for unit in units[:lead]]
    waiting = []
    for index, unit in enumerate(units):
        if index + lead < len(units):
            ready.append(products(*units[index + lead]))
        waiting.append((unit,) + weigh(*unit, *ready[index]))
        ready[index] = None
        if len(waiting) > lag:
            finish(*waiting.pop(0))
    for item in waiting:
        finish(*item)


def attention_backward(ends, merged, mixed, mixed_grad, total, row):
    count, width = merged.shape
    model = width // 3
    pairs = model // PAIR
    micro = count // row
    area = micro * pairs * 2 * row * row

    def third(index):
        return pl.BlockSpec((row, model), lambda r: (r, index))

    return pl.pallas_call(
        functools.partial(backward_kernel, pairs=pairs, step=32, lead=1, lag=0),
        grid=(micro,),
        in_specs=[
            pl.BlockSpec(memory_space=pltpu.SMEM),
            third(0),
            third(1),
            third(2),
            third(0),
            third(0),
            pl.BlockSpec((1, pairs, 2, row), lambda r: (r, 0, 0, 0)),
        ],
        out_specs=[pl.BlockSpec((row, width), lambda r: (r, 0)), vector_out(width)],
        out_shape=[shape(count, width), shape(1, width, kind=F32)],
        scratch_shapes=[pltpu.VMEM((row, row), F32)],
        compiler_params=kernel_limits(),
        cost_estimate=cost(area * 10 * HEAD * 4, count * width * 5, area * 3),
        name="attention_backward",
    )(ends, merged, merged, merged, mixed, mixed_grad, total)


def vector_slots(lengths):
    slots, fill = [], []
    for length in lengths:
        row = next((r for r, used in enumerate(fill) if used + length <= LANES), len(fill))
        if row == len(fill):
            fill.append(0)
        slots.append((row, fill[row], length))
        fill[row] += length
    return slots, len(fill)


def lane_of(devices, length, first):
    size = devices * length
    place = lax.broadcasted_iota(jnp.int32, (LANES, size), 1).astype(F32)
    inside = place - length * jnp.floor((place + 0.5) * (1.0 / length))
    lane = lax.broadcasted_iota(jnp.int32, (LANES, size), 0).astype(F32)
    return (lane == inside + first).astype(BF16)


def owner_of(devices, length):
    size = devices * length
    place = lax.broadcasted_iota(jnp.int32, (devices, size), 1)
    start = lax.broadcasted_iota(jnp.int32, (devices, size), 0) * length
    return (place >= start) & (place < start + length)


def vectors_from_table(table, slots):
    devices = table.shape[1]
    longest = devices * max(length for _, _, length in slots)

    def kernel(table_ref, out):
        for index, (row, first, length) in enumerate(slots):
            spread = mult(table_ref[row], lane_of(devices, length, first))
            out[index : index + 1, : devices * length] = column_sum(
                jnp.where(owner_of(devices, length), spread, 0.0)
            )

    return pl.pallas_call(
        kernel,
        out_shape=shape(len(slots), longest, kind=F32),
        compiler_params=kernel_limits(40),
        name="vectors_from_table",
    )(table)


def split(values, size):
    quotient = jnp.floor((values + 0.5) * (1.0 / size))
    return quotient, values - size * quotient


def table_from_vectors(vectors, slots, rows, devices, inner, core):
    def kernel(core_ref, *refs):
        vector_refs, outs = refs[:-2], refs[-2:]
        filled = [jnp.zeros((devices, LANES), F32) for _ in range(rows)]
        for (row, first, length), ref in zip(slots, vector_refs):
            own = jnp.where(owner_of(devices, length), ref[...], 0.0).astype(BF16)
            filled[row] = filled[row] + back_mult(own, lane_of(devices, length, first))
        stacked = jnp.concatenate(filled, axis=0).astype(BF16)
        target = lax.broadcasted_iota(jnp.int32, (devices // 2 * rows, devices * rows), 0)
        target = target.astype(F32)
        source = lax.broadcasted_iota(jnp.int32, (devices // 2 * rows, devices * rows), 1)
        source = source.astype(F32)
        block, row = split(target, rows)
        chip, y = split(block, inner)
        match = [
            source == row * devices + (chip * 2 + which) * inner + y for which in range(2)
        ]
        halves = [mult(one.astype(BF16), stacked).astype(BF16) for one in match]
        for which in range(2):

            @pl.when(core_ref[0] == which)
            def _():
                outs[0][...] = halves[which]
                outs[1][...] = halves[1 - which]

    return pl.pallas_call(
        kernel,
        in_specs=[pl.BlockSpec(memory_space=pltpu.SMEM)]
        + [pl.BlockSpec(memory_space=pltpu.VMEM)] * len(vectors),
        out_shape=[shape(devices // 2 * rows, LANES)] * 2,
        compiler_params=kernel_limits(40),
        name="table_from_vectors",
    )(core, *vectors)


class Links:
    def __init__(self, mesh):
        self.outer = mesh.shape["dp"]
        self.inner = mesh.shape["fsdp"]
        self.count = self.outer * self.inner
        self.far = [(k << 2) * self.inner for k in range(self.outer // 4)]
        self.near = [(b << 1) * self.inner + f for b in range(2) for f in range(self.inner)]
        self.core = self.inner

    def place(self):
        return lax.axis_index("dp") * self.inner + lax.axis_index("fsdp")

    def swap(self, piece, mask):
        return lax.ppermute(piece, AXES, [(i, i ^ mask) for i in range(self.count)])

    def far_step(self, shard):
        got = [self.swap(shard, mask) for mask in self.far[1:]]
        return lambda *others: jnp.stack([shard] + gate(got, *others))

    def far_doubled(self, shard):
        column = shard[None]
        while column.shape[0] < len(self.far):
            column = jnp.concatenate([column, self.swap(column, self.far[column.shape[0]])])
        return column

    def near_step(self, column):
        return [column] + [self.swap(column, mask) for mask in self.near[1:]]

    def near_halves(self, column):
        if len(self.near) != 4:
            plane = self.near_step(column)
            return plane, lambda *others: gate(plane, *others)
        side, inner = [self.swap(column, mask) for mask in (self.near[2], self.near[1])]
        plane = [column, inner, side]
        width = half_columns(column)

        def second(*others):
            left, right = gate((inner[:, :, :width], side[:, :, width:]), *others)
            return plane + [self.swap(left, self.near[2]), self.swap(right, self.near[1])]

        return plane, second

    def core_step(self, plane):
        return plane + [self.swap(piece, self.core) for piece in plane]

    def arrange(self, pieces, columns):
        far = self.far
        held = len(pieces)
        masks, ranges = list(self.near), [(0, pieces[0].shape[2])] * len(self.near)
        if held > 2 * len(masks):
            half = half_columns(pieces[0])
            masks, ranges = masks + masks[-1:], ranges[:-1] + [(0, half), (half, ranges[0][1])]
        masks, ranges = masks + [mask ^ self.core for mask in masks], ranges * 2
        rows = pieces[0].shape[1]

        def kernel(me_ref, *refs):
            targets, sem = refs[held:-1], refs[-1]
            me = me_ref[0]
            copies = []
            for piece, mask, (low, high) in zip(refs[:held], masks, ranges):
                for k, step in enumerate(far):
                    owner = jnp.bitwise_xor(me, mask ^ step)
                    for target, (start, width, parts) in zip(targets, columns):
                        for part in range(parts):
                            base = start + part * width
                            one, two = max(low, base), min(high, base + width)
                            if one >= two:
                                continue
                            copies.append(
                                pltpu.make_async_copy(
                                    piece.at[k, :, pl.ds(one - low, two - one)],
                                    target.at[owner * parts + part, :, pl.ds(one - base, two - one)],
                                    sem,
                                )
                            )
            for copy in copies:
                copy.start()
            for copy in copies:
                copy.wait()

        return pl.pallas_call(
            kernel,
            in_specs=[pl.BlockSpec(memory_space=pltpu.SMEM)]
            + [pl.BlockSpec(memory_space=pl.ANY)] * held,
            out_specs=[pl.BlockSpec(memory_space=pltpu.VMEM)] * len(columns),
            out_shape=[
                jax.ShapeDtypeStruct((self.count * parts, rows, width), BF16)
                for _, width, parts in columns
            ],
            scratch_shapes=[pltpu.SemaphoreType.DMA],
            compiler_params=pltpu.CompilerParams(vmem_limit_bytes=40 * 2**20),
            name="arrange",
        )(jnp.full((1,), self.place(), jnp.int32), *pieces)

    def position(self):
        dp = lax.axis_index("dp")
        return dp >> 2, (dp >> 1) & 1, dp & 1, lax.axis_index("fsdp")

    def core_sums(self, grads, join):
        _, side, _, inner = self.position()

        def view(array):
            rows = array.shape[0] * 2 // self.count
            return array.reshape(self.outer // 4, 2, self.inner, rows, array.shape[1])

        mine = [view(keep) for keep, _ in grads]
        got = [view(self.swap(send, self.core)) for _, send in grads]

        def finish(*others):
            received = gate(got, *others)
            sums = []
            for b in range(2):
                for f in range(self.inner):

                    def cut(array):
                        return pick(pick(array, side ^ b, 1), inner ^ f, 1).astype(F32)

                    sums.append(
                        join([(cut(a) + cut(b)).astype(BF16) for a, b in zip(mine, received)])
                    )
            return sums

        return finish

    def near_sums(self, sums):
        return self.far_parts(
            sums[:1] + [self.swap(part, mask) for part, mask in zip(sums[1:], self.near[1:])]
        )

    def far_parts(self, got):
        column = self.position()[0]

        def finish(*others):
            received = gate(got, *others)
            parts = []
            for k in range(len(self.far)):
                part = sum(pick(array, column ^ k, 0).astype(F32) for array in received)
                parts.append(part if k == 0 else part.astype(BF16))
            return parts

        return finish

    def far_sums(self, parts):
        got = [self.swap(part, mask) for part, mask in zip(parts[1:], self.far[1:])]

        def finish(*others):
            received = gate(got, *others)
            return functools.reduce(lambda sum, part: sum + part.astype(F32), received, parts[0])

        return finish


def half_columns(array):
    return array.shape[2] // 2 // LANES * LANES


def pick(array, index, axis):
    return lax.dynamic_index_in_dim(array, index, axis, keepdims=False)


def run(
    links,
    tokens,
    lengths,
    cotangent,
    attn_norm_gain,
    attn_norm_bias,
    qkv_weight,
    qkv_bias,
    out_weight,
    out_bias,
    mlp_norm_gain,
    mlp_norm_bias,
    up_weight,
    up_bias,
    down_weight,
    down_bias,
):
    micro, row, model = tokens.shape
    count = micro * row
    shard = qkv_weight.shape[0]
    wide = up_weight.shape[1]
    devices = links.count

    vectors = (
        attn_norm_gain,
        attn_norm_bias,
        qkv_bias,
        out_bias,
        mlp_norm_gain,
        mlp_norm_bias,
        up_bias,
        down_bias,
    )
    slots, table_rows = vector_slots([vector.shape[0] for vector in vectors])
    lines = []
    for line in range(table_rows):
        held = [v for v, slot in zip(vectors, slots) if slot[0] == line]
        held = jnp.concatenate(held)
        lines.append(jnp.pad(held, (0, LANES - held.shape[0])))
    extra = jnp.pad(jnp.stack(lines), ((0, shard - table_rows), (0, 0)))
    qkv_far = links.far_step(jnp.concatenate([qkv_weight, extra], axis=1))
    middle_in = jnp.concatenate([out_weight, up_weight], axis=1)
    middle_column = links.far_doubled(middle_in)
    qkv_column = qkv_far()
    qkv_plane = links.near_step(qkv_column)
    w_down = lax.all_gather(down_weight, AXES, axis=0, tiled=True)
    middle_start, middle_corner = links.near_halves(gate(middle_column, qkv_plane))
    w_qkv, extra = links.arrange(
        links.core_step(qkv_plane), [(0, 3 * model, 1), (3 * model, LANES, 1)]
    )
    w_qkv = w_qkv.reshape(model, 3 * model)
    table = vectors_from_table(extra[:, :table_rows].swapaxes(0, 1), slots)

    ends = jnp.cumsum(lengths.reshape(micro, -1), axis=1, dtype=jnp.int32)
    inputs = tokens.reshape(count, model)
    normed_one, merged = qkv_forward(inputs, table, w_qkv)
    middle_plane = middle_corner(merged)
    mixed, log_total = attention_forward(ends, gate(merged, middle_start), row)
    middle_pieces = links.core_step(middle_plane[:3] + gate(middle_plane[3:], mixed))
    w_out, w_up = links.arrange(gate(middle_pieces, mixed), [(0, model, 1), (model, wide, 1)])
    w_out = w_out.reshape(model, model)
    w_up = w_up.reshape(model, wide)
    (
        hidden,
        normed_two,
        activated,
        up_grad,
        down_grad,
        proj_grad,
        hidden_grad,
        mixed_grad,
        sum_gain_two,
        sum_shift_two,
        sum_up,
        sum_out,
        sum_down,
    ) = mlp(
        ends, mixed, inputs, cotangent.reshape(count, model), table, w_out, w_up, w_down, row
    )

    core = jnp.full((1,), links.position()[2], jnp.int32)
    group = links.inner * shard
    grad_down = whole_grad(activated, down_grad, BF16, "grad_down")
    down_block = lax.psum_scatter(grad_down, AXES, scatter_dimension=0, tiled=True)
    down_block = down_block.astype(F32)
    grad_up = weight_grad(core, group, normed_two, gate(up_grad, grad_down), "grad_up")
    grad_out = weight_grad(core, group, mixed, gate(proj_grad, grad_up), "grad_out")
    early = links.core_sums(
        [grad_out, grad_up], lambda cuts: jnp.concatenate(cuts, axis=2)
    )(grad_out)
    early_parts = links.near_sums(early)
    qkv_grad, sum_qkv = attention_backward(
        ends, merged, mixed, gate(mixed_grad, early), log_total, row
    )
    early_parts = early_parts(qkv_grad)
    early_block = links.far_sums(early_parts)
    token_grad, sum_gain_one, sum_shift_one = qkv_backward(
        gate(qkv_grad, early_parts), inputs, hidden_grad, table, w_qkv
    )
    sums = (
        sum_gain_one,
        sum_shift_one,
        sum_qkv,
        sum_out,
        sum_gain_two,
        sum_shift_two,
        sum_up,
        sum_down,
    )
    small = table_from_vectors(sums, slots, table_rows, devices, links.inner, core)
    grad_qkv = weight_grad(core, group, normed_one, gate(qkv_grad, token_grad), "grad_qkv")

    def with_small(cuts):
        grad, lines = cuts
        return jnp.concatenate(
            [grad, jnp.pad(lines, ((0, 0), (0, shard - table_rows), (0, 0)))], axis=2
        )

    late = links.core_sums([grad_qkv, small], with_small)(grad_qkv)
    late_parts = links.near_sums(late)
    block_out = mlp_out(hidden, gate(activated, late, down_block), table, w_down)
    early_block = early_block(block_out)
    late_block = links.far_sums(late_parts(block_out))()
    (
        gain_one_shard,
        bias_one_shard,
        bias_qkv_shard,
        bias_out_shard,
        gain_two_shard,
        bias_two_shard,
        bias_up_shard,
        bias_down_shard,
    ) = [
        late_block[line, 3 * model + start : 3 * model + start + length]
        for line, start, length in slots
    ]
    return (
        block_out.reshape(tokens.shape),
        token_grad.reshape(tokens.shape),
        gain_one_shard,
        bias_one_shard,
        late_block[:, : 3 * model],
        bias_qkv_shard,
        early_block[:, :model],
        bias_out_shard,
        gain_two_shard,
        bias_two_shard,
        early_block[:, model:],
        bias_up_shard,
        down_block,
        bias_down_shard,
    )


def solution(mesh):
    links = Links(mesh)
    rows = P(None, AXES, None)
    vector = P(AXES)
    matrix = P(AXES, None)
    params = (
        vector,
        vector,
        matrix,
        vector,
        matrix,
        vector,
        vector,
        vector,
        matrix,
        vector,
        matrix,
        vector,
    )
    return jax.shard_map(
        lambda *args: run(links, *args),
        mesh=mesh,
        in_specs=(rows, rows, rows) + params,
        out_specs=(rows, rows) + params,
        check_vma=False,
    )
```

```python
import functools
import math

import jax
import jax.numpy as jnp
from jax import lax
from jax.experimental import pallas as pl
from jax.experimental.pallas import tpu as pltpu
from jax.sharding import PartitionSpec as P

HEAD = 64
PAIR = 2 * HEAD
LANES = 128
SCALE = HEAD ** (-0.5)
AXES = ("dp", "fsdp")
F32 = jnp.float32
BF16 = jnp.bfloat16
HIDE = -1e30
LOG2E = 1.4426950408889634
GELU = 0.7978845608028654
ONCE = pl.Buffered(1)


def contract(left, right, left_dim, right_dim):
    return lax.dot_general(
        left, right, (((left_dim,), (right_dim,)), ((), ())), preferred_element_type=F32
    )


def mult(left, right):
    return contract(left, right, 1, 0)


def cross_rows(left, right):
    return contract(left, right, 0, 0)


def back_mult(grad_rows, weight):
    return contract(grad_rows, weight, 1, 1)


def normalize(inputs):
    centred = inputs - jnp.mean(inputs, axis=-1, keepdims=True)
    root = lax.rsqrt(jnp.mean(centred * centred, axis=-1, keepdims=True) + 1e-05)
    return centred * root, root


def norm_back(normed, root, grad, gain):
    scaled = grad * gain
    return root * (
        scaled
        - jnp.mean(scaled, axis=-1, keepdims=True)
        - normed * jnp.mean(scaled * normed, axis=-1, keepdims=True)
    )


def column_sum(values):
    return jnp.sum(values, axis=0, keepdims=True)


def gate(values, *others):
    return lax.optimization_barrier((values, others))[0]


def whole(array):
    return pl.BlockSpec(array.shape, lambda i: (0,) * array.ndim, pipeline_mode=ONCE)


def token_rows(tile, width):
    return pl.BlockSpec((tile, width), lambda i: (i, 0))


def vector_out(width):
    return pl.BlockSpec((1, width), lambda i: (0, 0))


def shape(*dims, kind=BF16):
    return jax.ShapeDtypeStruct(dims, kind)


def kernel_limits(mib=60):
    return pltpu.CompilerParams(vmem_limit_bytes=mib * 2**20)


def cost(flops, size, transcendentals=0):
    return pl.CostEstimate(flops=flops, bytes_accessed=size, transcendentals=transcendentals)


def first_step(*refs):
    @pl.when(pl.program_id(0) == 0)
    def _():
        for ref in refs:
            ref[...] = jnp.zeros_like(ref)


def qkv_forward_kernel(x_ref, vectors, weight, normed_ref, merged_ref, *, sub):
    count, model = x_ref.shape

    def norm(start):
        unit, _ = normalize(x_ref[start : start + sub, :].astype(F32))
        normed = (unit * vectors[0:1, :model] + vectors[1:2, :model]).astype(BF16)
        normed_ref[start : start + sub, :] = normed
        return normed

    normed = norm(0)
    for start in range(0, count, sub):
        later = norm(start + sub) if start + sub < count else None
        merged = mult(normed, weight[...]) + vectors[2:3, : 3 * model]
        merged_ref[start : start + sub, :] = merged.astype(BF16)
        normed = later


def qkv_forward(inputs, vectors, weight, tile=512, sub=128):
    count, model = inputs.shape
    width = weight.shape[1]
    return pl.pallas_call(
        functools.partial(qkv_forward_kernel, sub=sub),
        grid=(count // tile,),
        in_specs=[token_rows(tile, model), whole(vectors), whole(weight)],
        out_specs=[token_rows(tile, model), token_rows(tile, width)],
        out_shape=[shape(count, model), shape(count, width)],
        compiler_params=kernel_limits(60),
        cost_estimate=cost(
            2 * count * model * width, 2 * (2 * count * model + (count + model) * width)
        ),
        name="qkv_forward",
    )(inputs, vectors, weight)


def mlp_kernel(
    ends, mixed_ref, x_ref, cot_ref, vectors, w_out, w_up, w_down,
    hidden_ref, normed_ref, act_ref, up_grad_ref, down_grad_ref, proj_grad_ref, hidden_grad_ref,
    mixed_grad_ref, sum_gain, sum_shift, sum_up, sum_out, sum_down, *, row, sub, chunk
):
    first_step(sum_gain, sum_shift, sum_up, sum_out, sum_down)
    tile, model = x_ref.shape
    wide = w_up.shape[1]
    b_out, gain, shift = (vectors[k : k + 1, :model] for k in (3, 4, 5))
    step = pl.program_id(0)
    steps = row // tile
    last_end = ends[step // steps, ends.shape[1] - 1]
    units = [(start, at) for start in range(0, tile, sub) for at in range(0, wide, chunk)]
    normed, units_two, roots, totals = {}, {}, {}, {}

    def begin(start):
        rows = slice(start, start + sub)
        hidden = x_ref[rows, :].astype(F32) + mult(mixed_ref[rows, :], w_out[...]) + b_out
        hidden_ref[rows, :] = hidden
        units_two[start], roots[start] = normalize(hidden)
        normed[start] = (units_two[start] * gain + shift).astype(BF16)
        normed_ref[rows, :] = normed[start]
        place = lax.broadcasted_iota(jnp.int32, (sub, 1), 0) + (step % steps * tile + start)
        down_grad = jnp.where(place < last_end, cot_ref[rows, :], jnp.zeros((), BF16))
        down_grad_ref[rows, :] = down_grad
        sum_down[...] += column_sum(down_grad.astype(F32))

    def products(start, at):
        if start not in normed:
            begin(start)
        cols = slice(at, at + chunk)
        return (
            mult(normed[start], w_up[:, cols]) + vectors[6:7, cols],
            back_mult(down_grad_ref[start : start + sub, :], w_down[cols, :]),
        )

    def finish(start):
        rows = slice(start, start + sub)
        normed_grad = totals[start]
        sum_gain[...] += column_sum(normed_grad * units_two[start])
        sum_shift[...] += column_sum(normed_grad)
        hidden_grad = norm_back(units_two[start], roots[start], normed_grad, gain)
        hidden_grad = down_grad_ref[rows, :].astype(F32) + hidden_grad
        hidden_grad_ref[rows, :] = hidden_grad
        proj_grad = hidden_grad.astype(BF16)
        proj_grad_ref[rows, :] = proj_grad
        sum_out[...] += column_sum(proj_grad.astype(F32))
        mixed_grad_ref[rows, :] = back_mult(proj_grad, w_out[...]).astype(BF16)

    ready = products(*units[0])
    waiting = None
    for index, (start, at) in enumerate(units):
        u, act_grad = ready
        if index + 1 < len(units):
            ready = products(*units[index + 1])
        rows, cols = slice(start, start + sub), slice(at, at + chunk)
        square = u * u
        smooth = jnp.tanh(u * (GELU + (GELU * 0.044715) * square))
        part = 0.5 * smooth
        share = 0.5 + part
        act_ref[rows, cols] = (u * share).astype(BF16)
        slope = share + (u * (0.5 - part * smooth)) * (GELU + (3 * GELU * 0.044715) * square)
        up_grad = (slope * act_grad).astype(BF16)
        up_grad_ref[rows, cols] = up_grad
        sum_up[:, cols] += column_sum(up_grad.astype(F32))
        grad = back_mult(up_grad, w_up[:, cols])
        totals[start] = grad if start not in totals else totals[start] + grad
        if waiting is not None:
            finish(waiting)
            waiting = None
        if at + chunk == wide:
            waiting = start
    finish(waiting)


def mlp(ends, mixed, x, cot, vectors, w_out, w_up, w_down, row, tile=512, sub=512, chunk=768):
    count, model = x.shape
    wide = w_up.shape[1]
    consts = (vectors, w_out, w_up, w_down)
    widths = [(model, F32), (model, BF16), (wide, BF16), (wide, BF16), (model, BF16)]
    widths += [(model, BF16), (model, F32), (model, BF16)]
    sums = [model, model, wide, model, model]
    return pl.pallas_call(
        functools.partial(mlp_kernel, row=row, sub=sub, chunk=chunk),
        grid=(count // tile,),
        in_specs=[pl.BlockSpec(memory_space=pltpu.SMEM)]
        + [token_rows(tile, model)] * 3
        + [whole(item) for item in consts],
        out_specs=[token_rows(tile, width) for width, _ in widths]
        + [vector_out(width) for width in sums],
        out_shape=[shape(count, width, kind=kind) for width, kind in widths]
        + [shape(1, width, kind=F32) for width in sums],
        compiler_params=kernel_limits(),
        cost_estimate=cost(
            2 * count * model * (3 * wide + 2 * model), count * (26 * model + 4 * wide), count * wide
        ),
        name="mlp",
    )(ends, mixed, x, cot, *consts)


def mlp_out_kernel(hidden_ref, act_ref, vectors, w_down, out_ref):
    model = hidden_ref.shape[1]
    out = hidden_ref[...] + mult(act_ref[...], w_down[...]) + vectors[7:8, :model]
    out_ref[...] = out.astype(BF16)


def mlp_out(hidden, act, vectors, w_down, tile=256):
    count, model = hidden.shape
    wide = act.shape[1]
    return pl.pallas_call(
        mlp_out_kernel,
        grid=(count // tile,),
        in_specs=[token_rows(tile, model), token_rows(tile, wide), whole(vectors), whole(w_down)],
        out_specs=token_rows(tile, model),
        out_shape=shape(count, model),
        compiler_params=kernel_limits(),
        cost_estimate=cost(2 * count * model * wide, count * (6 * model + 2 * wide)),
        name="mlp_out",
    )(hidden, act, vectors, w_down)


def whole_grad_kernel(left_ref, right_ref, out_ref):
    out_ref[...] = cross_rows(left_ref[...], right_ref[...]).astype(out_ref.dtype)


def whole_grad(left, right, kind, name, tile=768):
    count, high = left.shape
    wide = right.shape[1]
    tile = min(tile, high)
    return pl.pallas_call(
        whole_grad_kernel,
        grid=(high // tile,),
        in_specs=[
            pl.BlockSpec((count, tile), lambda i: (0, i)),
            pl.BlockSpec((count, wide), lambda i: (0, 0), pipeline_mode=ONCE),
        ],
        out_specs=pl.BlockSpec((tile, wide), lambda i: (i, 0)),
        out_shape=shape(high, wide, kind=kind),
        compiler_params=kernel_limits(),
        cost_estimate=cost(
            2 * count * high * wide, 2 * (count * high + count * wide + 2 * high * wide)
        ),
        name=name,
    )(left, right)


def weight_grad_kernel(core_ref, left_ref, right_ref, keep, send, *, group):
    width = right_ref.shape[1]
    step_by = math.gcd(width, 2 * LANES)

    def product(start):
        return cross_rows(left_ref[...], right_ref[:, start : start + step_by])

    ready = product(0)
    for start in range(0, width, step_by):
        grad = ready
        if start + step_by < width:
            ready = product(start + step_by)
        store_halves(core_ref, grad, group, keep, send, slice(start, start + step_by))


def qkv_grads_kernel(
    core_ref, normed, grad_ref, sum_ref, weight, vectors, *refs, steps, group
):
    pairs, (sum_gain, sum_shift, by_grad, by_sum) = refs[: 2 * steps], refs[2 * steps :]
    step = pl.program_id(0)
    first_step(by_grad, by_sum)
    width = grad_ref.shape[1]
    step_by = math.gcd(width, 2 * LANES)

    def product(start):
        return cross_rows(normed[...], grad_ref[:, start : start + step_by])

    def tile(keep, send):
        ready = product(0)
        for start in range(0, width, step_by):
            grad = ready
            if start + step_by < width:
                ready = product(start + step_by)
            cols = slice(start, start + step_by)
            store_halves(core_ref, grad, group, keep, send, cols)
            for at in range(start, start + step_by, LANES):
                part = weight[:, at : at + LANES].astype(F32)
                by_grad[...] += part * grad[:, at - start : at - start + LANES]
                by_sum[...] += part * sum_ref[:, at : at + LANES]

    for index in range(steps):

        @pl.when(step == index)
        def _():
            tile(*pairs[2 * index : 2 * index + 2])

    @pl.when(step == steps - 1)
    def _():
        model = normed.shape[1]
        shift = column_sum(by_sum[...].T)
        sum_shift[...] = shift
        total = column_sum(by_grad[...].T)
        sum_gain[...] = (total - vectors[1:2, :model] * shift) / vectors[0:1, :model]


def qkv_grads(core, group, normed, grad, sums, weight, vectors, tile=768):
    count, model = normed.shape
    width = grad.shape[1]
    tile = min(tile, width)
    steps = width // tile
    return pl.pallas_call(
        functools.partial(qkv_grads_kernel, steps=steps, group=group),
        grid=(steps,),
        in_specs=[
            pl.BlockSpec(memory_space=pltpu.SMEM),
            whole(normed),
            pl.BlockSpec((count, tile), lambda i: (0, i)),
            pl.BlockSpec((1, tile), lambda i: (0, i)),
            pl.BlockSpec((model, tile), lambda i: (0, i)),
            whole(vectors),
        ],
        out_specs=[pl.BlockSpec((model // 2, tile), lambda i: (0, 0))] * (2 * steps)
        + [vector_out(model)] * 2,
        out_shape=[shape(model // 2, tile)] * (2 * steps) + [shape(1, model, kind=F32)] * 2,
        scratch_shapes=[pltpu.VMEM((model, LANES), F32)] * 2,
        compiler_params=kernel_limits(),
        cost_estimate=cost(
            2 * count * model * width, 2 * (count * model + count * width + 2 * model * width)
        ),
        name="qkv_grads",
    )(core, normed, grad, sums, weight, vectors)


def store_halves(core_ref, grad, group, keep, send, cols):
    first, second = [
        jnp.concatenate(
            [grad[k : k + group] for k in range(which * group, grad.shape[0], 2 * group)], axis=0
        )
        for which in range(2)
    ]
    swapped = core_ref[0] == 1
    keep[:, cols] = jnp.where(swapped, second, first).astype(BF16)
    send[:, cols] = jnp.where(swapped, first, second).astype(BF16)


def weight_grad(core, group, left, right, name, tile=768):
    count, high = left.shape
    wide = right.shape[1]
    tile = min(tile, wide)
    return pl.pallas_call(
        functools.partial(weight_grad_kernel, group=group),
        grid=(wide // tile,),
        in_specs=[
            pl.BlockSpec(memory_space=pltpu.SMEM),
            pl.BlockSpec((count, high), lambda i: (0, 0), pipeline_mode=ONCE),
            pl.BlockSpec((count, tile), lambda i: (0, i)),
        ],
        out_specs=[pl.BlockSpec((high // 2, tile), lambda i: (0, i))] * 2,
        out_shape=[shape(high // 2, wide)] * 2,
        compiler_params=kernel_limits(),
        cost_estimate=cost(
            2 * count * high * wide, 2 * (count * high + count * wide + high * wide)
        ),
        name=name,
    )(core, left, right)


def qkv_backward_kernel(
    grad_ref, x_ref, hidden_grad_ref, vectors, weight, out_ref, *, sub
):
    count, model = x_ref.shape
    gain = vectors[0:1, :model]

    def lower(start):
        return back_mult(grad_ref[start : start + sub, :], weight[...])

    ready = lower(0)
    for start in range(0, count, sub):
        normed_grad = ready
        if start + sub < count:
            ready = lower(start + sub)
        rows = slice(start, start + sub)
        unit, root = normalize(x_ref[rows, :].astype(F32))
        inner = norm_back(unit, root, normed_grad, gain)
        out_ref[rows, :] = (hidden_grad_ref[rows, :] + inner).astype(BF16)


def qkv_backward(grad, x, hidden_grad, vectors, weight, tile=512, sub=256):
    count, model = x.shape
    width = weight.shape[1]
    return pl.pallas_call(
        functools.partial(qkv_backward_kernel, sub=sub),
        grid=(count // tile,),
        in_specs=[token_rows(tile, width)]
        + [token_rows(tile, model)] * 2
        + [whole(vectors), whole(weight)],
        out_specs=token_rows(tile, model),
        out_shape=shape(count, model),
        compiler_params=kernel_limits(),
        cost_estimate=cost(
            2 * count * model * width, 2 * (4 * count * model + (count + model) * width)
        ),
        name="qkv_backward",
    )(grad, x, hidden_grad, vectors, weight)


def segments(ends, index, shape, axis):
    place = lax.broadcasted_iota(jnp.int32, shape, axis)
    found = jnp.zeros(shape, jnp.int32)
    for slot in range(ends.shape[1]):
        found = found + (ends[index, slot] <= place).astype(jnp.int32)
    return found


def allowed_bias(ends, row):
    index = pl.program_id(0)
    keys = lax.broadcasted_iota(jnp.int32, (row, row), 0)
    queries = lax.broadcasted_iota(jnp.int32, (row, row), 1)
    same = segments(ends, index, (row, 1), 0) == segments(ends, index, (1, row), 1)
    return jnp.where(same & (keys <= queries), 0.0, HIDE)


def pair_lanes(pair):
    return slice(pair * PAIR, (pair + 1) * PAIR)


def head_rows(head):
    return slice(head * HEAD, (head + 1) * HEAD)


def own_lanes(values, head):
    lane = lax.broadcasted_iota(jnp.int32, (1, PAIR), 1)
    return jnp.where((lane < HEAD) == (head == 0), values, jnp.zeros((), BF16))


def key_blocks(half, part, step):
    for start in range(0, (part + 1) * half, step):
        low = max(0, (start - part * half) // LANES * LANES) if start >= part * half else 0
        yield start, low


def widen(values, low, fill):
    if low == 0:
        return values
    pad = jnp.full((values.shape[0], low), fill, values.dtype)
    return jnp.concatenate([pad, values], axis=1)


def folded(values, combine):
    return combine(values.reshape(values.shape[0] // 8, 8, values.shape[1]), axis=0)


def unit_list(pairs):
    return [(pair, part, head) for pair in range(pairs) for part in range(2) for head in range(2)]


def forward_kernel(
    ends, q_ref, k_ref, v_ref, mixed_ref, total_ref, bias, *, pairs, step, lead
):
    row = q_ref.shape[0]
    half = row // 2
    bias[...] = allowed_bias(ends, row)

    def scores_of(pair, part, head):
        seen = (part + 1) * half
        queries = q_ref[part * half : seen, pair_lanes(pair)] * jnp.asarray(SCALE, BF16)
        return back_mult(k_ref[:seen, pair_lanes(pair)], own_lanes(queries, head))

    def weigh(part, scores):
        base = part * half
        top = jnp.full((8, half), HIDE, F32)
        shown = []
        for start, low in key_blocks(half, part, step):
            block = scores[start : start + step, low:]
            square = block * block + 1.0
            mag = square * (lax.rsqrt(square) * LOG2E)
            mag = mag + bias[start : start + step, base + low : base + half]
            shown.append(mag)
            top = jnp.maximum(top, widen(folded(mag, jnp.max), low, HIDE))
        top = jnp.max(top, axis=0, keepdims=True)
        total = jnp.zeros((8, half), F32)
        signed = []
        for (start, low), mag in zip(key_blocks(half, part, step), shown):
            weight = jnp.exp2(mag - top[:, low:])
            total = total + widen(folded(weight, jnp.sum), low, 0.0)
            block = jnp.tanh(scores[start : start + step, low:]) * weight
            signed.append(widen(block.astype(BF16), low, 0.0))
        return jnp.concatenate(signed, axis=0), top, jnp.sum(total, axis=0, keepdims=True)

    units = unit_list(pairs)
    scores = [scores_of(*unit) for unit in units[:lead]]
    turned, parts = {}, {}

    def finish(unit, signed, top, total):
        pair, part, head = unit
        here = slice(part * half, (part + 1) * half)
        total_ref[0, pair, head : head + 1, here] = top * (1.0 / LOG2E) + jnp.log(total)
        values = turned[pair][head_rows(head), : (part + 1) * half]
        parts[unit] = mult(values, signed) * (1.0 / total)
        if head == 1:
            both = jnp.concatenate([parts[pair, part, 0], parts[unit]], axis=0)
            mixed_ref[here, pair_lanes(pair)] = both.T.astype(BF16)

    waiting = None
    for index, unit in enumerate(units):
        if index + lead < len(units):
            scores.append(scores_of(*units[index + lead]))
        if unit[0] not in turned:
            turned[unit[0]] = v_ref[:, pair_lanes(unit[0])].T
        weighed = weigh(unit[1], scores[index])
        if waiting is not None:
            finish(*waiting)
        waiting = (unit,) + weighed
    finish(*waiting)


def attention_forward(ends, merged, row):
    count, width = merged.shape
    model = width // 3
    pairs = model // PAIR
    micro = count // row
    area = micro * pairs * 2 * row * row

    def third(index):
        return pl.BlockSpec((row, model), lambda r: (r, index))

    return pl.pallas_call(
        functools.partial(forward_kernel, pairs=pairs, step=32, lead=2),
        grid=(micro,),
        in_specs=[
            pl.BlockSpec(memory_space=pltpu.SMEM),
            third(0),
            third(1),
            third(2),
        ],
        out_specs=[
            pl.BlockSpec((row, model), lambda r: (r, 0)),
            pl.BlockSpec((1, pairs, 2, row), lambda r: (r, 0, 0, 0)),
        ],
        out_shape=[shape(count, model), shape(micro, pairs, 2, row, kind=F32)],
        scratch_shapes=[pltpu.VMEM((row, row), F32)],
        compiler_params=kernel_limits(),
        cost_estimate=cost(area * 4 * HEAD * 5, count * width * 3, area * 3),
        name="attention_forward",
    )(ends, merged, merged, merged)


def backward_kernel(
    ends, q_ref, k_ref, v_ref, mixed_ref, grad_ref, total_ref,
    out_ref, sum_ref, bias, *, pairs, step, lead, lag
):
    row = q_ref.shape[0]
    half = row // 2
    model = pairs * PAIR
    first_step(sum_ref)
    bias[...] = allowed_bias(ends, row)

    def put(section, pair, rows, values):
        cols = slice(section * model + pair * PAIR, section * model + (pair + 1) * PAIR)
        values = values.astype(BF16)
        out_ref[rows, cols] = values
        sum_ref[:, cols] += column_sum(values.astype(F32))

    def queries_and_grads(pair, part, head):
        here = slice(part * half, (part + 1) * half)
        queries = q_ref[here, pair_lanes(pair)] * jnp.asarray(SCALE, BF16)
        return own_lanes(queries, head), own_lanes(grad_ref[here, pair_lanes(pair)], head)

    def products(pair, part, head):
        seen = (part + 1) * half
        queries, grads = queries_and_grads(pair, part, head)
        return (
            back_mult(k_ref[:seen, pair_lanes(pair)], queries),
            back_mult(v_ref[:seen, pair_lanes(pair)], grads),
        )

    centres, turned, sums, query_parts = {}, {}, {}, {}

    def weigh(pair, part, head, scores, weight_grads):
        base = part * half
        here = slice(base, base + half)
        if (pair, part) not in centres:
            grads = grad_ref[here, pair_lanes(pair)].astype(F32)
            centres[pair, part] = (grads * mixed_ref[here, pair_lanes(pair)].astype(F32)).T
        centre = column_sum(centres[pair, part][head_rows(head)])
        total = total_ref[0, pair, head : head + 1, here] * LOG2E
        signed, score_grads = [], []
        for start, low in key_blocks(half, part, step):
            block = scores[start : start + step, low:]
            weight_grad = weight_grads[start : start + step, low:]
            square = block * block + 1.0
            root = lax.rsqrt(square)
            shift = bias[start : start + step, base + low : base + half] - total[:, low:]
            weight = jnp.exp2(square * (root * LOG2E) + shift)
            smooth = jnp.tanh(block)
            bent = weight_grad * smooth
            score_grad = weight * (
                (weight_grad - bent * smooth) + (block * root) * (bent - centre[:, low:])
            )
            signed.append(widen((smooth * weight).astype(BF16), low, 0.0))
            score_grads.append(widen(score_grad.astype(BF16), low, 0.0))
        return jnp.concatenate(signed, axis=0), jnp.concatenate(score_grads, axis=0)

    def finish(unit, signed, score_grads):
        pair, part, head = unit
        queries, grads = queries_and_grads(*unit)
        for section, grad in ((2, mult(signed, grads)), (1, mult(score_grads, queries))):
            for block in range(part + 1):
                add = grad[block * half : (block + 1) * half]
                key = (pair, section, block)
                sums[key] = add if key not in sums else sums[key] + add
        if pair not in turned:
            turned[pair] = k_ref[:, pair_lanes(pair)].T
        keys = turned[pair][head_rows(head), : (part + 1) * half]
        query_parts[unit] = mult(keys, score_grads)
        if head == 1:
            both = jnp.concatenate([query_parts[pair, part, 0], query_parts[unit]], axis=0)
            put(0, pair, slice(part * half, (part + 1) * half), both.T * SCALE)
        if head == 1 and part == 1:
            for section in (1, 2):
                for block in range(2):
                    rows = slice(block * half, (block + 1) * half)
                    put(section, pair, rows, sums[pair, section, block])

    units = unit_list(pairs)
    ready = [products(*unit) for unit in units[:lead]]
    waiting = []
    for index, unit in enumerate(units):
        if index + lead < len(units):
            ready.append(products(*units[index + lead]))
        waiting.append((unit,) + weigh(*unit, *ready[index]))
        ready[index] = None
        if len(waiting) > lag:
            finish(*waiting.pop(0))
    for item in waiting:
        finish(*item)


def attention_backward(ends, merged, mixed, mixed_grad, total, row):
    count, width = merged.shape
    model = width // 3
    pairs = model // PAIR
    micro = count // row
    area = micro * pairs * 2 * row * row

    def third(index):
        return pl.BlockSpec((row, model), lambda r: (r, index))

    return pl.pallas_call(
        functools.partial(backward_kernel, pairs=pairs, step=32, lead=1, lag=0),
        grid=(micro,),
        in_specs=[
            pl.BlockSpec(memory_space=pltpu.SMEM),
            third(0),
            third(1),
            third(2),
            third(0),
            third(0),
            pl.BlockSpec((1, pairs, 2, row), lambda r: (r, 0, 0, 0)),
        ],
        out_specs=[pl.BlockSpec((row, width), lambda r: (r, 0)), vector_out(width)],
        out_shape=[shape(count, width), shape(1, width, kind=F32)],
        scratch_shapes=[pltpu.VMEM((row, row), F32)],
        compiler_params=kernel_limits(),
        cost_estimate=cost(area * 10 * HEAD * 4, count * width * 5, area * 3),
        name="attention_backward",
    )(ends, merged, merged, merged, mixed, mixed_grad, total)


def vector_slots(lengths):
    slots, fill = [], []
    for length in lengths:
        row = next((r for r, used in enumerate(fill) if used + length <= LANES), len(fill))
        if row == len(fill):
            fill.append(0)
        slots.append((row, fill[row], length))
        fill[row] += length
    return slots, len(fill)


def lane_of(devices, length, first):
    size = devices * length
    place = lax.broadcasted_iota(jnp.int32, (LANES, size), 1).astype(F32)
    inside = place - length * jnp.floor((place + 0.5) * (1.0 / length))
    lane = lax.broadcasted_iota(jnp.int32, (LANES, size), 0).astype(F32)
    return (lane == inside + first).astype(BF16)


def owner_of(devices, length):
    size = devices * length
    place = lax.broadcasted_iota(jnp.int32, (devices, size), 1)
    start = lax.broadcasted_iota(jnp.int32, (devices, size), 0) * length
    return (place >= start) & (place < start + length)


def vectors_from_table(table, slots):
    devices = table.shape[1]
    longest = devices * max(length for _, _, length in slots)

    def kernel(table_ref, out):
        for index, (row, first, length) in enumerate(slots):
            spread = mult(table_ref[row], lane_of(devices, length, first))
            out[index : index + 1, : devices * length] = column_sum(
                jnp.where(owner_of(devices, length), spread, 0.0)
            )

    return pl.pallas_call(
        kernel,
        out_shape=shape(len(slots), longest, kind=F32),
        compiler_params=kernel_limits(40),
        name="vectors_from_table",
    )(table)


def split(values, size):
    quotient = jnp.floor((values + 0.5) * (1.0 / size))
    return quotient, values - size * quotient


def table_from_vectors(vectors, slots, rows, devices, inner, core):
    def kernel(core_ref, *refs):
        vector_refs, outs = refs[:-2], refs[-2:]
        filled = [jnp.zeros((devices, LANES), F32) for _ in range(rows)]
        for (row, first, length), ref in zip(slots, vector_refs):
            own = jnp.where(owner_of(devices, length), ref[...], 0.0).astype(BF16)
            filled[row] = filled[row] + back_mult(own, lane_of(devices, length, first))
        stacked = jnp.concatenate(filled, axis=0).astype(BF16)
        target = lax.broadcasted_iota(jnp.int32, (devices // 2 * rows, devices * rows), 0)
        target = target.astype(F32)
        source = lax.broadcasted_iota(jnp.int32, (devices // 2 * rows, devices * rows), 1)
        source = source.astype(F32)
        block, row = split(target, rows)
        chip, y = split(block, inner)
        match = [
            source == row * devices + (chip * 2 + which) * inner + y for which in range(2)
        ]
        halves = [mult(one.astype(BF16), stacked).astype(BF16) for one in match]
        for which in range(2):

            @pl.when(core_ref[0] == which)
            def _():
                outs[0][...] = halves[which]
                outs[1][...] = halves[1 - which]

    return pl.pallas_call(
        kernel,
        in_specs=[pl.BlockSpec(memory_space=pltpu.SMEM)]
        + [pl.BlockSpec(memory_space=pltpu.VMEM)] * len(vectors),
        out_shape=[shape(devices // 2 * rows, LANES)] * 2,
        compiler_params=kernel_limits(40),
        name="table_from_vectors",
    )(core, *vectors)


class Links:
    def __init__(self, mesh):
        self.outer = mesh.shape["dp"]
        self.inner = mesh.shape["fsdp"]
        self.count = self.outer * self.inner
        self.far = [(k << 2) * self.inner for k in range(self.outer // 4)]
        self.near = [(b << 1) * self.inner + f for b in range(2) for f in range(self.inner)]
        self.core = self.inner

    def place(self):
        return lax.axis_index("dp") * self.inner + lax.axis_index("fsdp")

    def swap(self, piece, mask):
        return lax.ppermute(piece, AXES, [(i, i ^ mask) for i in range(self.count)])

    def far_step(self, shard):
        got = [self.swap(shard, mask) for mask in self.far[1:]]
        return lambda *others: jnp.stack([shard] + gate(got, *others))

    def far_doubled(self, shard):
        column = shard[None]
        while column.shape[0] < len(self.far):
            column = jnp.concatenate([column, self.swap(column, self.far[column.shape[0]])])
        return column

    def near_step(self, column):
        return [column] + [self.swap(column, mask) for mask in self.near[1:]]

    def near_halves(self, column):
        if len(self.near) != 4:
            plane = self.near_step(column)
            return plane, lambda *others: gate(plane, *others)
        side, inner = [self.swap(column, mask) for mask in (self.near[2], self.near[1])]
        plane = [column, inner, side]
        width = half_columns(column)

        def second(*others):
            left, right = gate((inner[:, :, :width], side[:, :, width:]), *others)
            return plane + [self.swap(left, self.near[2]), self.swap(right, self.near[1])]

        return plane, second

    def core_step(self, plane):
        return plane + [self.swap(piece, self.core) for piece in plane]

    def arrange(self, pieces, columns):
        far = self.far
        held = len(pieces)
        masks, ranges = list(self.near), [(0, pieces[0].shape[2])] * len(self.near)
        if held > 2 * len(masks):
            half = half_columns(pieces[0])
            masks, ranges = masks + masks[-1:], ranges[:-1] + [(0, half), (half, ranges[0][1])]
        masks, ranges = masks + [mask ^ self.core for mask in masks], ranges * 2
        rows = pieces[0].shape[1]

        def kernel(me_ref, *refs):
            targets, sem = refs[held:-1], refs[-1]
            me = me_ref[0]
            copies = []
            for piece, mask, (low, high) in zip(refs[:held], masks, ranges):
                for k, step in enumerate(far):
                    owner = jnp.bitwise_xor(me, mask ^ step)
                    for target, (start, width, parts) in zip(targets, columns):
                        for part in range(parts):
                            base = start + part * width
                            one, two = max(low, base), min(high, base + width)
                            if one >= two:
                                continue
                            copies.append(
                                pltpu.make_async_copy(
                                    piece.at[k, :, pl.ds(one - low, two - one)],
                                    target.at[owner * parts + part, :, pl.ds(one - base, two - one)],
                                    sem,
                                )
                            )
            for copy in copies:
                copy.start()
            for copy in copies:
                copy.wait()

        return pl.pallas_call(
            kernel,
            in_specs=[pl.BlockSpec(memory_space=pltpu.SMEM)]
            + [pl.BlockSpec(memory_space=pl.ANY)] * held,
            out_specs=[pl.BlockSpec(memory_space=pltpu.VMEM)] * len(columns),
            out_shape=[
                jax.ShapeDtypeStruct((self.count * parts, rows, width), BF16)
                for _, width, parts in columns
            ],
            scratch_shapes=[pltpu.SemaphoreType.DMA],
            compiler_params=pltpu.CompilerParams(vmem_limit_bytes=40 * 2**20),
            name="arrange",
        )(jnp.full((1,), self.place(), jnp.int32), *pieces)

    def position(self):
        dp = lax.axis_index("dp")
        return dp >> 2, (dp >> 1) & 1, dp & 1, lax.axis_index("fsdp")

    def core_swap(self, pair):
        return pair[0], self.swap(pair[1], self.core)

    def core_sums(self, pairs, join):
        _, side, _, inner = self.position()

        def view(array):
            rows = array.shape[0] * 2 // self.count
            return array.reshape(self.outer // 4, 2, self.inner, rows, array.shape[1])

        mine = [view(keep) for keep, _ in pairs]
        got = [view(received) for _, received in pairs]

        def finish(*others):
            received = gate(got, *others) if others else got
            sums = []
            for b in range(2):
                for f in range(self.inner):

                    def cut(array):
                        return pick(pick(array, side ^ b, 1), inner ^ f, 1).astype(F32)

                    sums.append(
                        join([(cut(a) + cut(b)).astype(BF16) for a, b in zip(mine, received)])
                    )
            return sums

        return finish

    def near_swaps(self, sums):
        return sums[:1] + [self.swap(part, mask) for part, mask in zip(sums[1:], self.near[1:])]

    def near_sums(self, sums):
        return self.far_parts(self.near_swaps(sums))

    def far_parts(self, got):
        column = self.position()[0]

        def finish(*others):
            received = gate(got, *others)
            parts = []
            for k in range(len(self.far)):
                part = sum(pick(array, column ^ k, 0).astype(F32) for array in received)
                parts.append(part if k == 0 else part.astype(BF16))
            return parts

        return finish

    def far_sums(self, parts):
        got = [self.swap(part, mask) for part, mask in zip(parts[1:], self.far[1:])]

        def finish(*others):
            received = gate(got, *others)
            return functools.reduce(lambda sum, part: sum + part.astype(F32), received, parts[0])

        return got, finish


def far_start(links, sums):
    column = links.position()[0]

    def part(k):
        return sum(pick(array, column ^ k, 0).astype(F32) for array in sums)

    if len(links.far) != 4:
        parts = [part(k) for k in range(len(links.far))]
        return (), lambda *others: (
            gate(parts[0], *others),
            {k: parts[k].astype(BF16) for k in range(1, len(parts))},
        )
    got = links.swap(jnp.stack([part(2), part(3)]).astype(BF16), links.far[2])

    def second(*others):
        received = gate(got, *others).astype(F32)
        return part(0) + received[0], {1: (part(1) + received[1]).astype(BF16)}

    return got, second


def far_join(links, blocks):
    got = {}
    for k in range(1, len(links.far)):
        sent = [(index, parts[k]) for index, (_, parts) in enumerate(blocks) if k in parts]
        arrived = links.swap(jnp.concatenate([part for _, part in sent], axis=1), links.far[k])
        at = 0
        for index, part in sent:
            got.setdefault(index, []).append((arrived, at, part.shape[1]))
            at += part.shape[1]

    def finish(*others):
        results = []
        for index, (own, _) in enumerate(blocks):
            arrays = gate([arrived for arrived, _, _ in got[index]], *others)
            for array, (_, at, width) in zip(arrays, got[index]):
                own = own + array[:, at : at + width].astype(F32)
            results.append(own)
        return results

    return finish


def half_columns(array):
    return array.shape[2] // 2 // LANES * LANES


def pick(array, index, axis):
    return lax.dynamic_index_in_dim(array, index, axis, keepdims=False)


def run(
    links,
    tokens,
    lengths,
    cotangent,
    attn_norm_gain,
    attn_norm_bias,
    qkv_weight,
    qkv_bias,
    out_weight,
    out_bias,
    mlp_norm_gain,
    mlp_norm_bias,
    up_weight,
    up_bias,
    down_weight,
    down_bias,
):
    micro, row, model = tokens.shape
    count = micro * row
    shard = qkv_weight.shape[0]
    wide = up_weight.shape[1]
    devices = links.count

    vectors = (
        attn_norm_gain,
        attn_norm_bias,
        qkv_bias,
        out_bias,
        mlp_norm_gain,
        mlp_norm_bias,
        up_bias,
        down_bias,
    )
    slots, table_rows = vector_slots([vector.shape[0] for vector in vectors])
    lines = []
    for line in range(table_rows):
        held = [v for v, slot in zip(vectors, slots) if slot[0] == line]
        held = jnp.concatenate(held)
        lines.append(jnp.pad(held, (0, LANES - held.shape[0])))
    extra = jnp.pad(jnp.stack(lines), ((0, shard - table_rows), (0, 0)))
    qkv_far = links.far_step(jnp.concatenate([qkv_weight, extra], axis=1))
    middle_in = jnp.concatenate([out_weight, up_weight], axis=1)
    middle_column = links.far_doubled(middle_in)
    qkv_column = qkv_far()
    qkv_plane = links.near_step(qkv_column)
    w_down = lax.all_gather(down_weight, AXES, axis=0, tiled=True)
    middle_start, middle_corner = links.near_halves(gate(middle_column, qkv_plane))
    w_qkv, extra = links.arrange(
        links.core_step(qkv_plane), [(0, 3 * model, 1), (3 * model, LANES, 1)]
    )
    w_qkv = w_qkv.reshape(model, 3 * model)
    table = vectors_from_table(extra[:, :table_rows].swapaxes(0, 1), slots)

    ends = jnp.cumsum(lengths.reshape(micro, -1), axis=1, dtype=jnp.int32)
    inputs = tokens.reshape(count, model)
    normed_one, merged = qkv_forward(inputs, table, w_qkv)
    middle_plane = middle_corner(merged)
    mixed, log_total = attention_forward(ends, gate(merged, middle_start), row)
    middle_pieces = links.core_step(middle_plane[:3] + gate(middle_plane[3:], mixed))
    w_out, w_up = links.arrange(gate(middle_pieces, mixed), [(0, model, 1), (model, wide, 1)])
    w_out = w_out.reshape(model, model)
    w_up = w_up.reshape(model, wide)
    (
        hidden,
        normed_two,
        activated,
        up_grad,
        down_grad,
        proj_grad,
        hidden_grad,
        mixed_grad,
        sum_gain_two,
        sum_shift_two,
        sum_up,
        sum_out,
        sum_down,
    ) = mlp(
        ends, mixed, inputs, cotangent.reshape(count, model), table, w_out, w_up, w_down, row
    )

    core = jnp.full((1,), links.position()[2], jnp.int32)
    group = links.inner * shard
    grad_up = weight_grad(core, group, normed_two, up_grad, "grad_up")
    grad_up = links.core_swap(grad_up)
    grad_down = whole_grad(activated, gate(down_grad, grad_up[0]), BF16, "grad_down")
    down_block = lax.psum_scatter(grad_down, AXES, scatter_dimension=0, tiled=True)
    grad_out = weight_grad(core, group, mixed, gate(proj_grad, grad_down), "grad_out")
    early = links.core_sums(
        [links.core_swap(grad_out), grad_up], lambda cuts: jnp.concatenate(cuts, axis=2)
    )(grad_out[0])
    early_near = links.near_swaps(early)
    qkv_grad, sum_qkv = attention_backward(
        ends, merged, mixed, gate(mixed_grad, early), log_total, row
    )
    early_near = gate(early_near, qkv_grad)
    early_first, early_second = far_start(links, early_near)
    *grad_qkv, sum_gain_one, sum_shift_one = qkv_grads(
        core, group, normed_one, gate(qkv_grad, early_near), sum_qkv, w_qkv, table
    )
    sums = (
        sum_gain_one,
        sum_shift_one,
        sum_qkv,
        sum_out,
        sum_gain_two,
        sum_shift_two,
        sum_up,
        sum_down,
    )
    small = table_from_vectors(sums, slots, table_rows, devices, links.inner, core)

    def side_by_side(cuts):
        lines = jnp.pad(cuts[-1], ((0, 0), (0, shard - table_rows), (0, 0)))
        return jnp.concatenate([*cuts[:-1], lines], axis=2)

    late = [links.core_swap(pair) for pair in zip(grad_qkv[::2], grad_qkv[1::2])]
    late = links.core_sums([*late, links.core_swap(small)], side_by_side)()
    late_parts = links.near_sums(late)
    block_out = mlp_out(hidden, gate(activated, late), table, w_down)
    early_own, early_sent = early_second(block_out)
    late_parts = late_parts(block_out)
    late_sent = {k: late_parts[k] for k in range(1, len(late_parts))}
    last = far_join(links, [(early_own, early_sent), (late_parts[0], late_sent)])
    token_grad = qkv_backward(
        gate(qkv_grad, late_parts, early_sent, block_out),
        inputs,
        hidden_grad,
        table,
        w_qkv,
    )
    early_block, late_block = last(token_grad)
    down_block = gate(down_block, token_grad).astype(F32)
    (
        gain_one_shard,
        bias_one_shard,
        bias_qkv_shard,
        bias_out_shard,
        gain_two_shard,
        bias_two_shard,
        bias_up_shard,
        bias_down_shard,
    ) = [
        late_block[line, 3 * model + start : 3 * model + start + length]
        for line, start, length in slots
    ]
    return (
        block_out.reshape(tokens.shape),
        token_grad.reshape(tokens.shape),
        gain_one_shard,
        bias_one_shard,
        late_block[:, : 3 * model],
        bias_qkv_shard,
        early_block[:, :model],
        bias_out_shard,
        gain_two_shard,
        bias_two_shard,
        early_block[:, model:],
        bias_up_shard,
        down_block,
        bias_down_shard,
    )


def solution(mesh):
    links = Links(mesh)
    rows = P(None, AXES, None)
    vector = P(AXES)
    matrix = P(AXES, None)
    params = (
        vector,
        vector,
        matrix,
        vector,
        matrix,
        vector,
        vector,
        vector,
        matrix,
        vector,
        matrix,
        vector,
    )
    return jax.shard_map(
        lambda *args: run(links, *args),
        mesh=mesh,
        in_specs=(rows, rows, rows) + params,
        out_specs=(rows, rows) + params,
        check_vma=False,
    )
```

```python
import functools
import math

import jax
import jax.numpy as jnp
from jax import lax
from jax.experimental import pallas as pl
from jax.experimental.pallas import tpu as pltpu
from jax.sharding import PartitionSpec as P

HEAD = 64
PAIR = 2 * HEAD
LANES = 128
SCALE = HEAD ** (-0.5)
AXES = ("dp", "fsdp")
F32 = jnp.float32
BF16 = jnp.bfloat16
HIDE = -1e30
LOG2E = 1.4426950408889634
GELU = 0.7978845608028654
ONCE = pl.Buffered(1)


def contract(left, right, left_dim, right_dim):
    return lax.dot_general(
        left, right, (((left_dim,), (right_dim,)), ((), ())), preferred_element_type=F32
    )


def mult(left, right):
    return contract(left, right, 1, 0)


def cross_rows(left, right):
    return contract(left, right, 0, 0)


def back_mult(grad_rows, weight):
    return contract(grad_rows, weight, 1, 1)


def normalize(inputs):
    centred = inputs - jnp.mean(inputs, axis=-1, keepdims=True)
    root = lax.rsqrt(jnp.mean(centred * centred, axis=-1, keepdims=True) + 1e-05)
    return centred * root, root


def norm_back(normed, root, grad, gain):
    scaled = grad * gain
    return root * (
        scaled
        - jnp.mean(scaled, axis=-1, keepdims=True)
        - normed * jnp.mean(scaled * normed, axis=-1, keepdims=True)
    )


def column_sum(values):
    return jnp.sum(values, axis=0, keepdims=True)


def gate(values, *others):
    return lax.optimization_barrier((values, others))[0]


def whole(array):
    return pl.BlockSpec(array.shape, lambda i: (0,) * array.ndim, pipeline_mode=ONCE)


def token_rows(tile, width):
    return pl.BlockSpec((tile, width), lambda i: (i, 0))


def vector_out(width):
    return pl.BlockSpec((1, width), lambda i: (0, 0))


def shape(*dims, kind=BF16):
    return jax.ShapeDtypeStruct(dims, kind)


def kernel_limits(mib=60):
    return pltpu.CompilerParams(vmem_limit_bytes=mib * 2**20)


def cost(flops, size, transcendentals=0):
    return pl.CostEstimate(flops=flops, bytes_accessed=size, transcendentals=transcendentals)


def first_step(*refs):
    @pl.when(pl.program_id(0) == 0)
    def _():
        for ref in refs:
            ref[...] = jnp.zeros_like(ref)


def qkv_forward_kernel(x_ref, vectors, weight, normed_ref, merged_ref, *, sub):
    count, model = x_ref.shape

    def norm(start):
        unit, _ = normalize(x_ref[start : start + sub, :].astype(F32))
        normed = (unit * vectors[0:1, :model] + vectors[1:2, :model]).astype(BF16)
        normed_ref[start : start + sub, :] = normed
        return normed

    normed = norm(0)
    for start in range(0, count, sub):
        later = norm(start + sub) if start + sub < count else None
        merged = mult(normed, weight[...]) + vectors[2:3, : 3 * model]
        merged_ref[start : start + sub, :] = merged.astype(BF16)
        normed = later


def qkv_forward(inputs, vectors, weight, tile=512, sub=128):
    count, model = inputs.shape
    width = weight.shape[1]
    return pl.pallas_call(
        functools.partial(qkv_forward_kernel, sub=sub),
        grid=(count // tile,),
        in_specs=[token_rows(tile, model), whole(vectors), whole(weight)],
        out_specs=[token_rows(tile, model), token_rows(tile, width)],
        out_shape=[shape(count, model), shape(count, width)],
        compiler_params=kernel_limits(60),
        cost_estimate=cost(
            2 * count * model * width, 2 * (2 * count * model + (count + model) * width)
        ),
        name="qkv_forward",
    )(inputs, vectors, weight)


def mlp_kernel(
    ends, mixed_ref, x_ref, cot_ref, vectors, w_out, w_up, w_down,
    hidden_ref, normed_ref, act_ref, up_grad_ref, down_grad_ref, proj_grad_ref, hidden_grad_ref,
    mixed_grad_ref, sum_gain, sum_shift, sum_up, sum_out, sum_down, *, row, sub, chunk
):
    first_step(sum_gain, sum_shift, sum_up, sum_out, sum_down)
    tile, model = x_ref.shape
    wide = w_up.shape[1]
    b_out, gain, shift = (vectors[k : k + 1, :model] for k in (3, 4, 5))
    step = pl.program_id(0)
    steps = row // tile
    last_end = ends[step // steps, ends.shape[1] - 1]
    units = [(start, at) for start in range(0, tile, sub) for at in range(0, wide, chunk)]
    normed, units_two, roots, totals = {}, {}, {}, {}

    def begin(start):
        rows = slice(start, start + sub)
        hidden = x_ref[rows, :].astype(F32) + mult(mixed_ref[rows, :], w_out[...]) + b_out
        hidden_ref[rows, :] = hidden
        units_two[start], roots[start] = normalize(hidden)
        normed[start] = (units_two[start] * gain + shift).astype(BF16)
        normed_ref[rows, :] = normed[start]
        place = lax.broadcasted_iota(jnp.int32, (sub, 1), 0) + (step % steps * tile + start)
        down_grad = jnp.where(place < last_end, cot_ref[rows, :], jnp.zeros((), BF16))
        down_grad_ref[rows, :] = down_grad
        sum_down[...] += column_sum(down_grad.astype(F32))

    def products(start, at):
        if start not in normed:
            begin(start)
        cols = slice(at, at + chunk)
        return (
            mult(normed[start], w_up[:, cols]) + vectors[6:7, cols],
            back_mult(down_grad_ref[start : start + sub, :], w_down[cols, :]),
        )

    def finish(start):
        rows = slice(start, start + sub)
        normed_grad = totals[start]
        sum_gain[...] += column_sum(normed_grad * units_two[start])
        sum_shift[...] += column_sum(normed_grad)
        hidden_grad = norm_back(units_two[start], roots[start], normed_grad, gain)
        hidden_grad = down_grad_ref[rows, :].astype(F32) + hidden_grad
        hidden_grad_ref[rows, :] = hidden_grad
        proj_grad = hidden_grad.astype(BF16)
        proj_grad_ref[rows, :] = proj_grad
        sum_out[...] += column_sum(proj_grad.astype(F32))
        mixed_grad_ref[rows, :] = back_mult(proj_grad, w_out[...]).astype(BF16)

    ready = products(*units[0])
    waiting = None
    for index, (start, at) in enumerate(units):
        u, act_grad = ready
        if index + 1 < len(units):
            ready = products(*units[index + 1])
        rows, cols = slice(start, start + sub), slice(at, at + chunk)
        square = u * u
        smooth = jnp.tanh(u * (GELU + (GELU * 0.044715) * square))
        part = 0.5 * smooth
        share = 0.5 + part
        act_ref[rows, cols] = (u * share).astype(BF16)
        slope = share + (u * (0.5 - part * smooth)) * (GELU + (3 * GELU * 0.044715) * square)
        up_grad = (slope * act_grad).astype(BF16)
        up_grad_ref[rows, cols] = up_grad
        sum_up[:, cols] += column_sum(up_grad.astype(F32))
        grad = back_mult(up_grad, w_up[:, cols])
        totals[start] = grad if start not in totals else totals[start] + grad
        if waiting is not None:
            finish(waiting)
            waiting = None
        if at + chunk == wide:
            waiting = start
    finish(waiting)


def mlp(ends, mixed, x, cot, vectors, w_out, w_up, w_down, row, tile=512, sub=512, chunk=768):
    count, model = x.shape
    wide = w_up.shape[1]
    consts = (vectors, w_out, w_up, w_down)
    widths = [(model, F32), (model, BF16), (wide, BF16), (wide, BF16), (model, BF16)]
    widths += [(model, BF16), (model, F32), (model, BF16)]
    sums = [model, model, wide, model, model]
    return pl.pallas_call(
        functools.partial(mlp_kernel, row=row, sub=sub, chunk=chunk),
        grid=(count // tile,),
        in_specs=[pl.BlockSpec(memory_space=pltpu.SMEM)]
        + [token_rows(tile, model)] * 3
        + [whole(item) for item in consts],
        out_specs=[token_rows(tile, width) for width, _ in widths]
        + [vector_out(width) for width in sums],
        out_shape=[shape(count, width, kind=kind) for width, kind in widths]
        + [shape(1, width, kind=F32) for width in sums],
        compiler_params=kernel_limits(),
        cost_estimate=cost(
            2 * count * model * (3 * wide + 2 * model), count * (26 * model + 4 * wide), count * wide
        ),
        name="mlp",
    )(ends, mixed, x, cot, *consts)


def mlp_out_kernel(hidden_ref, act_ref, vectors, w_down, out_ref):
    model = hidden_ref.shape[1]
    out = hidden_ref[...] + mult(act_ref[...], w_down[...]) + vectors[7:8, :model]
    out_ref[...] = out.astype(BF16)


def mlp_out(hidden, act, vectors, w_down, tile=256):
    count, model = hidden.shape
    wide = act.shape[1]
    return pl.pallas_call(
        mlp_out_kernel,
        grid=(count // tile,),
        in_specs=[token_rows(tile, model), token_rows(tile, wide), whole(vectors), whole(w_down)],
        out_specs=token_rows(tile, model),
        out_shape=shape(count, model),
        compiler_params=kernel_limits(),
        cost_estimate=cost(2 * count * model * wide, count * (6 * model + 2 * wide)),
        name="mlp_out",
    )(hidden, act, vectors, w_down)


def whole_grad_kernel(left_ref, right_ref, out_ref):
    out_ref[...] = cross_rows(left_ref[...], right_ref[...]).astype(out_ref.dtype)


def whole_grad(left, right, kind, name, tile=768):
    count, high = left.shape
    wide = right.shape[1]
    tile = min(tile, high)
    return pl.pallas_call(
        whole_grad_kernel,
        grid=(high // tile,),
        in_specs=[
            pl.BlockSpec((count, tile), lambda i: (0, i)),
            pl.BlockSpec((count, wide), lambda i: (0, 0), pipeline_mode=ONCE),
        ],
        out_specs=pl.BlockSpec((tile, wide), lambda i: (i, 0)),
        out_shape=shape(high, wide, kind=kind),
        compiler_params=kernel_limits(),
        cost_estimate=cost(
            2 * count * high * wide, 2 * (count * high + count * wide + 2 * high * wide)
        ),
        name=name,
    )(left, right)


def weight_grad_kernel(core_ref, left_ref, right_ref, keep, send, *, group):
    width = right_ref.shape[1]
    step_by = math.gcd(width, 2 * LANES)

    def product(start):
        return cross_rows(left_ref[...], right_ref[:, start : start + step_by])

    ready = product(0)
    for start in range(0, width, step_by):
        grad = ready
        if start + step_by < width:
            ready = product(start + step_by)
        store_halves(core_ref, grad, group, keep, send, slice(start, start + step_by))


def qkv_grads_kernel(
    core_ref, normed, grad_ref, sum_ref, weight, vectors, *refs, steps, group, table
):
    others, pairs = refs[:6], refs[6 : 6 + 2 * steps]
    small_keep, small_send, by_grad, by_sum = refs[6 + 2 * steps :]
    step = pl.program_id(0)
    first_step(by_grad, by_sum)
    width = grad_ref.shape[1]
    step_by = math.gcd(width, 2 * LANES)

    def product(start):
        return cross_rows(normed[...], grad_ref[:, start : start + step_by])

    def tile(keep, send):
        ready = product(0)
        for start in range(0, width, step_by):
            grad = ready
            if start + step_by < width:
                ready = product(start + step_by)
            cols = slice(start, start + step_by)
            store_halves(core_ref, grad, group, keep, send, cols)
            for at in range(start, start + step_by, LANES):
                part = weight[:, at : at + LANES].astype(F32)
                by_grad[...] += part * grad[:, at - start : at - start + LANES]
                by_sum[...] += part * sum_ref[:, at : at + LANES]

    for index in range(steps):

        @pl.when(step == index)
        def _():
            tile(*pairs[2 * index : 2 * index + 2])

    @pl.when(step == steps - 1)
    def _():
        model = normed.shape[1]
        shift = column_sum(by_sum[...].T)
        total = column_sum(by_grad[...].T)
        gain = (total - vectors[1:2, :model] * shift) / vectors[0:1, :model]
        sums = [gain, shift] + [other[...] for other in others]
        fill_table(core_ref, sums, *table, small_keep, small_send)


def qkv_grads(core, group, normed, grad, others, weight, vectors, table, tile=768):
    count, model = normed.shape
    width = grad.shape[1]
    tile = min(tile, width)
    steps = width // tile
    _, _, shard, devices, _ = table
    small = devices // 2 * shard
    return pl.pallas_call(
        functools.partial(qkv_grads_kernel, steps=steps, group=group, table=table),
        grid=(steps,),
        in_specs=[
            pl.BlockSpec(memory_space=pltpu.SMEM),
            whole(normed),
            pl.BlockSpec((count, tile), lambda i: (0, i)),
            pl.BlockSpec((1, tile), lambda i: (0, i)),
            pl.BlockSpec((model, tile), lambda i: (0, i)),
            whole(vectors),
        ]
        + [whole(other) for other in others],
        out_specs=[pl.BlockSpec((model // 2, tile), lambda i: (0, 0))] * (2 * steps)
        + [pl.BlockSpec((small, LANES), lambda i: (0, 0))] * 2,
        out_shape=[shape(model // 2, tile)] * (2 * steps) + [shape(small, LANES)] * 2,
        scratch_shapes=[pltpu.VMEM((model, LANES), F32)] * 2,
        compiler_params=kernel_limits(),
        cost_estimate=cost(
            2 * count * model * width, 2 * (count * model + count * width + 2 * model * width)
        ),
        name="qkv_grads",
    )(core, normed, grad, others[0], weight, vectors, *others)


def store_halves(core_ref, grad, group, keep, send, cols):
    first, second = [
        jnp.concatenate(
            [grad[k : k + group] for k in range(which * group, grad.shape[0], 2 * group)], axis=0
        )
        for which in range(2)
    ]
    swapped = core_ref[0] == 1
    keep[:, cols] = jnp.where(swapped, second, first).astype(BF16)
    send[:, cols] = jnp.where(swapped, first, second).astype(BF16)


def weight_grad(core, group, left, right, name, tile=768):
    count, high = left.shape
    wide = right.shape[1]
    tile = min(tile, wide)
    return pl.pallas_call(
        functools.partial(weight_grad_kernel, group=group),
        grid=(wide // tile,),
        in_specs=[
            pl.BlockSpec(memory_space=pltpu.SMEM),
            pl.BlockSpec((count, high), lambda i: (0, 0), pipeline_mode=ONCE),
            pl.BlockSpec((count, tile), lambda i: (0, i)),
        ],
        out_specs=[pl.BlockSpec((high // 2, tile), lambda i: (0, i))] * 2,
        out_shape=[shape(high // 2, wide)] * 2,
        compiler_params=kernel_limits(),
        cost_estimate=cost(
            2 * count * high * wide, 2 * (count * high + count * wide + high * wide)
        ),
        name=name,
    )(core, left, right)


def qkv_backward_kernel(
    grad_ref, x_ref, hidden_grad_ref, vectors, weight, out_ref, *, sub
):
    count, model = x_ref.shape
    gain = vectors[0:1, :model]

    def lower(start):
        return back_mult(grad_ref[start : start + sub, :], weight[...])

    ready = lower(0)
    for start in range(0, count, sub):
        normed_grad = ready
        if start + sub < count:
            ready = lower(start + sub)
        rows = slice(start, start + sub)
        unit, root = normalize(x_ref[rows, :].astype(F32))
        inner = norm_back(unit, root, normed_grad, gain)
        out_ref[rows, :] = (hidden_grad_ref[rows, :] + inner).astype(BF16)


def qkv_backward(grad, x, hidden_grad, vectors, weight, tile=512, sub=256):
    count, model = x.shape
    width = weight.shape[1]
    return pl.pallas_call(
        functools.partial(qkv_backward_kernel, sub=sub),
        grid=(count // tile,),
        in_specs=[token_rows(tile, width)]
        + [token_rows(tile, model)] * 2
        + [whole(vectors), whole(weight)],
        out_specs=token_rows(tile, model),
        out_shape=shape(count, model),
        compiler_params=kernel_limits(),
        cost_estimate=cost(
            2 * count * model * width, 2 * (4 * count * model + (count + model) * width)
        ),
        name="qkv_backward",
    )(grad, x, hidden_grad, vectors, weight)


def segments(ends, index, shape, axis):
    place = lax.broadcasted_iota(jnp.int32, shape, axis)
    found = jnp.zeros(shape, jnp.int32)
    for slot in range(ends.shape[1]):
        found = found + (ends[index, slot] <= place).astype(jnp.int32)
    return found


def allowed_bias(ends, row):
    index = pl.program_id(0)
    keys = lax.broadcasted_iota(jnp.int32, (row, row), 0)
    queries = lax.broadcasted_iota(jnp.int32, (row, row), 1)
    same = segments(ends, index, (row, 1), 0) == segments(ends, index, (1, row), 1)
    return jnp.where(same & (keys <= queries), 0.0, HIDE)


def pair_lanes(pair):
    return slice(pair * PAIR, (pair + 1) * PAIR)


def head_rows(head):
    return slice(head * HEAD, (head + 1) * HEAD)


def own_lanes(values, head):
    lane = lax.broadcasted_iota(jnp.int32, (1, PAIR), 1)
    return jnp.where((lane < HEAD) == (head == 0), values, jnp.zeros((), BF16))


def key_blocks(half, part, step):
    for start in range(0, (part + 1) * half, step):
        low = max(0, (start - part * half) // LANES * LANES) if start >= part * half else 0
        yield start, low


def widen(values, low, fill):
    if low == 0:
        return values
    pad = jnp.full((values.shape[0], low), fill, values.dtype)
    return jnp.concatenate([pad, values], axis=1)


def folded(values, combine):
    return combine(values.reshape(values.shape[0] // 8, 8, values.shape[1]), axis=0)


def unit_list(pairs):
    return [(pair, part, head) for pair in range(pairs) for part in range(2) for head in range(2)]


def forward_kernel(
    ends, q_ref, k_ref, v_ref, mixed_ref, total_ref, bias, *, pairs, step, lead
):
    row = q_ref.shape[0]
    half = row // 2
    bias[...] = allowed_bias(ends, row)

    def scores_of(pair, part, head):
        seen = (part + 1) * half
        queries = q_ref[part * half : seen, pair_lanes(pair)] * jnp.asarray(SCALE, BF16)
        return back_mult(k_ref[:seen, pair_lanes(pair)], own_lanes(queries, head))

    def weigh(part, scores):
        base = part * half
        top = jnp.full((8, half), HIDE, F32)
        shown = []
        for start, low in key_blocks(half, part, step):
            block = scores[start : start + step, low:]
            square = block * block + 1.0
            mag = square * (lax.rsqrt(square) * LOG2E)
            mag = mag + bias[start : start + step, base + low : base + half]
            shown.append(mag)
            top = jnp.maximum(top, widen(folded(mag, jnp.max), low, HIDE))
        top = jnp.max(top, axis=0, keepdims=True)
        total = jnp.zeros((8, half), F32)
        signed = []
        for (start, low), mag in zip(key_blocks(half, part, step), shown):
            weight = jnp.exp2(mag - top[:, low:])
            total = total + widen(folded(weight, jnp.sum), low, 0.0)
            block = jnp.tanh(scores[start : start + step, low:]) * weight
            signed.append(widen(block.astype(BF16), low, 0.0))
        return jnp.concatenate(signed, axis=0), top, jnp.sum(total, axis=0, keepdims=True)

    units = unit_list(pairs)
    scores = [scores_of(*unit) for unit in units[:lead]]
    turned, parts = {}, {}

    def finish(unit, signed, top, total):
        pair, part, head = unit
        here = slice(part * half, (part + 1) * half)
        total_ref[0, pair, head : head + 1, here] = top * (1.0 / LOG2E) + jnp.log(total)
        values = turned[pair][head_rows(head), : (part + 1) * half]
        parts[unit] = mult(values, signed) * (1.0 / total)
        if head == 1:
            both = jnp.concatenate([parts[pair, part, 0], parts[unit]], axis=0)
            mixed_ref[here, pair_lanes(pair)] = both.T.astype(BF16)

    waiting = None
    for index, unit in enumerate(units):
        if index + lead < len(units):
            scores.append(scores_of(*units[index + lead]))
        if unit[0] not in turned:
            turned[unit[0]] = v_ref[:, pair_lanes(unit[0])].T
        weighed = weigh(unit[1], scores[index])
        if waiting is not None:
            finish(*waiting)
        waiting = (unit,) + weighed
    finish(*waiting)


def attention_forward(ends, merged, row):
    count, width = merged.shape
    model = width // 3
    pairs = model // PAIR
    micro = count // row
    area = micro * pairs * 2 * row * row

    def third(index):
        return pl.BlockSpec((row, model), lambda r: (r, index))

    return pl.pallas_call(
        functools.partial(forward_kernel, pairs=pairs, step=32, lead=2),
        grid=(micro,),
        in_specs=[
            pl.BlockSpec(memory_space=pltpu.SMEM),
            third(0),
            third(1),
            third(2),
        ],
        out_specs=[
            pl.BlockSpec((row, model), lambda r: (r, 0)),
            pl.BlockSpec((1, pairs, 2, row), lambda r: (r, 0, 0, 0)),
        ],
        out_shape=[shape(count, model), shape(micro, pairs, 2, row, kind=F32)],
        scratch_shapes=[pltpu.VMEM((row, row), F32)],
        compiler_params=kernel_limits(),
        cost_estimate=cost(area * 4 * HEAD * 5, count * width * 3, area * 3),
        name="attention_forward",
    )(ends, merged, merged, merged)


def backward_kernel(
    ends, q_ref, k_ref, v_ref, mixed_ref, grad_ref, total_ref,
    out_ref, sum_ref, bias, *, pairs, step, lead, lag
):
    row = q_ref.shape[0]
    half = row // 2
    model = pairs * PAIR
    first_step(sum_ref)
    bias[...] = allowed_bias(ends, row)

    def put(section, pair, rows, values):
        cols = slice(section * model + pair * PAIR, section * model + (pair + 1) * PAIR)
        values = values.astype(BF16)
        out_ref[rows, cols] = values
        sum_ref[:, cols] += column_sum(values.astype(F32))

    def queries_and_grads(pair, part, head):
        here = slice(part * half, (part + 1) * half)
        queries = q_ref[here, pair_lanes(pair)] * jnp.asarray(SCALE, BF16)
        return own_lanes(queries, head), own_lanes(grad_ref[here, pair_lanes(pair)], head)

    def products(pair, part, head):
        seen = (part + 1) * half
        queries, grads = queries_and_grads(pair, part, head)
        return (
            back_mult(k_ref[:seen, pair_lanes(pair)], queries),
            back_mult(v_ref[:seen, pair_lanes(pair)], grads),
        )

    centres, turned, sums, query_parts = {}, {}, {}, {}

    def weigh(pair, part, head, scores, weight_grads):
        base = part * half
        here = slice(base, base + half)
        if (pair, part) not in centres:
            grads = grad_ref[here, pair_lanes(pair)].astype(F32)
            centres[pair, part] = (grads * mixed_ref[here, pair_lanes(pair)].astype(F32)).T
        centre = column_sum(centres[pair, part][head_rows(head)])
        total = total_ref[0, pair, head : head + 1, here] * LOG2E
        signed, score_grads = [], []
        for start, low in key_blocks(half, part, step):
            block = scores[start : start + step, low:]
            weight_grad = weight_grads[start : start + step, low:]
            square = block * block + 1.0
            root = lax.rsqrt(square)
            shift = bias[start : start + step, base + low : base + half] - total[:, low:]
            weight = jnp.exp2(square * (root * LOG2E) + shift)
            smooth = jnp.tanh(block)
            bent = weight_grad * smooth
            score_grad = weight * (
                (weight_grad - bent * smooth) + (block * root) * (bent - centre[:, low:])
            )
            signed.append(widen((smooth * weight).astype(BF16), low, 0.0))
            score_grads.append(widen(score_grad.astype(BF16), low, 0.0))
        return jnp.concatenate(signed, axis=0), jnp.concatenate(score_grads, axis=0)

    def finish(unit, signed, score_grads):
        pair, part, head = unit
        queries, grads = queries_and_grads(*unit)
        for section, grad in ((2, mult(signed, grads)), (1, mult(score_grads, queries))):
            for block in range(part + 1):
                add = grad[block * half : (block + 1) * half]
                key = (pair, section, block)
                sums[key] = add if key not in sums else sums[key] + add
        if pair not in turned:
            turned[pair] = k_ref[:, pair_lanes(pair)].T
        keys = turned[pair][head_rows(head), : (part + 1) * half]
        query_parts[unit] = mult(keys, score_grads)
        if head == 1:
            both = jnp.concatenate([query_parts[pair, part, 0], query_parts[unit]], axis=0)
            put(0, pair, slice(part * half, (part + 1) * half), both.T * SCALE)
        if head == 1 and part == 1:
            for section in (1, 2):
                for block in range(2):
                    rows = slice(block * half, (block + 1) * half)
                    put(section, pair, rows, sums[pair, section, block])

    units = unit_list(pairs)
    ready = [products(*unit) for unit in units[:lead]]
    waiting = []
    for index, unit in enumerate(units):
        if index + lead < len(units):
            ready.append(products(*units[index + lead]))
        waiting.append((unit,) + weigh(*unit, *ready[index]))
        ready[index] = None
        if len(waiting) > lag:
            finish(*waiting.pop(0))
    for item in waiting:
        finish(*item)


def attention_backward(ends, merged, mixed, mixed_grad, total, row):
    count, width = merged.shape
    model = width // 3
    pairs = model // PAIR
    micro = count // row
    area = micro * pairs * 2 * row * row

    def third(index):
        return pl.BlockSpec((row, model), lambda r: (r, index))

    return pl.pallas_call(
        functools.partial(backward_kernel, pairs=pairs, step=32, lead=1, lag=0),
        grid=(micro,),
        in_specs=[
            pl.BlockSpec(memory_space=pltpu.SMEM),
            third(0),
            third(1),
            third(2),
            third(0),
            third(0),
            pl.BlockSpec((1, pairs, 2, row), lambda r: (r, 0, 0, 0)),
        ],
        out_specs=[pl.BlockSpec((row, width), lambda r: (r, 0)), vector_out(width)],
        out_shape=[shape(count, width), shape(1, width, kind=F32)],
        scratch_shapes=[pltpu.VMEM((row, row), F32)],
        compiler_params=kernel_limits(),
        cost_estimate=cost(area * 10 * HEAD * 4, count * width * 5, area * 3),
        name="attention_backward",
    )(ends, merged, merged, merged, mixed, mixed_grad, total)


def vector_slots(lengths):
    slots, fill = [], []
    for length in lengths:
        row = next((r for r, used in enumerate(fill) if used + length <= LANES), len(fill))
        if row == len(fill):
            fill.append(0)
        slots.append((row, fill[row], length))
        fill[row] += length
    return slots, len(fill)


def lane_of(devices, length, first):
    size = devices * length
    place = lax.broadcasted_iota(jnp.int32, (LANES, size), 1).astype(F32)
    inside = place - length * jnp.floor((place + 0.5) * (1.0 / length))
    lane = lax.broadcasted_iota(jnp.int32, (LANES, size), 0).astype(F32)
    return (lane == inside + first).astype(BF16)


def owner_of(devices, length):
    size = devices * length
    place = lax.broadcasted_iota(jnp.int32, (devices, size), 1)
    start = lax.broadcasted_iota(jnp.int32, (devices, size), 0) * length
    return (place >= start) & (place < start + length)


def vectors_from_table(table, slots):
    devices = table.shape[1]
    longest = devices * max(length for _, _, length in slots)

    def kernel(table_ref, out):
        for index, (row, first, length) in enumerate(slots):
            spread = mult(table_ref[row], lane_of(devices, length, first))
            out[index : index + 1, : devices * length] = column_sum(
                jnp.where(owner_of(devices, length), spread, 0.0)
            )

    return pl.pallas_call(
        kernel,
        out_shape=shape(len(slots), longest, kind=F32),
        compiler_params=kernel_limits(40),
        name="vectors_from_table",
    )(table)


def split(values, size):
    quotient = jnp.floor((values + 0.5) * (1.0 / size))
    return quotient, values - size * quotient


def fill_table(core_ref, vectors, slots, rows, shard, devices, inner, keep, send):
    filled = [jnp.zeros((devices, LANES), F32) for _ in range(rows)]
    for (row, first, length), vector in zip(slots, vectors):
        own = jnp.where(owner_of(devices, length), vector, 0.0).astype(BF16)
        filled[row] = filled[row] + back_mult(own, lane_of(devices, length, first))
    stacked = jnp.concatenate(filled, axis=0).astype(BF16)
    size = (devices // 2 * shard, devices * rows)
    target = lax.broadcasted_iota(jnp.int32, size, 0).astype(F32)
    source = lax.broadcasted_iota(jnp.int32, size, 1).astype(F32)
    block, row = split(target, shard)
    chip, y = split(block, inner)
    swapped = core_ref[0] == 1
    halves = []
    for which in range(2):
        match = source == row * devices + (chip * 2 + which) * inner + y
        halves.append(mult(jnp.where(row < rows, match.astype(F32), 0.0).astype(BF16), stacked))
    keep[...] = jnp.where(swapped, halves[1], halves[0]).astype(BF16)
    send[...] = jnp.where(swapped, halves[0], halves[1]).astype(BF16)


class Links:
    def __init__(self, mesh):
        self.outer = mesh.shape["dp"]
        self.inner = mesh.shape["fsdp"]
        self.count = self.outer * self.inner
        self.far = [(k << 2) * self.inner for k in range(self.outer // 4)]
        self.near = [(b << 1) * self.inner + f for b in range(2) for f in range(self.inner)]
        self.core = self.inner

    def place(self):
        return lax.axis_index("dp") * self.inner + lax.axis_index("fsdp")

    def swap(self, piece, mask):
        return lax.ppermute(piece, AXES, [(i, i ^ mask) for i in range(self.count)])

    def far_step(self, shard):
        got = [self.swap(shard, mask) for mask in self.far[1:]]
        return lambda *others: jnp.stack([shard] + gate(got, *others))

    def far_doubled(self, shard):
        column = shard[None]
        while column.shape[0] < len(self.far):
            column = jnp.concatenate([column, self.swap(column, self.far[column.shape[0]])])
        return column

    def near_step(self, column):
        return [column] + [self.swap(column, mask) for mask in self.near[1:]]

    def near_halves(self, column):
        if len(self.near) != 4:
            plane = self.near_step(column)
            return plane, lambda *others: gate(plane, *others)
        side, inner = [self.swap(column, mask) for mask in (self.near[2], self.near[1])]
        plane = [column, inner, side]
        width = half_columns(column)

        def second(*others):
            left, right = gate((inner[:, :, :width], side[:, :, width:]), *others)
            return plane + [self.swap(left, self.near[2]), self.swap(right, self.near[1])]

        return plane, second

    def core_step(self, plane):
        return plane + [self.swap(piece, self.core) for piece in plane]

    def arrange(self, pieces, columns):
        far = self.far
        held = len(pieces)
        masks, ranges = list(self.near), [(0, pieces[0].shape[2])] * len(self.near)
        if held > 2 * len(masks):
            half = half_columns(pieces[0])
            masks, ranges = masks + masks[-1:], ranges[:-1] + [(0, half), (half, ranges[0][1])]
        masks, ranges = masks + [mask ^ self.core for mask in masks], ranges * 2
        rows = pieces[0].shape[1]

        def kernel(me_ref, *refs):
            results = refs[held : held + len(columns)]
            targets = refs[held + len(columns) : held + 2 * len(columns)]
            sems, out_sem = refs[-2:]
            me = me_ref[0]
            copies = [[] for _ in columns]
            for piece, mask, (low, high) in zip(refs[:held], masks, ranges):
                for k, step in enumerate(far):
                    owner = jnp.bitwise_xor(me, mask ^ step)
                    for which, (start, width, parts) in enumerate(columns):
                        for part in range(parts):
                            base = start + part * width
                            one, two = max(low, base), min(high, base + width)
                            if one >= two:
                                continue
                            copies[which].append(
                                pltpu.make_async_copy(
                                    piece.at[k, :, pl.ds(one - low, two - one)],
                                    targets[which].at[
                                        owner * parts + part, :, pl.ds(one - base, two - one)
                                    ],
                                    sems.at[which],
                                )
                            )
            for group in copies:
                for copy in group:
                    copy.start()
            outs = [
                pltpu.make_async_copy(target, result, out_sem.at[which])
                for which, (target, result) in enumerate(zip(targets, results))
            ]
            for group, out in zip(copies, outs):
                for copy in group:
                    copy.wait()
                out.start()
            for out in outs:
                out.wait()

        return pl.pallas_call(
            kernel,
            in_specs=[pl.BlockSpec(memory_space=pltpu.SMEM)]
            + [pl.BlockSpec(memory_space=pl.ANY)] * held,
            out_specs=[pl.BlockSpec(memory_space=pl.ANY)] * len(columns),
            out_shape=[
                jax.ShapeDtypeStruct((self.count * parts, rows, width), BF16)
                for _, width, parts in columns
            ],
            scratch_shapes=[
                pltpu.VMEM((self.count * parts, rows, width), BF16) for _, width, parts in columns
            ]
            + [pltpu.SemaphoreType.DMA((len(columns),))] * 2,
            compiler_params=kernel_limits(),
            name="arrange",
        )(jnp.full((1,), self.place(), jnp.int32), *pieces)

    def position(self):
        dp = lax.axis_index("dp")
        return dp >> 2, (dp >> 1) & 1, dp & 1, lax.axis_index("fsdp")

    def core_swap(self, pair):
        return pair[0], self.swap(pair[1], self.core)

    def kernel_sums(self, pairs, name):
        _, side, _, inner = self.position()
        far, span = len(self.far), self.inner
        rows = pairs[0][0].shape[0] * 2 // self.count
        widths = [keep.shape[1] for keep, _ in pairs]

        def view(array):
            return array.reshape(far, 2, span, rows, array.shape[1])

        count = 2 * len(pairs)

        def kernel(place, *refs):
            sources, refs = refs[:count], refs[count:]
            outs, held, sems = refs[: 2 * span], refs[2 * span : -1], refs[-1]
            copies = [
                pltpu.make_async_copy(source, target, sems.at[index])
                for index, (source, target) in enumerate(zip(sources, held))
            ]
            for copy in copies:
                copy.start()
            at = 0
            for index, width in enumerate(widths):
                one, two = held[2 * index], held[2 * index + 1]
                copies[2 * index].wait()
                copies[2 * index + 1].wait()
                for partner, out in enumerate(outs):
                    x = jnp.bitwise_xor(place[0], partner // span)
                    y = jnp.bitwise_xor(place[1], partner % span)
                    for z in range(far):
                        total = one[z, x, y].astype(F32) + two[z, x, y].astype(F32)
                        out[z, :, at : at + width] = total.astype(BF16)
                at += width

        size = self.count // 2 * rows * sum(widths)
        arrays = [view(array) for pair in pairs for array in pair]
        call = pl.pallas_call(
            kernel,
            in_specs=[pl.BlockSpec(memory_space=pltpu.SMEM)]
            + [pl.BlockSpec(memory_space=pl.ANY)] * count,
            out_shape=[shape(far, rows, sum(widths))] * (2 * span),
            scratch_shapes=[pltpu.VMEM(array.shape, BF16) for array in arrays]
            + [pltpu.SemaphoreType.DMA((count,))],
            compiler_params=kernel_limits(),
            cost_estimate=cost(size, 6 * size),
            name=name,
        )
        place = jnp.stack([side, inner]).astype(jnp.int32)
        return list(call(place, *arrays))

    def fused_sums(self, pairs, join):
        _, side, _, inner = self.position()

        def view(array):
            rows = array.shape[0] * 2 // self.count
            return array.reshape(self.outer // 4, 2, self.inner, rows, array.shape[1])

        mine = [view(keep) for keep, _ in pairs]
        got = [view(received) for _, received in pairs]

        def finish(*others):
            received = gate(got, *others) if others else got
            sums = []
            for b in range(2):
                for f in range(self.inner):

                    def cut(array):
                        return pick(pick(array, side ^ b, 1), inner ^ f, 1).astype(F32)

                    sums.append(
                        join([(cut(a) + cut(b)).astype(BF16) for a, b in zip(mine, received)])
                    )
            return sums

        return finish

    def near_swaps(self, sums):
        return sums[:1] + [self.swap(part, mask) for part, mask in zip(sums[1:], self.near[1:])]

    def near_sums(self, sums):
        return self.far_parts(self.near_swaps(sums))

    def far_parts(self, got):
        column = self.position()[0]

        def finish(*others):
            received = gate(got, *others)
            parts = []
            for k in range(len(self.far)):
                part = sum(pick(array, column ^ k, 0).astype(F32) for array in received)
                parts.append(part if k == 0 else part.astype(BF16))
            return parts

        return finish

    def far_sums(self, parts):
        got = [self.swap(part, mask) for part, mask in zip(parts[1:], self.far[1:])]

        def finish(*others):
            received = gate(got, *others)
            return functools.reduce(lambda sum, part: sum + part.astype(F32), received, parts[0])

        return got, finish


def far_start(links, sums):
    column = links.position()[0]

    def part(k):
        return sum(pick(array, column ^ k, 0).astype(F32) for array in sums)

    if len(links.far) != 4:
        parts = [part(k) for k in range(len(links.far))]
        return (), lambda *others: (
            gate(parts[0], *others),
            {k: parts[k].astype(BF16) for k in range(1, len(parts))},
        )
    got = links.swap(jnp.stack([part(2), part(3)]).astype(BF16), links.far[2])

    def second(*others):
        received = gate(got, *others).astype(F32)
        return part(0) + received[0], {1: (part(1) + received[1]).astype(BF16)}

    return got, second


def far_join(links, blocks):
    got = {}
    for k in range(1, len(links.far)):
        sent = [(index, parts[k]) for index, (_, parts) in enumerate(blocks) if k in parts]
        arrived = links.swap(jnp.concatenate([part for _, part in sent], axis=1), links.far[k])
        at = 0
        for index, part in sent:
            got.setdefault(index, []).append((arrived, at, part.shape[1]))
            at += part.shape[1]

    return got, [own for own, _ in blocks]


def last_sums(got, owns, splits, down):
    arrays, order = [], {}
    for pieces in got.values():
        for array, _, _ in pieces:
            if id(array) not in order:
                order[id(array)] = len(arrays)
                arrays.append(array)

    def kernel(*refs):
        own_refs, refs = refs[: len(owns)], refs[len(owns) :]
        array_refs, refs = refs[: len(arrays)], refs[len(arrays) :]
        outs = list(refs[1:])
        for index, own in enumerate(own_refs):
            for start, width in splits[index]:
                total = own[:, start : start + width]
                for array, at, _ in got[index]:
                    part = array_refs[order[id(array)]][:, at + start : at + start + width]
                    total = total + part.astype(F32)
                outs.pop(0)[...] = total
        outs.pop(0)[...] = refs[0][...].astype(F32)

    rows = owns[0].shape[0]
    return pl.pallas_call(
        kernel,
        out_shape=[shape(rows, width, kind=F32) for cuts in splits for _, width in cuts]
        + [shape(*down.shape, kind=F32)],
        compiler_params=kernel_limits(24),
        name="last_sums",
    )(*owns, *arrays, down)


def half_columns(array):
    return array.shape[2] // 2 // LANES * LANES


def pick(array, index, axis):
    return lax.dynamic_index_in_dim(array, index, axis, keepdims=False)


def run(
    links,
    tokens,
    lengths,
    cotangent,
    attn_norm_gain,
    attn_norm_bias,
    qkv_weight,
    qkv_bias,
    out_weight,
    out_bias,
    mlp_norm_gain,
    mlp_norm_bias,
    up_weight,
    up_bias,
    down_weight,
    down_bias,
):
    micro, row, model = tokens.shape
    count = micro * row
    shard = qkv_weight.shape[0]
    wide = up_weight.shape[1]
    devices = links.count

    vectors = (
        attn_norm_gain,
        attn_norm_bias,
        qkv_bias,
        out_bias,
        mlp_norm_gain,
        mlp_norm_bias,
        up_bias,
        down_bias,
    )
    slots, table_rows = vector_slots([vector.shape[0] for vector in vectors])
    lines = []
    for line in range(table_rows):
        held = [v for v, slot in zip(vectors, slots) if slot[0] == line]
        held = jnp.concatenate(held)
        lines.append(jnp.pad(held, (0, LANES - held.shape[0])))
    extra = jnp.pad(jnp.stack(lines), ((0, shard - table_rows), (0, 0)))
    qkv_far = links.far_step(jnp.concatenate([qkv_weight, extra], axis=1))
    middle_in = jnp.concatenate([out_weight, up_weight], axis=1)
    middle_column = links.far_doubled(middle_in)
    qkv_column = qkv_far()
    qkv_plane = links.near_step(qkv_column)
    w_down = lax.all_gather(down_weight, AXES, axis=0, tiled=True)
    middle_start, middle_corner = links.near_halves(gate(middle_column, qkv_plane))
    w_qkv, extra = links.arrange(
        links.core_step(qkv_plane), [(0, 3 * model, 1), (3 * model, LANES, 1)]
    )
    w_qkv = w_qkv.reshape(model, 3 * model)
    table = vectors_from_table(extra[:, :table_rows].swapaxes(0, 1), slots)

    ends = jnp.cumsum(lengths.reshape(micro, -1), axis=1, dtype=jnp.int32)
    inputs = tokens.reshape(count, model)
    normed_one, merged = qkv_forward(inputs, table, w_qkv)
    middle_plane = middle_corner(merged)
    mixed, log_total = attention_forward(ends, gate(merged, middle_start), row)
    middle_pieces = links.core_step(middle_plane[:3] + gate(middle_plane[3:], mixed))
    w_out, w_up = links.arrange(gate(middle_pieces, mixed), [(0, model, 1), (model, wide, 1)])
    w_out = w_out.reshape(model, model)
    w_up = w_up.reshape(model, wide)
    (
        hidden,
        normed_two,
        activated,
        up_grad,
        down_grad,
        proj_grad,
        hidden_grad,
        mixed_grad,
        sum_gain_two,
        sum_shift_two,
        sum_up,
        sum_out,
        sum_down,
    ) = mlp(
        ends, mixed, inputs, cotangent.reshape(count, model), table, w_out, w_up, w_down, row
    )

    core = jnp.full((1,), links.position()[2], jnp.int32)
    group = links.inner * shard
    grad_up = weight_grad(core, group, normed_two, up_grad, "grad_up")
    grad_up = links.core_swap(grad_up)
    grad_down = whole_grad(activated, gate(down_grad, grad_up[0]), BF16, "grad_down")
    down_block = lax.psum_scatter(grad_down, AXES, scatter_dimension=0, tiled=True)
    grad_out = weight_grad(core, group, mixed, gate(proj_grad, grad_down), "grad_out")
    early = links.fused_sums(
        [links.core_swap(grad_out), grad_up], lambda cuts: jnp.concatenate(cuts, axis=2)
    )(grad_out[0])
    early_near = links.near_swaps(early)
    qkv_grad, sum_qkv = attention_backward(
        ends, merged, mixed, gate(mixed_grad, early), log_total, row
    )
    early_near = gate(early_near, qkv_grad)
    early_first, early_second = far_start(links, early_near)
    *grad_qkv, small_keep, small_send = qkv_grads(
        core,
        group,
        normed_one,
        gate(qkv_grad, early_near),
        (sum_qkv, sum_out, sum_gain_two, sum_shift_two, sum_up, sum_down),
        w_qkv,
        table,
        (slots, table_rows, shard, devices, links.inner),
    )
    small = (small_keep, small_send)

    late = [links.core_swap(pair) for pair in zip(grad_qkv[::2], grad_qkv[1::2])]
    late = links.kernel_sums([*late, links.core_swap(small)], "late_sums")
    late_parts = links.near_sums(late)
    block_out = mlp_out(hidden, gate(activated, late), table, w_down)
    early_own, early_sent = early_second(block_out)
    late_parts = late_parts(block_out)
    late_sent = {k: late_parts[k] for k in range(1, len(late_parts))}
    got, owns = far_join(links, [(early_own, early_sent), (late_parts[0], late_sent)])
    token_grad = qkv_backward(
        gate(qkv_grad, late_parts, early_sent, block_out),
        inputs,
        hidden_grad,
        table,
        w_qkv,
    )
    keys = [(index, place) for index in got for place in range(len(got[index]))]
    arrived = gate([got[index][place][0] for index, place in keys], token_grad)
    unique = {}
    for (index, place), array in zip(keys, arrived):
        array = unique.setdefault(id(got[index][place][0]), array)
        got[index][place] = (array,) + got[index][place][1:]
    out_block, up_block, qkv_block, small_block, down_block = last_sums(
        got, owns, [[(0, model), (model, wide)], [(0, 3 * model), (3 * model, LANES)]], down_block
    )
    (
        gain_one_shard,
        bias_one_shard,
        bias_qkv_shard,
        bias_out_shard,
        gain_two_shard,
        bias_two_shard,
        bias_up_shard,
        bias_down_shard,
    ) = [
        small_block[line, start : start + length]
        for line, start, length in slots
    ]
    return (
        block_out.reshape(tokens.shape),
        token_grad.reshape(tokens.shape),
        gain_one_shard,
        bias_one_shard,
        qkv_block,
        bias_qkv_shard,
        out_block,
        bias_out_shard,
        gain_two_shard,
        bias_two_shard,
        up_block,
        bias_up_shard,
        down_block,
        bias_down_shard,
    )


def solution(mesh):
    links = Links(mesh)
    rows = P(None, AXES, None)
    vector = P(AXES)
    matrix = P(AXES, None)
    params = (
        vector,
        vector,
        matrix,
        vector,
        matrix,
        vector,
        vector,
        vector,
        matrix,
        vector,
        matrix,
        vector,
    )
    return jax.shard_map(
        lambda *args: run(links, *args),
        mesh=mesh,
        in_specs=(rows, rows, rows) + params,
        out_specs=(rows, rows) + params,
        check_vma=False,
    )
```

```python
import functools
import math

import jax
import jax.numpy as jnp
from jax import lax
from jax.experimental import pallas as pl
from jax.experimental.pallas import tpu as pltpu
from jax.sharding import PartitionSpec as P

HEAD = 64
PAIR = 2 * HEAD
LANES = 128
SCALE = HEAD ** (-0.5)
AXES = ("dp", "fsdp")
F32 = jnp.float32
BF16 = jnp.bfloat16
HIDE = -1e30
LOG2E = 1.4426950408889634
GELU = 0.7978845608028654
ONCE = pl.Buffered(1)


def contract(left, right, left_dim, right_dim):
    return lax.dot_general(
        left, right, (((left_dim,), (right_dim,)), ((), ())), preferred_element_type=F32
    )


def mult(left, right):
    return contract(left, right, 1, 0)


def cross_rows(left, right):
    return contract(left, right, 0, 0)


def back_mult(grad_rows, weight):
    return contract(grad_rows, weight, 1, 1)


def normalize(inputs):
    centred = inputs - jnp.mean(inputs, axis=-1, keepdims=True)
    root = lax.rsqrt(jnp.mean(centred * centred, axis=-1, keepdims=True) + 1e-05)
    return centred * root, root


def norm_back(normed, root, grad, gain):
    scaled = grad * gain
    return root * (
        scaled
        - jnp.mean(scaled, axis=-1, keepdims=True)
        - normed * jnp.mean(scaled * normed, axis=-1, keepdims=True)
    )


def column_sum(values):
    return jnp.sum(values, axis=0, keepdims=True)


def gate(values, *others):
    return lax.optimization_barrier((values, others))[0]


def whole(array):
    return pl.BlockSpec(array.shape, lambda i: (0,) * array.ndim, pipeline_mode=ONCE)


def token_rows(tile, width):
    return pl.BlockSpec((tile, width), lambda i: (i, 0))


def vector_out(width):
    return pl.BlockSpec((1, width), lambda i: (0, 0))


def shape(*dims, kind=BF16):
    return jax.ShapeDtypeStruct(dims, kind)


def kernel_limits(mib=60):
    return pltpu.CompilerParams(vmem_limit_bytes=mib * 2**20)


def cost(flops, size, transcendentals=0):
    return pl.CostEstimate(flops=flops, bytes_accessed=size, transcendentals=transcendentals)


def first_step(*refs):
    @pl.when(pl.program_id(0) == 0)
    def _():
        for ref in refs:
            ref[...] = jnp.zeros_like(ref)


def qkv_forward_kernel(x_ref, vectors, weight, normed_ref, merged_ref, *, sub):
    count, model = x_ref.shape

    def norm(start):
        unit, _ = normalize(x_ref[start : start + sub, :].astype(F32))
        normed = (unit * vectors[0:1, :model] + vectors[1:2, :model]).astype(BF16)
        normed_ref[start : start + sub, :] = normed
        return normed

    normed = norm(0)
    for start in range(0, count, sub):
        later = norm(start + sub) if start + sub < count else None
        merged = mult(normed, weight[...]) + vectors[2:3, : 3 * model]
        merged_ref[start : start + sub, :] = merged.astype(BF16)
        normed = later


def qkv_forward(inputs, vectors, weight, tile=512, sub=128):
    count, model = inputs.shape
    width = weight.shape[1]
    return pl.pallas_call(
        functools.partial(qkv_forward_kernel, sub=sub),
        grid=(count // tile,),
        in_specs=[token_rows(tile, model), whole(vectors), whole(weight)],
        out_specs=[token_rows(tile, model), token_rows(tile, width)],
        out_shape=[shape(count, model), shape(count, width)],
        compiler_params=kernel_limits(60),
        cost_estimate=cost(
            2 * count * model * width, 2 * (2 * count * model + (count + model) * width)
        ),
        name="qkv_forward",
    )(inputs, vectors, weight)


def mlp_kernel(
    ends, mixed_ref, x_ref, cot_ref, vectors, w_out, w_up, w_down,
    hidden_ref, normed_ref, act_ref, up_grad_ref, down_grad_ref, proj_grad_ref, hidden_grad_ref,
    mixed_grad_ref, sum_gain, sum_shift, sum_up, sum_out, sum_down, *, row, sub, chunk
):
    first_step(sum_gain, sum_shift, sum_up, sum_out, sum_down)
    tile, model = x_ref.shape
    wide = w_up.shape[1]
    b_out, gain, shift = (vectors[k : k + 1, :model] for k in (3, 4, 5))
    step = pl.program_id(0)
    steps = row // tile
    last_end = ends[step // steps, ends.shape[1] - 1]
    units = [(start, at) for start in range(0, tile, sub) for at in range(0, wide, chunk)]
    normed, units_two, roots, totals = {}, {}, {}, {}

    def begin(start):
        rows = slice(start, start + sub)
        hidden = x_ref[rows, :].astype(F32) + mult(mixed_ref[rows, :], w_out[...]) + b_out
        hidden_ref[rows, :] = hidden
        units_two[start], roots[start] = normalize(hidden)
        normed[start] = (units_two[start] * gain + shift).astype(BF16)
        normed_ref[rows, :] = normed[start]
        place = lax.broadcasted_iota(jnp.int32, (sub, 1), 0) + (step % steps * tile + start)
        down_grad = jnp.where(place < last_end, cot_ref[rows, :], jnp.zeros((), BF16))
        down_grad_ref[rows, :] = down_grad
        sum_down[...] += column_sum(down_grad.astype(F32))

    def products(start, at):
        if start not in normed:
            begin(start)
        cols = slice(at, at + chunk)
        return (
            mult(normed[start], w_up[:, cols]) + vectors[6:7, cols],
            back_mult(down_grad_ref[start : start + sub, :], w_down[cols, :]),
        )

    def finish(start):
        rows = slice(start, start + sub)
        normed_grad = totals[start]
        sum_gain[...] += column_sum(normed_grad * units_two[start])
        sum_shift[...] += column_sum(normed_grad)
        hidden_grad = norm_back(units_two[start], roots[start], normed_grad, gain)
        hidden_grad = down_grad_ref[rows, :].astype(F32) + hidden_grad
        hidden_grad_ref[rows, :] = hidden_grad
        proj_grad = hidden_grad.astype(BF16)
        proj_grad_ref[rows, :] = proj_grad
        sum_out[...] += column_sum(proj_grad.astype(F32))
        mixed_grad_ref[rows, :] = back_mult(proj_grad, w_out[...]).astype(BF16)

    ready = products(*units[0])
    waiting = None
    for index, (start, at) in enumerate(units):
        u, act_grad = ready
        if index + 1 < len(units):
            ready = products(*units[index + 1])
        rows, cols = slice(start, start + sub), slice(at, at + chunk)
        square = u * u
        smooth = jnp.tanh(u * (GELU + (GELU * 0.044715) * square))
        part = 0.5 * smooth
        share = 0.5 + part
        act_ref[rows, cols] = (u * share).astype(BF16)
        slope = share + (u * (0.5 - part * smooth)) * (GELU + (3 * GELU * 0.044715) * square)
        up_grad = (slope * act_grad).astype(BF16)
        up_grad_ref[rows, cols] = up_grad
        sum_up[:, cols] += column_sum(up_grad.astype(F32))
        grad = back_mult(up_grad, w_up[:, cols])
        totals[start] = grad if start not in totals else totals[start] + grad
        if waiting is not None:
            finish(waiting)
            waiting = None
        if at + chunk == wide:
            waiting = start
    finish(waiting)


def mlp(ends, mixed, x, cot, vectors, w_out, w_up, w_down, row, tile=512, sub=512, chunk=768):
    count, model = x.shape
    wide = w_up.shape[1]
    consts = (vectors, w_out, w_up, w_down)
    widths = [(model, F32), (model, BF16), (wide, BF16), (wide, BF16), (model, BF16)]
    widths += [(model, BF16), (model, F32), (model, BF16)]
    sums = [model, model, wide, model, model]
    return pl.pallas_call(
        functools.partial(mlp_kernel, row=row, sub=sub, chunk=chunk),
        grid=(count // tile,),
        in_specs=[pl.BlockSpec(memory_space=pltpu.SMEM)]
        + [token_rows(tile, model)] * 3
        + [whole(item) for item in consts],
        out_specs=[token_rows(tile, width) for width, _ in widths]
        + [vector_out(width) for width in sums],
        out_shape=[shape(count, width, kind=kind) for width, kind in widths]
        + [shape(1, width, kind=F32) for width in sums],
        compiler_params=kernel_limits(),
        cost_estimate=cost(
            2 * count * model * (3 * wide + 2 * model), count * (26 * model + 4 * wide), count * wide
        ),
        name="mlp",
    )(ends, mixed, x, cot, *consts)


def mlp_out_kernel(hidden_ref, act_ref, vectors, w_down, out_ref):
    model = hidden_ref.shape[1]
    out = hidden_ref[...] + mult(act_ref[...], w_down[...]) + vectors[7:8, :model]
    out_ref[...] = out.astype(BF16)


def mlp_out(hidden, act, vectors, w_down, tile=512):
    count, model = hidden.shape
    wide = act.shape[1]
    return pl.pallas_call(
        mlp_out_kernel,
        grid=(count // tile,),
        in_specs=[token_rows(tile, model), token_rows(tile, wide), whole(vectors), whole(w_down)],
        out_specs=token_rows(tile, model),
        out_shape=shape(count, model),
        compiler_params=kernel_limits(),
        cost_estimate=cost(2 * count * model * wide, count * (6 * model + 2 * wide)),
        name="mlp_out",
    )(hidden, act, vectors, w_down)


def whole_grad_kernel(left_ref, right_ref, out_ref):
    out_ref[...] = cross_rows(left_ref[...], right_ref[...]).astype(out_ref.dtype)


def whole_grad(left, right, kind, name, tile=512):
    count, high = left.shape
    wide = right.shape[1]
    tile = min(tile, high)
    return pl.pallas_call(
        whole_grad_kernel,
        grid=(high // tile,),
        in_specs=[
            pl.BlockSpec((count, tile), lambda i: (0, i)),
            pl.BlockSpec((count, wide), lambda i: (0, 0), pipeline_mode=ONCE),
        ],
        out_specs=pl.BlockSpec((tile, wide), lambda i: (i, 0)),
        out_shape=shape(high, wide, kind=kind),
        compiler_params=kernel_limits(),
        cost_estimate=cost(
            2 * count * high * wide, 2 * (count * high + count * wide + 2 * high * wide)
        ),
        name=name,
    )(left, right)


def weight_grad_kernel(core_ref, left_ref, right_ref, keep, send, *, group):
    width = right_ref.shape[1]
    step_by = math.gcd(width, 2 * LANES)

    def product(start):
        return cross_rows(left_ref[...], right_ref[:, start : start + step_by])

    ready = product(0)
    for start in range(0, width, step_by):
        grad = ready
        if start + step_by < width:
            ready = product(start + step_by)
        store_halves(core_ref, grad, group, keep, send, slice(start, start + step_by))


def qkv_grads_kernel(
    core_ref, normed, grad_ref, sum_ref, weight, vectors, *refs, steps, group, table
):
    others, pairs = refs[:6], refs[6 : 6 + 2 * steps]
    small_keep, small_send, by_grad, by_sum = refs[6 + 2 * steps :]
    step = pl.program_id(0)
    first_step(by_grad, by_sum)
    width = grad_ref.shape[1]
    step_by = math.gcd(width, 2 * LANES)

    def product(start):
        return cross_rows(normed[...], grad_ref[:, start : start + step_by])

    def tile(keep, send):
        ready = product(0)
        for start in range(0, width, step_by):
            grad = ready
            if start + step_by < width:
                ready = product(start + step_by)
            cols = slice(start, start + step_by)
            store_halves(core_ref, grad, group, keep, send, cols)
            for at in range(start, start + step_by, LANES):
                part = weight[:, at : at + LANES].astype(F32)
                by_grad[...] += part * grad[:, at - start : at - start + LANES]
                by_sum[...] += part * sum_ref[:, at : at + LANES]

    for index in range(steps):

        @pl.when(step == index)
        def _():
            tile(*pairs[2 * index : 2 * index + 2])

    @pl.when(step == steps - 1)
    def _():
        model = normed.shape[1]
        shift = column_sum(by_sum[...].T)
        total = column_sum(by_grad[...].T)
        gain = (total - vectors[1:2, :model] * shift) / vectors[0:1, :model]
        sums = [gain, shift] + [other[...] for other in others]
        fill_table(core_ref, sums, *table, small_keep, small_send)


def qkv_grads(core, group, normed, grad, others, weight, vectors, table, tile=768):
    count, model = normed.shape
    width = grad.shape[1]
    tile = min(tile, width)
    steps = width // tile
    _, _, shard, devices, _ = table
    small = devices // 2 * shard
    return pl.pallas_call(
        functools.partial(qkv_grads_kernel, steps=steps, group=group, table=table),
        grid=(steps,),
        in_specs=[
            pl.BlockSpec(memory_space=pltpu.SMEM),
            whole(normed),
            pl.BlockSpec((count, tile), lambda i: (0, i)),
            pl.BlockSpec((1, tile), lambda i: (0, i)),
            pl.BlockSpec((model, tile), lambda i: (0, i)),
            whole(vectors),
        ]
        + [whole(other) for other in others],
        out_specs=[pl.BlockSpec((model // 2, tile), lambda i: (0, 0))] * (2 * steps)
        + [pl.BlockSpec((small, LANES), lambda i: (0, 0))] * 2,
        out_shape=[shape(model // 2, tile)] * (2 * steps) + [shape(small, LANES)] * 2,
        scratch_shapes=[pltpu.VMEM((model, LANES), F32)] * 2,
        compiler_params=kernel_limits(),
        cost_estimate=cost(
            2 * count * model * width, 2 * (count * model + count * width + 2 * model * width)
        ),
        name="qkv_grads",
    )(core, normed, grad, others[0], weight, vectors, *others)


def store_halves(core_ref, grad, group, keep, send, cols):
    first, second = [
        jnp.concatenate(
            [grad[k : k + group] for k in range(which * group, grad.shape[0], 2 * group)], axis=0
        )
        for which in range(2)
    ]
    swapped = core_ref[0] == 1
    keep[:, cols] = jnp.where(swapped, second, first).astype(BF16)
    send[:, cols] = jnp.where(swapped, first, second).astype(BF16)


def weight_grad(core, group, left, right, name, tile=768):
    count, high = left.shape
    wide = right.shape[1]
    tile = min(tile, wide)
    return pl.pallas_call(
        functools.partial(weight_grad_kernel, group=group),
        grid=(wide // tile,),
        in_specs=[
            pl.BlockSpec(memory_space=pltpu.SMEM),
            pl.BlockSpec((count, high), lambda i: (0, 0), pipeline_mode=ONCE),
            pl.BlockSpec((count, tile), lambda i: (0, i)),
        ],
        out_specs=[pl.BlockSpec((high // 2, tile), lambda i: (0, i))] * 2,
        out_shape=[shape(high // 2, wide)] * 2,
        compiler_params=kernel_limits(),
        cost_estimate=cost(
            2 * count * high * wide, 2 * (count * high + count * wide + high * wide)
        ),
        name=name,
    )(core, left, right)


def qkv_backward_kernel(
    grad_ref, x_ref, hidden_grad_ref, vectors, weight, out_ref, *, sub
):
    count, model = x_ref.shape
    gain = vectors[0:1, :model]

    def lower(start):
        return back_mult(grad_ref[start : start + sub, :], weight[...])

    ready = lower(0)
    for start in range(0, count, sub):
        normed_grad = ready
        if start + sub < count:
            ready = lower(start + sub)
        rows = slice(start, start + sub)
        unit, root = normalize(x_ref[rows, :].astype(F32))
        inner = norm_back(unit, root, normed_grad, gain)
        out_ref[rows, :] = (hidden_grad_ref[rows, :] + inner).astype(BF16)


def qkv_backward(grad, x, hidden_grad, vectors, weight, tile=512, sub=256):
    count, model = x.shape
    width = weight.shape[1]
    return pl.pallas_call(
        functools.partial(qkv_backward_kernel, sub=sub),
        grid=(count // tile,),
        in_specs=[token_rows(tile, width)]
        + [token_rows(tile, model)] * 2
        + [whole(vectors), whole(weight)],
        out_specs=token_rows(tile, model),
        out_shape=shape(count, model),
        compiler_params=kernel_limits(),
        cost_estimate=cost(
            2 * count * model * width, 2 * (4 * count * model + (count + model) * width)
        ),
        name="qkv_backward",
    )(grad, x, hidden_grad, vectors, weight)


def segments(ends, index, row):
    place = lax.broadcasted_iota(jnp.int32, (8, row), 1)
    found = jnp.zeros((8, row), F32)
    for slot in range(ends.shape[1]):
        found = found + jnp.where(ends[index, slot] <= place, 1.0, 0.0)
    return found


def allowed_bias(ends, row):
    found = segments(ends, pl.program_id(0), row)
    keys = lax.broadcasted_iota(jnp.int32, (row, row), 0)
    queries = lax.broadcasted_iota(jnp.int32, (row, row), 1)
    same = found.T[:, 0:1] == found[0:1]
    return jnp.where(same & (keys <= queries), 0.0, HIDE)


def pair_lanes(pair):
    return slice(pair * PAIR, (pair + 1) * PAIR)


def head_rows(head):
    return slice(head * HEAD, (head + 1) * HEAD)


def own_lanes(values, head):
    lane = lax.broadcasted_iota(jnp.int32, (1, PAIR), 1)
    return jnp.where((lane < HEAD) == (head == 0), values, jnp.zeros((), BF16))


def key_blocks(half, part, step):
    for start in range(0, (part + 1) * half, step):
        low = max(0, (start - part * half) // LANES * LANES) if start >= part * half else 0
        yield start, low


def widen(values, low, fill):
    if low == 0:
        return values
    pad = jnp.full((values.shape[0], low), fill, values.dtype)
    return jnp.concatenate([pad, values], axis=1)


def folded(values, combine):
    return combine(values.reshape(values.shape[0] // 8, 8, values.shape[1]), axis=0)


def unit_list(pairs):
    return [(pair, part, head) for pair in range(pairs) for part in range(2) for head in range(2)]


def forward_kernel(
    ends, q_ref, k_ref, v_ref, mixed_ref, total_ref, bias, *, pairs, step, lead
):
    row = q_ref.shape[0]
    half = row // 2
    bias[...] = allowed_bias(ends, row)

    def scores_of(pair, part, head):
        seen = (part + 1) * half
        queries = q_ref[part * half : seen, pair_lanes(pair)] * jnp.asarray(SCALE, BF16)
        return back_mult(k_ref[:seen, pair_lanes(pair)], own_lanes(queries, head))

    def weigh(part, scores):
        base = part * half
        top = jnp.full((8, half), HIDE, F32)
        shown = []
        for start, low in key_blocks(half, part, step):
            block = scores[start : start + step, low:]
            square = block * block + 1.0
            mag = square * (lax.rsqrt(square) * LOG2E)
            mag = mag + bias[start : start + step, base + low : base + half]
            shown.append(mag)
            top = jnp.maximum(top, widen(folded(mag, jnp.max), low, HIDE))
        top = jnp.max(top, axis=0, keepdims=True)
        total = jnp.zeros((8, half), F32)
        signed = []
        for (start, low), mag in zip(key_blocks(half, part, step), shown):
            weight = jnp.exp2(mag - top[:, low:])
            total = total + widen(folded(weight, jnp.sum), low, 0.0)
            block = jnp.tanh(scores[start : start + step, low:]) * weight
            signed.append(widen(block.astype(BF16), low, 0.0))
        return jnp.concatenate(signed, axis=0), top, jnp.sum(total, axis=0, keepdims=True)

    units = unit_list(pairs)
    scores = [scores_of(*unit) for unit in units[:lead]]
    turned, parts = {}, {}

    def finish(unit, signed, top, total):
        pair, part, head = unit
        here = slice(part * half, (part + 1) * half)
        total_ref[0, pair, head : head + 1, here] = top * (1.0 / LOG2E) + jnp.log(total)
        values = turned[pair][head_rows(head), : (part + 1) * half]
        parts[unit] = mult(values, signed) * (1.0 / total)
        if head == 1:
            both = jnp.concatenate([parts[pair, part, 0], parts[unit]], axis=0)
            mixed_ref[here, pair_lanes(pair)] = both.T.astype(BF16)

    waiting = None
    for index, unit in enumerate(units):
        if index + lead < len(units):
            scores.append(scores_of(*units[index + lead]))
        if unit[0] not in turned:
            turned[unit[0]] = v_ref[:, pair_lanes(unit[0])].T
        weighed = weigh(unit[1], scores[index])
        if waiting is not None:
            finish(*waiting)
        waiting = (unit,) + weighed
    finish(*waiting)


def attention_forward(ends, merged, row):
    count, width = merged.shape
    model = width // 3
    pairs = model // PAIR
    micro = count // row
    area = micro * pairs * 2 * row * row

    def third(index):
        return pl.BlockSpec((row, model), lambda r: (r, index))

    return pl.pallas_call(
        functools.partial(forward_kernel, pairs=pairs, step=32, lead=2),
        grid=(micro,),
        in_specs=[
            pl.BlockSpec(memory_space=pltpu.SMEM),
            third(0),
            third(1),
            third(2),
        ],
        out_specs=[
            pl.BlockSpec((row, model), lambda r: (r, 0)),
            pl.BlockSpec((1, pairs, 2, row), lambda r: (r, 0, 0, 0)),
        ],
        out_shape=[shape(count, model), shape(micro, pairs, 2, row, kind=F32)],
        scratch_shapes=[pltpu.VMEM((row, row), F32)],
        compiler_params=kernel_limits(),
        cost_estimate=cost(area * 4 * HEAD * 5, count * width * 3, area * 3),
        name="attention_forward",
    )(ends, merged, merged, merged)


def backward_kernel(
    ends, q_ref, k_ref, v_ref, mixed_ref, grad_ref, total_ref,
    out_ref, sum_ref, bias, *, pairs, step, lead, lag
):
    row = q_ref.shape[0]
    half = row // 2
    model = pairs * PAIR
    first_step(sum_ref)
    bias[...] = allowed_bias(ends, row)

    def put(section, pair, rows, values):
        cols = slice(section * model + pair * PAIR, section * model + (pair + 1) * PAIR)
        values = values.astype(BF16)
        out_ref[rows, cols] = values
        sum_ref[:, cols] += column_sum(values.astype(F32))

    def queries_and_grads(pair, part, head):
        here = slice(part * half, (part + 1) * half)
        queries = q_ref[here, pair_lanes(pair)] * jnp.asarray(SCALE, BF16)
        return own_lanes(queries, head), own_lanes(grad_ref[here, pair_lanes(pair)], head)

    def products(pair, part, head):
        seen = (part + 1) * half
        queries, grads = queries_and_grads(pair, part, head)
        return (
            back_mult(k_ref[:seen, pair_lanes(pair)], queries),
            back_mult(v_ref[:seen, pair_lanes(pair)], grads),
        )

    centres, turned, sums, query_parts = {}, {}, {}, {}

    def weigh(pair, part, head, scores, weight_grads):
        base = part * half
        here = slice(base, base + half)
        if (pair, part) not in centres:
            grads = grad_ref[here, pair_lanes(pair)].astype(F32)
            centres[pair, part] = (grads * mixed_ref[here, pair_lanes(pair)].astype(F32)).T
        centre = column_sum(centres[pair, part][head_rows(head)])
        total = total_ref[0, pair, head : head + 1, here] * LOG2E
        signed, score_grads = [], []
        for start, low in key_blocks(half, part, step):
            block = scores[start : start + step, low:]
            weight_grad = weight_grads[start : start + step, low:]
            square = block * block + 1.0
            root = lax.rsqrt(square)
            shift = bias[start : start + step, base + low : base + half] - total[:, low:]
            weight = jnp.exp2(square * (root * LOG2E) + shift)
            smooth = jnp.tanh(block)
            bent = weight_grad * smooth
            score_grad = weight * (
                (weight_grad - bent * smooth) + (block * root) * (bent - centre[:, low:])
            )
            signed.append(widen((smooth * weight).astype(BF16), low, 0.0))
            score_grads.append(widen(score_grad.astype(BF16), low, 0.0))
        return jnp.concatenate(signed, axis=0), jnp.concatenate(score_grads, axis=0)

    def finish(unit, signed, score_grads):
        pair, part, head = unit
        queries, grads = queries_and_grads(*unit)
        for section, grad in ((2, mult(signed, grads)), (1, mult(score_grads, queries))):
            for block in range(part + 1):
                add = grad[block * half : (block + 1) * half]
                key = (pair, section, block)
                sums[key] = add if key not in sums else sums[key] + add
        if pair not in turned:
            turned[pair] = k_ref[:, pair_lanes(pair)].T
        keys = turned[pair][head_rows(head), : (part + 1) * half]
        query_parts[unit] = mult(keys, score_grads)
        if head == 1:
            both = jnp.concatenate([query_parts[pair, part, 0], query_parts[unit]], axis=0)
            put(0, pair, slice(part * half, (part + 1) * half), both.T * SCALE)
        if head == 1 and part == 1:
            for section in (1, 2):
                for block in range(2):
                    rows = slice(block * half, (block + 1) * half)
                    put(section, pair, rows, sums[pair, section, block])

    units = unit_list(pairs)
    ready = [products(*unit) for unit in units[:lead]]
    waiting = []
    for index, unit in enumerate(units):
        if index + lead < len(units):
            ready.append(products(*units[index + lead]))
        waiting.append((unit,) + weigh(*unit, *ready[index]))
        ready[index] = None
        if len(waiting) > lag:
            finish(*waiting.pop(0))
    for item in waiting:
        finish(*item)


def attention_backward(ends, merged, mixed, mixed_grad, total, row):
    count, width = merged.shape
    model = width // 3
    pairs = model // PAIR
    micro = count // row
    area = micro * pairs * 2 * row * row

    def third(index):
        return pl.BlockSpec((row, model), lambda r: (r, index))

    return pl.pallas_call(
        functools.partial(backward_kernel, pairs=pairs, step=32, lead=1, lag=0),
        grid=(micro,),
        in_specs=[
            pl.BlockSpec(memory_space=pltpu.SMEM),
            third(0),
            third(1),
            third(2),
            third(0),
            third(0),
            pl.BlockSpec((1, pairs, 2, row), lambda r: (r, 0, 0, 0)),
        ],
        out_specs=[pl.BlockSpec((row, width), lambda r: (r, 0)), vector_out(width)],
        out_shape=[shape(count, width), shape(1, width, kind=F32)],
        scratch_shapes=[pltpu.VMEM((row, row), F32)],
        compiler_params=kernel_limits(),
        cost_estimate=cost(area * 10 * HEAD * 4, count * width * 5, area * 3),
        name="attention_backward",
    )(ends, merged, merged, merged, mixed, mixed_grad, total)


def vector_slots(lengths):
    slots, fill = [], []
    for length in lengths:
        row = next((r for r, used in enumerate(fill) if used + length <= LANES), len(fill))
        if row == len(fill):
            fill.append(0)
        slots.append((row, fill[row], length))
        fill[row] += length
    return slots, len(fill)


def lane_of(devices, length, first):
    size = devices * length
    place = lax.broadcasted_iota(jnp.int32, (LANES, size), 1).astype(F32)
    inside = place - length * jnp.floor((place + 0.5) * (1.0 / length))
    lane = lax.broadcasted_iota(jnp.int32, (LANES, size), 0).astype(F32)
    return (lane == inside + first).astype(BF16)


def owner_of(devices, length):
    size = devices * length
    place = lax.broadcasted_iota(jnp.int32, (devices, size), 1)
    start = lax.broadcasted_iota(jnp.int32, (devices, size), 0) * length
    return (place >= start) & (place < start + length)


def vectors_from_table(table, slots):
    devices = table.shape[0]
    longest = devices * max(length for _, _, length in slots)

    def kernel(table_ref, out):
        lines = table_ref[...].astype(F32)
        lines = {row: lines[:, row, :].astype(BF16) for row, _, _ in slots}
        for index, (row, first, length) in enumerate(slots):
            spread = mult(lines[row], lane_of(devices, length, first))
            out[index : index + 1, : devices * length] = column_sum(
                jnp.where(owner_of(devices, length), spread, 0.0)
            )

    return pl.pallas_call(
        kernel,
        out_shape=shape(len(slots), longest, kind=F32),
        compiler_params=kernel_limits(40),
        name="vectors_from_table",
    )(table)


def split(values, size):
    quotient = jnp.floor((values + 0.5) * (1.0 / size))
    return quotient, values - size * quotient


def fill_table(core_ref, vectors, slots, rows, shard, devices, inner, keep, send):
    filled = [jnp.zeros((devices, LANES), F32) for _ in range(rows)]
    for (row, first, length), vector in zip(slots, vectors):
        own = jnp.where(owner_of(devices, length), vector, 0.0).astype(BF16)
        filled[row] = filled[row] + back_mult(own, lane_of(devices, length, first))
    stacked = jnp.concatenate(filled, axis=0).astype(BF16)
    size = (devices // 2 * shard, devices * rows)
    target = lax.broadcasted_iota(jnp.int32, size, 0).astype(F32)
    source = lax.broadcasted_iota(jnp.int32, size, 1).astype(F32)
    block, row = split(target, shard)
    chip, y = split(block, inner)
    swapped = core_ref[0] == 1
    halves = []
    for which in range(2):
        match = source == row * devices + (chip * 2 + which) * inner + y
        halves.append(mult(jnp.where(row < rows, match.astype(F32), 0.0).astype(BF16), stacked))
    keep[...] = jnp.where(swapped, halves[1], halves[0]).astype(BF16)
    send[...] = jnp.where(swapped, halves[0], halves[1]).astype(BF16)


class Links:
    def __init__(self, mesh):
        self.outer = mesh.shape["dp"]
        self.inner = mesh.shape["fsdp"]
        self.count = self.outer * self.inner
        self.far = [(k << 2) * self.inner for k in range(self.outer // 4)]
        self.near = [(b << 1) * self.inner + f for b in range(2) for f in range(self.inner)]
        self.core = self.inner

    def place(self):
        return lax.axis_index("dp") * self.inner + lax.axis_index("fsdp")

    def swap(self, piece, mask):
        return lax.ppermute(piece, AXES, [(i, i ^ mask) for i in range(self.count)])

    def far_step(self, shard):
        got = [self.swap(shard, mask) for mask in self.far[1:]]
        return lambda *others: jnp.stack([shard] + gate(got, *others))

    def far_doubled(self, shard):
        column = shard[None]
        while column.shape[0] < len(self.far):
            column = jnp.concatenate([column, self.swap(column, self.far[column.shape[0]])])
        return column

    def near_step(self, column):
        return [column] + [self.swap(column, mask) for mask in self.near[1:]]

    def near_halves(self, column):
        if len(self.near) != 4:
            plane = self.near_step(column)
            return plane, lambda *others: gate(plane, *others)
        side, inner = [self.swap(column, mask) for mask in (self.near[2], self.near[1])]
        plane = [column, inner, side]
        width = half_columns(column)

        def second(*others):
            left, right = gate((inner[:, :, :width], side[:, :, width:]), *others)
            return plane + [self.swap(left, self.near[2]), self.swap(right, self.near[1])]

        return plane, second

    def core_step(self, plane):
        return plane + [self.swap(piece, self.core) for piece in plane]

    def arrange(self, pieces, columns):
        far = self.far
        held = len(pieces)
        masks, ranges = list(self.near), [(0, pieces[0].shape[2])] * len(self.near)
        if held > 2 * len(masks):
            half = half_columns(pieces[0])
            masks, ranges = masks + masks[-1:], ranges[:-1] + [(0, half), (half, ranges[0][1])]
        masks, ranges = masks + [mask ^ self.core for mask in masks], ranges * 2
        rows = pieces[0].shape[1]

        def kernel(me_ref, *refs):
            results = refs[held : held + len(columns)]
            targets = refs[held + len(columns) : held + 2 * len(columns)]
            sems, out_sem = refs[-2:]
            me = me_ref[0]
            copies = [[] for _ in columns]
            for piece, mask, (low, high) in zip(refs[:held], masks, ranges):
                for k, step in enumerate(far):
                    owner = jnp.bitwise_xor(me, mask ^ step)
                    for which, (start, width, parts) in enumerate(columns):
                        for part in range(parts):
                            base = start + part * width
                            one, two = max(low, base), min(high, base + width)
                            if one >= two:
                                continue
                            copies[which].append(
                                pltpu.make_async_copy(
                                    piece.at[k, :, pl.ds(one - low, two - one)],
                                    targets[which].at[
                                        owner * parts + part, :, pl.ds(one - base, two - one)
                                    ],
                                    sems.at[which],
                                )
                            )
            for group in copies:
                for copy in group:
                    copy.start()
            outs = [
                pltpu.make_async_copy(target, result, out_sem.at[which])
                for which, (target, result) in enumerate(zip(targets, results))
            ]
            for group, out in zip(copies, outs):
                for copy in group:
                    copy.wait()
                out.start()
            for out in outs:
                out.wait()

        return pl.pallas_call(
            kernel,
            in_specs=[pl.BlockSpec(memory_space=pltpu.SMEM)]
            + [pl.BlockSpec(memory_space=pl.ANY)] * held,
            out_specs=[pl.BlockSpec(memory_space=pl.ANY)] * len(columns),
            out_shape=[
                jax.ShapeDtypeStruct((self.count * parts, rows, width), BF16)
                for _, width, parts in columns
            ],
            scratch_shapes=[
                pltpu.VMEM((self.count * parts, rows, width), BF16) for _, width, parts in columns
            ]
            + [pltpu.SemaphoreType.DMA((len(columns),))] * 2,
            compiler_params=kernel_limits(),
            name="arrange",
        )(jnp.full((1,), self.place(), jnp.int32), *pieces)

    def position(self):
        dp = lax.axis_index("dp")
        return dp >> 2, (dp >> 1) & 1, dp & 1, lax.axis_index("fsdp")

    def core_swap(self, pair):
        return pair[0], self.swap(pair[1], self.core)

    def kernel_sums(self, pairs, name):
        _, side, _, inner = self.position()
        far, span = len(self.far), self.inner
        rows = pairs[0][0].shape[0] * 2 // self.count
        widths = [keep.shape[1] for keep, _ in pairs]

        def view(array):
            return array.reshape(far, 2, span, rows, array.shape[1])

        count = len(pairs)

        def kernel(place, *refs):
            own, sources, refs = refs[:count], refs[count : 2 * count], refs[2 * count :]
            outs, held, sems = refs[: 2 * span], refs[2 * span : -1], refs[-1]
            copies = [
                pltpu.make_async_copy(source, target, sems.at[index])
                for index, (source, target) in enumerate(zip(sources, held))
            ]
            for copy in copies:
                copy.start()
            at = 0
            for index, width in enumerate(widths):
                copies[index].wait()
                for partner, out in enumerate(outs):
                    x = jnp.bitwise_xor(place[0], partner // span)
                    y = jnp.bitwise_xor(place[1], partner % span)
                    for z in range(far):
                        total = own[index][z, x, y].astype(F32) + held[index][z, x, y].astype(F32)
                        out[z, :, at : at + width] = total.astype(BF16)
                at += width

        size = self.count // 2 * rows * sum(widths)
        arrays = [view(keep) for keep, _ in pairs] + [view(received) for _, received in pairs]
        call = pl.pallas_call(
            kernel,
            in_specs=[pl.BlockSpec(memory_space=pltpu.SMEM)]
            + [pl.BlockSpec(memory_space=pltpu.VMEM)] * count
            + [pl.BlockSpec(memory_space=pl.ANY)] * count,
            out_shape=[shape(far, rows, sum(widths))] * (2 * span),
            scratch_shapes=[pltpu.VMEM(array.shape, BF16) for array in arrays[count:]]
            + [pltpu.SemaphoreType.DMA((count,))],
            compiler_params=kernel_limits(52),
            cost_estimate=cost(size, 6 * size),
            name=name,
        )
        place = jnp.stack([side, inner]).astype(jnp.int32)
        return list(call(place, *arrays))

    def fused_sums(self, pairs, join):
        _, side, _, inner = self.position()

        def view(array):
            rows = array.shape[0] * 2 // self.count
            return array.reshape(self.outer // 4, 2, self.inner, rows, array.shape[1])

        mine = [view(keep) for keep, _ in pairs]
        got = [view(received) for _, received in pairs]

        def finish(*others):
            received = gate(got, *others) if others else got
            sums = []
            for b in range(2):
                for f in range(self.inner):

                    def cut(array):
                        return pick(pick(array, side ^ b, 1), inner ^ f, 1).astype(F32)

                    sums.append(
                        join([(cut(a) + cut(b)).astype(BF16) for a, b in zip(mine, received)])
                    )
            return sums

        return finish

    def near_swaps(self, sums):
        return sums[:1] + [self.swap(part, mask) for part, mask in zip(sums[1:], self.near[1:])]

    def near_sums(self, sums):
        return self.far_parts(self.near_swaps(sums))

    def far_parts(self, got):
        column = self.position()[0]

        def finish(*others):
            received = gate(got, *others)
            parts = []
            for k in range(len(self.far)):
                part = sum(pick(array, column ^ k, 0).astype(F32) for array in received)
                parts.append(part if k == 0 else part.astype(BF16))
            return parts

        return finish

    def far_sums(self, parts):
        got = [self.swap(part, mask) for part, mask in zip(parts[1:], self.far[1:])]

        def finish(*others):
            received = gate(got, *others)
            return functools.reduce(lambda sum, part: sum + part.astype(F32), received, parts[0])

        return got, finish


def far_start(links, sums):
    column = links.position()[0]

    def part(k):
        return sum(pick(array, column ^ k, 0).astype(F32) for array in sums)

    if len(links.far) != 4:
        parts = [part(k) for k in range(len(links.far))]
        return (), lambda *others: (
            gate(parts[0], *others),
            {k: parts[k].astype(BF16) for k in range(1, len(parts))},
        )
    got = links.swap(jnp.stack([part(2), part(3)]).astype(BF16), links.far[2])

    def second(*others):
        received = gate(got, *others).astype(F32)
        return part(0) + received[0], {1: (part(1) + received[1]).astype(BF16)}

    return got, second


def far_join(links, blocks):
    got = {}
    for k in range(1, len(links.far)):
        sent = [(index, parts[k]) for index, (_, parts) in enumerate(blocks) if k in parts]
        arrived = links.swap(jnp.concatenate([part for _, part in sent], axis=1), links.far[k])
        at = 0
        for index, part in sent:
            got.setdefault(index, []).append((arrived, at, part.shape[1]))
            at += part.shape[1]

    return got, [own for own, _ in blocks]


def last_sums(got, owns, splits, down):
    arrays, order = [], {}
    for pieces in got.values():
        for array, _, _ in pieces:
            if id(array) not in order:
                order[id(array)] = len(arrays)
                arrays.append(array)

    def kernel(*refs):
        own_refs, refs = refs[: len(owns)], refs[len(owns) :]
        array_refs, refs = refs[: len(arrays)], refs[len(arrays) :]
        outs = list(refs[1:])
        for index, own in enumerate(own_refs):
            for start, width in splits[index]:
                total = own[:, start : start + width]
                for array, at, _ in got[index]:
                    part = array_refs[order[id(array)]][:, at + start : at + start + width]
                    total = total + part.astype(F32)
                outs.pop(0)[...] = total
        outs.pop(0)[...] = refs[0][...].astype(F32)

    rows = owns[0].shape[0]
    return pl.pallas_call(
        kernel,
        out_shape=[shape(rows, width, kind=F32) for cuts in splits for _, width in cuts]
        + [shape(*down.shape, kind=F32)],
        compiler_params=kernel_limits(24),
        name="last_sums",
    )(*owns, *arrays, down)


def half_columns(array):
    return array.shape[2] // 2 // LANES * LANES


def pick(array, index, axis):
    return lax.dynamic_index_in_dim(array, index, axis, keepdims=False)


def run(
    links,
    tokens,
    lengths,
    cotangent,
    attn_norm_gain,
    attn_norm_bias,
    qkv_weight,
    qkv_bias,
    out_weight,
    out_bias,
    mlp_norm_gain,
    mlp_norm_bias,
    up_weight,
    up_bias,
    down_weight,
    down_bias,
):
    micro, row, model = tokens.shape
    count = micro * row
    shard = qkv_weight.shape[0]
    wide = up_weight.shape[1]
    devices = links.count

    vectors = (
        attn_norm_gain,
        attn_norm_bias,
        qkv_bias,
        out_bias,
        mlp_norm_gain,
        mlp_norm_bias,
        up_bias,
        down_bias,
    )
    slots, table_rows = vector_slots([vector.shape[0] for vector in vectors])
    lines = []
    for line in range(table_rows):
        held = [v for v, slot in zip(vectors, slots) if slot[0] == line]
        held = jnp.concatenate(held)
        lines.append(jnp.pad(held, (0, LANES - held.shape[0])))
    extra = jnp.pad(jnp.stack(lines), ((0, shard - table_rows), (0, 0)))
    qkv_far = links.far_step(jnp.concatenate([qkv_weight, extra], axis=1))
    middle_in = jnp.concatenate([out_weight, up_weight], axis=1)
    middle_column = links.far_doubled(middle_in)
    qkv_column = qkv_far()
    qkv_plane = links.near_step(qkv_column)
    w_down = lax.all_gather(down_weight, AXES, axis=0, tiled=True)
    middle_start, middle_corner = links.near_halves(gate(middle_column, qkv_plane))
    w_qkv, extra = links.arrange(
        links.core_step(qkv_plane), [(0, 3 * model, 1), (3 * model, LANES, 1)]
    )
    w_qkv = w_qkv.reshape(model, 3 * model)
    table = vectors_from_table(extra, slots)

    ends = jnp.cumsum(lengths.reshape(micro, -1), axis=1, dtype=jnp.int32)
    inputs = tokens.reshape(count, model)
    normed_one, merged = qkv_forward(inputs, table, w_qkv)
    middle_plane = middle_corner(merged)
    mixed, log_total = attention_forward(ends, gate(merged, middle_start), row)
    middle_pieces = links.core_step(middle_plane[:3] + gate(middle_plane[3:], mixed))
    w_out, w_up = links.arrange(gate(middle_pieces, mixed), [(0, model, 1), (model, wide, 1)])
    w_out = w_out.reshape(model, model)
    w_up = w_up.reshape(model, wide)
    (
        hidden,
        normed_two,
        activated,
        up_grad,
        down_grad,
        proj_grad,
        hidden_grad,
        mixed_grad,
        sum_gain_two,
        sum_shift_two,
        sum_up,
        sum_out,
        sum_down,
    ) = mlp(
        ends, mixed, inputs, cotangent.reshape(count, model), table, w_out, w_up, w_down, row
    )

    core = jnp.full((1,), links.position()[2], jnp.int32)
    group = links.inner * shard
    grad_up = weight_grad(core, group, normed_two, up_grad, "grad_up")
    grad_up = links.core_swap(grad_up)
    grad_out = weight_grad(core, group, mixed, gate(proj_grad, grad_up[0]), "grad_out")
    grad_out = links.core_swap(grad_out)
    grad_down = whole_grad(activated, gate(down_grad, grad_out[0]), BF16, "grad_down")
    down_block = lax.psum_scatter(grad_down, AXES, scatter_dimension=0, tiled=True)
    early = links.fused_sums(
        [grad_out, grad_up], lambda cuts: jnp.concatenate(cuts, axis=2)
    )(grad_down)
    early_near = links.near_swaps(early)
    qkv_grad, sum_qkv = attention_backward(
        ends, merged, mixed, gate(mixed_grad, early), log_total, row
    )
    early_near = gate(early_near, qkv_grad)
    early_first, early_second = far_start(links, early_near)
    *grad_qkv, small_keep, small_send = qkv_grads(
        core,
        group,
        normed_one,
        gate(qkv_grad, early_near),
        (sum_qkv, sum_out, sum_gain_two, sum_shift_two, sum_up, sum_down),
        w_qkv,
        table,
        (slots, table_rows, shard, devices, links.inner),
    )
    small = (small_keep, small_send)

    late = [links.core_swap(pair) for pair in zip(grad_qkv[::2], grad_qkv[1::2])]
    late = links.kernel_sums([*late, links.core_swap(small)], "late_sums")
    late_parts = links.near_sums(late)
    block_out = mlp_out(hidden, gate(activated, late), table, w_down)
    early_own, early_sent = early_second(block_out)
    late_parts = late_parts(block_out)
    late_sent = {k: late_parts[k] for k in range(1, len(late_parts))}
    got, owns = far_join(links, [(early_own, early_sent), (late_parts[0], late_sent)])
    token_grad = qkv_backward(
        gate(qkv_grad, late_parts, early_sent, block_out),
        inputs,
        hidden_grad,
        table,
        w_qkv,
    )
    keys = [(index, place) for index in got for place in range(len(got[index]))]
    arrived = gate([got[index][place][0] for index, place in keys], token_grad)
    unique = {}
    for (index, place), array in zip(keys, arrived):
        array = unique.setdefault(id(got[index][place][0]), array)
        got[index][place] = (array,) + got[index][place][1:]
    out_block, up_block, qkv_block, small_block, down_block = last_sums(
        got, owns, [[(0, model), (model, wide)], [(0, 3 * model), (3 * model, LANES)]], down_block
    )
    (
        gain_one_shard,
        bias_one_shard,
        bias_qkv_shard,
        bias_out_shard,
        gain_two_shard,
        bias_two_shard,
        bias_up_shard,
        bias_down_shard,
    ) = [
        small_block[line, start : start + length]
        for line, start, length in slots
    ]
    return (
        block_out.reshape(tokens.shape),
        token_grad.reshape(tokens.shape),
        gain_one_shard,
        bias_one_shard,
        qkv_block,
        bias_qkv_shard,
        out_block,
        bias_out_shard,
        gain_two_shard,
        bias_two_shard,
        up_block,
        bias_up_shard,
        down_block,
        bias_down_shard,
    )


def solution(mesh):
    links = Links(mesh)
    rows = P(None, AXES, None)
    vector = P(AXES)
    matrix = P(AXES, None)
    params = (
        vector,
        vector,
        matrix,
        vector,
        matrix,
        vector,
        vector,
        vector,
        matrix,
        vector,
        matrix,
        vector,
    )
    return jax.shard_map(
        lambda *args: run(links, *args),
        mesh=mesh,
        in_specs=(rows, rows, rows) + params,
        out_specs=(rows, rows) + params,
        check_vma=False,
    )
```
